32 devices in a mesh: dp: 8 (over z, y), tensor: 4 (over x, core).
Axes of the slice: x: 2, y: 2, z: 4, core: 2. Of those that a mesh axis runs over, the one named last changes fastest.
Arguments:
- tokens: bfloat16 [4096, 1536], P('dp'), may hold values from -6 to 6
- lengths: int32 [2], replicated, may hold values from 1537 to 2048, as said below
- norm_conv: float32 [1536], replicated, may hold values from 0.5 to 1.5
- conv_in: bfloat16 [1536, 3, 1536], P(None, None, 'tensor'), may hold values from -0.15625 to 0.15625
- conv_kernel: bfloat16 [3, 1536], P(None, 'tensor'), may hold values from -3.5 to 3.5
- conv_out: bfloat16 [1536, 1536], P('tensor'), may hold values from -0.15625 to 0.15625
- norm_mlp_one: float32 [1536], replicated, may hold values from 0.5 to 1.5
- gate_up_one: bfloat16 [1536, 2, 6912], P(None, None, 'tensor'), may hold values from -0.15625 to 0.15625
- down_one: bfloat16 [6912, 1536], P('tensor'), may hold values from -0.078125 to 0.078125
- norm_attn: float32 [1536], replicated, may hold values from 0.5 to 1.5
- query_weight: bfloat16 [1536, 1536], P(None, 'tensor'), may hold values from -0.15625 to 0.15625
- kv_weight: bfloat16 [1536, 2, 512], P(None, None, 'tensor'), may hold values from -0.15625 to 0.15625
- query_gain: float32 [64], replicated, may hold values from 0.5 to 1.5
- key_gain: float32 [64], replicated, may hold values from 0.5 to 1.5
- attn_out: bfloat16 [1536, 1536], P('tensor'), may hold values from -0.625 to 0.625
- norm_mlp_two: float32 [1536], replicated, may hold values from 0.5 to 1.5
- gate_up_two: bfloat16 [1536, 2, 6912], P(None, None, 'tensor'), may hold values from -0.15625 to 0.15625
- down_two: bfloat16 [6912, 1536], P('tensor'), may hold values from -0.078125 to 0.078125
- cotangent: bfloat16 [4096, 1536], P('dp'), may hold values from -6 to 6
Outputs:
- output: bfloat16 [4096, 1536], P('dp')
- grad_tokens: float32 [4096, 1536], P('dp')
- grad_norm_conv: float32 [1536], replicated
- grad_conv_in: float32 [1536, 3, 1536], P('dp', None, 'tensor')
- grad_conv_kernel: float32 [3, 1536], P(None, 'tensor')
- grad_conv_out: float32 [1536, 1536], P('tensor', 'dp')
- grad_norm_mlp_one: float32 [1536], replicated
- grad_gate_up_one: float32 [1536, 2, 6912], P('dp', None, 'tensor')
- grad_down_one: float32 [6912, 1536], P('tensor', 'dp')
- grad_norm_attn: float32 [1536], replicated
- grad_query_weight: float32 [1536, 1536], P('dp', 'tensor')
- grad_kv_weight: float32 [1536, 2, 512], P('dp', None, 'tensor')
- grad_query_gain: float32 [64], replicated
- grad_key_gain: float32 [64], replicated
- grad_attn_out: float32 [1536, 1536], P('tensor', 'dp')
- grad_norm_mlp_two: float32 [1536], replicated
- grad_gate_up_two: float32 [1536, 2, 6912], P('dp', None, 'tensor')
- grad_down_two: float32 [6912, 1536], P('tensor', 'dp')
The draws below stay inside these ranges and needn't reach their ends.
Inputs may be any that keep to these rules, and one draw needn't show every extreme that they name: `lengths`: some sequence has exactly 2048 live tokens.
All inputs are finite; a program needn't handle non-finite values.
Results may differ from the reference program's by a relative error of at most 0.025.
Values may be sent and summed in bfloat16 or wider, within the bound.
A program may use at most 320 MiB of HBM per device.

```python
import jax
import jax.numpy as jnp
from jax import lax

D = 1536
FF = 6912
HEADS = 24
KV_HEADS = 8
HEAD = 64
KW = 3
SPAN = 4
TOK_DEV = 512
SLOTS = 2048
NSEQ = 2
TOKENS = 4096
LEN_MIN = 1537
GROUP = 3


def draw_lengths(key, part):
    key = jax.random.fold_in(key, 11)
    length_key, chosen_key = jax.random.split(key)
    sampled = jax.random.randint(length_key, (NSEQ,), LEN_MIN, SLOTS + 1)
    chosen = jax.random.randint(chosen_key, (), 0, NSEQ)
    return jnp.where(jnp.arange(NSEQ) == chosen, SLOTS, sampled).astype(jnp.int32)


def shard_levels(rng, dims, cuts, least, high):
    level, own = 1.0, jax.random.fold_in(rng, 6)
    for axis_at, blocks in cuts:
        heights = jnp.exp(jax.random.uniform(jax.random.fold_in(own, axis_at), (blocks,), jnp.float32, least / len(cuts), high / len(cuts)))
        level = level * jnp.repeat(heights, dims[axis_at] // blocks).reshape([-1 if axis == axis_at else 1 for axis in range(len(dims))])
    return level


def normal_values(rng, dims, deviation, reach, pieces=(), kind=jnp.bfloat16):
    array = deviation * jax.random.normal(rng, dims, jnp.float32)
    if pieces:
        array = array * shard_levels(rng, dims, pieces, -0.22, 0.18)
    return jnp.clip(array, -reach, reach).astype(kind)


def setup_inputs(seed: int = 0) -> dict:
    keys = jax.random.split(jax.random.key(seed), 20)
    tokens = normal_values(keys[0], (TOKENS, D), 1.0, 6.0, ((0, 8),))
    lengths = draw_lengths(jax.random.fold_in(keys[19], 71), 0)
    norm_conv = jnp.clip(1.0 + 0.1 * jax.random.normal(keys[2], (D,), jnp.float32), 0.5, 1.5)
    conv_in = normal_values(keys[3], (D, 3, D), D ** -0.5, 0.15625, ((2, 4),))
    conv_kernel = normal_values(keys[4], (KW, D), KW ** -0.5, 3.5, ((1, 4),))
    conv_out = normal_values(keys[5], (D, D), D ** -0.5, 0.15625, ((0, 4),))
    norm_mlp_one = jnp.clip(1.0 + 0.1 * jax.random.normal(keys[6], (D,), jnp.float32), 0.5, 1.5)
    gate_up_one = normal_values(keys[7], (D, 2, FF), D ** -0.5, 0.15625, ((2, 4),))
    down_one = normal_values(keys[8], (FF, D), FF ** -0.5, 0.078125, ((0, 4),))
    norm_attn = jnp.clip(1.0 + 0.1 * jax.random.normal(keys[9], (D,), jnp.float32), 0.5, 1.5)
    query_weight = normal_values(keys[10], (D, HEADS * HEAD), D ** -0.5, 0.15625, ((1, 4),))
    kv_weight = normal_values(keys[11], (D, 2, KV_HEADS * HEAD), D ** -0.5, 0.15625, ((2, 4),))
    query_gain = jnp.clip(1.0 + 0.1 * jax.random.normal(keys[12], (HEAD,), jnp.float32), 0.5, 1.5)
    key_gain = jnp.clip(1.0 + 0.1 * jax.random.normal(keys[13], (HEAD,), jnp.float32), 0.5, 1.5)
    attn_out = normal_values(keys[14], (HEADS * HEAD, D), (HEADS * HEAD // 16) ** -0.5, 0.625, ((0, 4),))
    norm_mlp_two = jnp.clip(1.0 + 0.1 * jax.random.normal(keys[15], (D,), jnp.float32), 0.5, 1.5)
    gate_up_two = normal_values(keys[16], (D, 2, FF), D ** -0.5, 0.15625, ((2, 4),))
    down_two = normal_values(keys[17], (FF, D), FF ** -0.5, 0.078125, ((0, 4),))
    cotangent = normal_values(keys[18], (TOKENS, D), 1.0, 6.0, ((0, 8),))
    return {"tokens": tokens, "lengths": lengths, "norm_conv": norm_conv, "conv_in": conv_in, "conv_kernel": conv_kernel, "conv_out": conv_out, "norm_mlp_one": norm_mlp_one, "gate_up_one": gate_up_one, "down_one": down_one, "norm_attn": norm_attn, "query_weight": query_weight, "kv_weight": kv_weight, "query_gain": query_gain, "key_gain": key_gain, "attn_out": attn_out, "norm_mlp_two": norm_mlp_two, "gate_up_two": gate_up_two, "down_two": down_two, "cotangent": cotangent}


@jax.custom_vjp
def low(v):
    return lax.optimization_barrier(v.astype(jnp.bfloat16)).astype(jnp.float32)

@jax.custom_vjp
def low_back(v):
    return v

def low_keep(v):
    return (low(v), None)

def low_pass(kept, grad):
    return (grad,)

def back_keep(v):
    return (v, None)

def back_low(kept, grad):
    return (low(grad),)
low.defvjp(low_keep, low_pass)
low_back.defvjp(back_keep, back_low)
EPSILON = 1e-05
THETA = 1000000.0
HIGHEST = lax.Precision.HIGHEST

def product(left, right):
    return jnp.dot(left, right, precision=HIGHEST)

def rms_norm(values, gain):
    inverse = lax.rsqrt(lax.optimization_barrier(jnp.mean(values * values, axis=-1, keepdims=True)) + EPSILON)
    return values * inverse * gain

def rope_tables(positions):
    frequency = THETA ** (-2.0 * jnp.arange(HEAD // 2).astype(jnp.float32) / HEAD)
    angles = positions[:, None] * frequency[None, :]
    angles = jnp.concatenate([angles, angles], axis=-1)[:, None, :]
    return (jnp.cos(angles), jnp.sin(angles))

def rotate(values, cosine, sine_table):
    middle = values.shape[-1] // 2
    turned = jnp.concatenate([-values[..., middle:], values[..., :middle]], axis=-1)
    return values * cosine + turned * sine_table

def conv_mixer(hidden, gain, conv_in, conv_kernel, conv_out):
    normed = low(rms_norm(hidden, gain))
    projected = low_back(product(normed, conv_in.reshape(D, 3 * D)))
    before = projected[:, :D]
    after = projected[:, D:2 * D]
    signal = projected[:, 2 * D:]
    mixed = before * signal
    padded = jnp.concatenate([jnp.zeros((KW - 1, D), mixed.dtype), mixed], axis=0)
    convolved = conv_kernel[0] * padded[0:SLOTS]
    for offset in range(1, KW):
        convolved = convolved + conv_kernel[offset] * padded[offset:offset + SLOTS]
    gated = low(after * convolved)
    return low_back(product(gated, conv_out))

def feed_forward(hidden, gain, gate_up, down):
    normed = low(rms_norm(hidden, gain))
    joined = low_back(product(normed, gate_up.reshape(D, 2 * FF)))
    active = low(jax.nn.silu(joined[:, :FF]) * joined[:, FF:])
    return low_back(product(active, down))

def attention(hidden, gain, query_weight, kv_weight, query_gain, key_gain, attn_out, is_valid, cosine, sine_table):
    normed = low(rms_norm(hidden, gain))
    queries = low_back(product(normed, query_weight)).reshape(SLOTS, HEADS, HEAD)
    joined = low_back(product(normed, kv_weight.reshape(D, 2 * KV_HEADS * HEAD)))
    key_rows = joined[:, :KV_HEADS * HEAD].reshape(SLOTS, KV_HEADS, HEAD)
    value_rows = low(joined[:, KV_HEADS * HEAD:].reshape(SLOTS, KV_HEADS, HEAD))
    queries = low(rotate(rms_norm(queries, query_gain), cosine, sine_table))
    key_rows = low(rotate(rms_norm(key_rows, key_gain), cosine, sine_table))
    grouped = queries.reshape(SPAN, TOK_DEV, KV_HEADS, GROUP, HEAD)
    starts = jnp.arange(SPAN, dtype=jnp.int32) * TOK_DEV
    key_index = jnp.arange(SLOTS, dtype=jnp.int32)
    factor = HEAD ** (-0.5)

    def block(items):
        query_block, start = items
        raw = jnp.einsum('qkgd,skd->kgqs', query_block, key_rows, precision=HIGHEST)
        scores = low_back(raw) * factor
        query_index = start + jnp.arange(TOK_DEV, dtype=jnp.int32)
        allowed = (key_index[None, :] <= query_index[:, None]) & is_valid[None, :]
        scores = jnp.where(allowed, scores, -1e+30)
        peak = lax.optimization_barrier(jnp.max(scores, axis=-1, keepdims=True))
        expo = jnp.exp(scores - peak)
        weights = low(expo / lax.optimization_barrier(jnp.sum(expo, axis=-1, keepdims=True)))
        return jnp.einsum('kgqs,skd->qkgd', weights, value_rows, precision=HIGHEST)
    attended = lax.map(jax.checkpoint(block), (grouped, starts))
    attended = low(low_back(attended.reshape(SLOTS, HEADS * HEAD)))
    return low_back(product(attended, attn_out))

def both_layers(sequence, weights, is_valid, cosine, sine_table):
    norm_conv, conv_in, conv_kernel, conv_out, norm_mlp_one, gate_up_one, down_one, norm_attn, query_weight, kv_weight, query_gain, key_gain, attn_out, norm_mlp_two, gate_up_two, down_two = weights
    hidden = sequence + conv_mixer(sequence, norm_conv, conv_in, conv_kernel, conv_out)
    hidden = hidden + feed_forward(hidden, norm_mlp_one, gate_up_one, down_one)
    hidden = hidden + attention(hidden, norm_attn, query_weight, kv_weight, query_gain, key_gain, attn_out, is_valid, cosine, sine_table)
    return hidden + feed_forward(hidden, norm_mlp_two, gate_up_two, down_two)

def add_arrays(first_array, second_array):
    return first_array + second_array

def reference(tokens, lengths, norm_conv, conv_in, conv_kernel, conv_out, norm_mlp_one, gate_up_one, down_one, norm_attn, query_weight, kv_weight, query_gain, key_gain, attn_out, norm_mlp_two, gate_up_two, down_two, cotangent):
    weights = tuple((item.astype(jnp.float32) for item in (norm_conv, conv_in, conv_kernel, conv_out, norm_mlp_one, gate_up_one, down_one, norm_attn, query_weight, kv_weight, query_gain, key_gain, attn_out, norm_mlp_two, gate_up_two, down_two)))
    sequences = tokens.astype(jnp.float32).reshape(NSEQ, SLOTS, D)
    gradients = cotangent.astype(jnp.float32).reshape(NSEQ, SLOTS, D)
    cosine, sine_table = rope_tables(jnp.arange(SLOTS).astype(jnp.float32))

    def one_sequence(totals, items):
        sequence, incoming, length = items
        is_valid = jnp.arange(SLOTS, dtype=jnp.int32) < length

        def forward(values, params):
            return both_layers(values, params, is_valid, cosine, sine_table)
        result, pullback = jax.vjp(forward, sequence, weights)
        grad_input, grad_weights = pullback(incoming * is_valid[:, None].astype(jnp.float32))
        totals = jax.tree.map(add_arrays, totals, grad_weights)
        return (totals, (result, grad_input))
    zeros = jax.tree.map(jnp.zeros_like, weights)
    totals, (results, grad_inputs) = lax.scan(one_sequence, zeros, (sequences, gradients, lengths))
    return (results.reshape(TOKENS, D).astype(jnp.bfloat16), grad_inputs.reshape(TOKENS, D), totals[0], totals[1], totals[2], totals[3], totals[4], totals[5], totals[6], totals[7], totals[8], totals[9], totals[10], totals[11], totals[12], totals[13], totals[14], totals[15])
```

```python
import jax
import jax.numpy as jnp
from jax import lax
from jax.sharding import PartitionSpec as P

HEAD = 64
KW = 3
SPAN = 4
GROUP = 3


EPSILON = 1e-05
THETA = 1000000.0
BF16 = jnp.bfloat16
F32 = jnp.float32


def matmul(left, right):
    return jnp.dot(left, right, preferred_element_type=F32)


def outer_sum(left, right):
    return lax.dot_general(left, right, (((0,), (0,)), ((), ())), preferred_element_type=F32)


def inner_back(left, right):
    return lax.dot_general(left, right, (((1,), (1,)), ((), ())), preferred_element_type=F32)


def normalize(values, gain):
    inverse = lax.rsqrt(jnp.mean(values * values, axis=-1, keepdims=True) + EPSILON)
    return (values * inverse * gain, inverse)


def normalize_back(values, inverse, gain, grad_result):
    weighted = grad_result * gain
    grad_gain = jnp.sum(grad_result * values * inverse, axis=tuple(range(values.ndim - 1)))
    inner = jnp.mean(weighted * values, axis=-1, keepdims=True)
    grad_values = inverse * (weighted - values * inverse * inverse * inner)
    return (grad_values, grad_gain)


def rotate(values, cosine, sine_table):
    middle = values.shape[-1] // 2
    turned = jnp.concatenate([-values[..., middle:], values[..., :middle]], axis=-1)
    return values * cosine + turned * sine_table


def rotate_back(grads, cosine, sine_table):
    middle = grads.shape[-1] // 2
    scaled = grads * sine_table
    turned = jnp.concatenate([scaled[..., middle:], -scaled[..., :middle]], axis=-1)
    return grads * cosine + turned


def swap(block, axis, bit):
    route = [(i, i ^ bit) for i in range(lax.axis_size(axis))]
    return lax.ppermute(block, axis, route)


def scatter_rows(partial_b):
    rows = partial_b.shape[0]
    half, quarter = rows // 2, rows // 4
    got = swap(partial_b[half:], "tensor", 1)
    far = (partial_b[quarter:half].astype(F32) + got[quarter:].astype(F32)).astype(BF16)
    got_far = swap(far, "tensor", 2)
    own = partial_b[:quarter].astype(F32) + got[:quarter].astype(F32)
    return own + got_far.astype(F32)


def gather_rows(own):
    pair = jnp.concatenate([own, swap(own, "tensor", 2)], axis=0)
    return jnp.concatenate([pair, swap(pair, "tensor", 1)], axis=0)


def block_owners(index):
    return [index, index ^ 2, index ^ 1, index ^ 3]


def to_local(values, index):
    quarter = values.shape[0] // 4
    return jnp.concatenate(
        [lax.dynamic_slice_in_dim(values, o * quarter, quarter) for o in block_owners(index)]
    )


def to_true(values, index):
    quarter = values.shape[0] // 4
    places = []
    for block in range(4):
        shift = block ^ index
        place = ((shift & 1) << 1) | (shift >> 1)
        places.append(lax.dynamic_slice_in_dim(values, place * quarter, quarter))
    return jnp.concatenate(places)


def ring_order(count):
    return list(range(0, count, 2)) + [i for i in range(count - 1, -1, -1) if i % 2 == 1]


class Ring:
    def __init__(self, count):
        self.count = count
        self.order = ring_order(count)
        place = [0] * count
        for at, device in enumerate(self.order):
            place[device] = at
        self.place = jnp.array(place, jnp.int32)[lax.axis_index("dp")]
        self.table = jnp.array(self.order, jnp.int32)
        pairs = [(self.order[i], self.order[(i + 1) % count]) for i in range(count)]
        self.routes = (pairs, [(b, a) for a, b in pairs])

    def owner(self, distance):
        return self.table[lax.rem(self.place + distance + self.count, self.count)]

    def sum_scatter(self, grads):
        rows = grads.shape[0] // self.count
        half = rows // 2
        sums = []
        for side in range(2):
            sign = -1 if side == 0 else 1
            held = None
            for step in range(self.count):
                owner = self.owner(sign * (step + 1)) if step < self.count - 1 else lax.axis_index("dp")
                term = lax.dynamic_slice_in_dim(grads, owner * rows + side * half, half if side == 0 else rows - half)
                if held is None:
                    total = term
                else:
                    total = held.astype(F32) + term.astype(F32)
                if step < self.count - 1:
                    held = lax.ppermute(total.astype(BF16), "dp", self.routes[side])
            sums.append(total)
        return jnp.concatenate(sums, axis=0)


def split_gate_up(weight):
    return weight[:, 0, :], weight[:, 1, :]


def score_block(grouped, near_keys, positions, key_positions, key_ok, factor):
    raw = (
        jnp.einsum("qkgd,skd->kgqs", grouped, near_keys, preferred_element_type=jnp.float32)
        * factor
    )
    allowed = (key_positions[None, :] <= positions[:, None]) & key_ok[None, :]
    return jnp.where(allowed, raw, -1e30)


def mlp_hidden(normed_b, gate_w, up_w):
    gate = matmul(normed_b, gate_w)
    upward = matmul(normed_b, up_w)
    active_b = (jax.nn.silu(gate) * upward).astype(BF16)
    return gate, upward, active_b


def mlp_back_hidden(grad_b, down, gate, upward):
    grad_active = inner_back(grad_b, down)
    sigma = jax.nn.sigmoid(gate)
    grad_gate = (grad_active * upward * sigma * (1.0 + gate * (1.0 - sigma))).astype(BF16)
    grad_upward = (grad_active * gate * sigma).astype(BF16)
    return grad_gate, grad_upward


def local(
    tokens,
    lengths,
    norm_conv,
    conv_in,
    conv_kernel,
    conv_out,
    norm_mlp_one,
    gate_up_one,
    down_one,
    norm_attn,
    query_weight,
    kv_weight,
    query_gain,
    key_gain,
    attn_out,
    norm_mlp_two,
    gate_up_two,
    down_two,
    cotangent,
):
    row_count = tokens.shape[0]
    width = tokens.shape[1]
    quarter = row_count // 4
    channels = conv_out.shape[0]
    local_heads = query_weight.shape[1] // HEAD
    local_kv = kv_weight.shape[2] // HEAD
    device = lax.axis_index("dp")
    devices = lax.axis_size("dp")
    index = lax.axis_index("tensor")
    sequence = device // SPAN
    place_index = device % SPAN
    length = lengths[sequence]
    ring = Ring(devices)
    offsets = jnp.concatenate(
        [o * quarter + jnp.arange(quarter, dtype=jnp.int32) for o in block_owners(index)]
    )
    positions = place_index * row_count + offsets
    is_valid = positions < length
    frequency = THETA ** (-2.0 * jnp.arange(HEAD // 2, dtype=jnp.float32) / HEAD)
    angles = positions.astype(jnp.float32)[:, None] * frequency[None, :]
    angles = jnp.concatenate([angles, angles], axis=-1)[:, None, :]
    cosine = jnp.cos(angles)
    sine_table = jnp.sin(angles)
    factor = HEAD ** (-0.5)
    kernel = conv_kernel.astype(jnp.float32)
    rim_rows = KW - 1
    gate_one, up_one = split_gate_up(gate_up_one)
    gate_two, up_two = split_gate_up(gate_up_two)
    forward_route = [(i, i + 1) for i in range(devices - 1) if (i + 1) % SPAN]
    backward_route = [(b, a) for a, b in forward_route]

    inputs = tokens.astype(F32)
    normed_conv, inverse_conv = normalize(inputs, norm_conv)
    normed_conv_b = normed_conv.astype(BF16)
    weight_in = conv_in.reshape(width, 3 * channels)
    projected = matmul(normed_conv_b, weight_in)
    before = projected[:, :channels]
    after = projected[:, channels : 2 * channels]
    signal = projected[:, 2 * channels :]
    mixed = before * signal
    rim_in = lax.ppermute(mixed[row_count - rim_rows :], "dp", forward_route)
    padded = jnp.concatenate([rim_in, mixed], axis=0)
    convolved = kernel[0] * padded[0:row_count]
    for offset in range(1, KW):
        convolved = convolved + kernel[offset] * padded[offset : offset + row_count]
    gated_b = to_local((after * convolved).astype(BF16), index)
    inputs_own = lax.dynamic_slice_in_dim(tokens, index * quarter, quarter).astype(F32)
    one_own = inputs_own + scatter_rows(matmul(gated_b, conv_out).astype(BF16))

    norm_one, inverse_one = normalize(one_own, norm_mlp_one)
    norm_one_b = gather_rows(norm_one.astype(BF16))
    gate_a, up_a, active_one = mlp_hidden(norm_one_b, gate_one, up_one)
    two_own = one_own + scatter_rows(matmul(active_one, down_one).astype(BF16))

    normed_attn, inverse_attn = normalize(two_own, norm_attn)
    normed_attn_b = gather_rows(normed_attn.astype(BF16))
    kv_flat = kv_weight.reshape(width, 2 * local_kv * HEAD)
    joined = matmul(normed_attn_b, kv_flat)
    key_raw = joined[:, : local_kv * HEAD].reshape(row_count, local_kv, HEAD)
    value_rows = joined[:, local_kv * HEAD :].reshape(row_count, local_kv, HEAD).astype(BF16)
    key_norm, key_inverse = normalize(key_raw, key_gain)
    key_rot = rotate(key_norm, cosine, sine_table).astype(BF16)
    stacked = jnp.stack([key_rot, value_rows])
    pieces = [stacked]
    for distance in range(1, SPAN):
        route = [(i, i + distance) for i in range(devices) if i % SPAN + distance < SPAN]
        pieces.append(lax.ppermute(stacked, "dp", route))
    query_raw = matmul(normed_attn_b, query_weight).reshape(row_count, local_heads, HEAD)
    query_norm, query_inverse = normalize(query_raw, query_gain)
    query_rot = rotate(query_norm, cosine, sine_table).astype(BF16)
    grouped = query_rot.reshape(row_count, local_kv, GROUP, HEAD)
    nearby = jnp.concatenate(pieces, axis=1)
    key_positions = jnp.concatenate([positions - distance * row_count for distance in range(SPAN)])
    key_ok = (key_positions >= 0) & (key_positions < length)
    near_keys = nearby[0]
    near_values = nearby[1]
    scores = score_block(grouped, near_keys, positions, key_positions, key_ok, factor)
    peak = jnp.max(scores, axis=-1, keepdims=True)
    expo = jnp.exp(scores - peak)
    total = jnp.sum(expo, axis=-1, keepdims=True)
    log_total = peak + jnp.log(total)
    weights_b = (expo / total).astype(BF16)
    attended = jnp.einsum(
        "kgqs,skd->qkgd", weights_b, near_values, preferred_element_type=jnp.float32
    )
    attended_b = attended.reshape(row_count, local_heads * HEAD).astype(BF16)
    three_own = two_own + scatter_rows(matmul(attended_b, attn_out).astype(BF16))

    norm_two, inverse_two = normalize(three_own, norm_mlp_two)
    norm_two_b = gather_rows(norm_two.astype(BF16))
    gate_b, up_b, active_two = mlp_hidden(norm_two_b, gate_two, up_two)
    grad_result = to_local(cotangent, index).astype(F32) * is_valid[:, None].astype(F32)
    grad_result_b = grad_result.astype(BF16)
    sum_down_two = ring.sum_scatter(outer_sum(grad_result_b, active_two).astype(BF16))
    grad_gate, grad_up = mlp_back_hidden(grad_result_b, down_two, gate_b, up_b)
    sum_gate_two = ring.sum_scatter(outer_sum(norm_two_b, grad_gate).astype(BF16))
    sum_up_two = ring.sum_scatter(outer_sum(norm_two_b, grad_up).astype(BF16))
    partial_normed = inner_back(grad_gate, gate_two) + inner_back(grad_up, up_two)
    grad_normed = scatter_rows(partial_normed.astype(BF16))
    grad_inner, grad_norm_mlp_two = normalize_back(three_own, inverse_two, norm_mlp_two, grad_normed)
    grad_three = grad_result[:quarter] + grad_inner

    output_own = (three_own + scatter_rows(matmul(active_two, down_two).astype(BF16))).astype(BF16)
    output = to_true(gather_rows(output_own), index)

    grad_branch = gather_rows(grad_three.astype(BF16))
    grad_attn_out = outer_sum(grad_branch, attended_b)
    grad_attended = (
        inner_back(grad_branch, attn_out)
        .astype(BF16)
        .reshape(row_count, local_kv, GROUP, HEAD)
    )
    scores = score_block(grouped, near_keys, positions, key_positions, key_ok, factor)
    probs = jnp.exp(scores - log_total)
    probs_b = probs.astype(BF16)
    grad_probs = jnp.einsum(
        "qkgd,skd->kgqs", grad_attended, near_values, preferred_element_type=jnp.float32
    )
    delta = jnp.sum(probs * grad_probs, axis=-1, keepdims=True)
    grad_scores = (probs * (grad_probs - delta) * factor).astype(BF16)
    grad_query = jnp.einsum(
        "kgqs,skd->qkgd", grad_scores, near_keys, preferred_element_type=jnp.float32
    ).reshape(row_count, local_heads, HEAD)
    grad_keys_near = jnp.einsum(
        "kgqs,qkgd->skd", grad_scores, grouped, preferred_element_type=jnp.float32
    )
    grad_values_near = jnp.einsum(
        "kgqs,qkgd->skd", probs_b, grad_attended, preferred_element_type=jnp.float32
    )
    grad_nearby = jnp.stack([grad_keys_near, grad_values_near])
    owned = grad_nearby[:, :row_count]
    for distance in range(1, SPAN):
        route = [(i + distance, i) for i in range(devices) if i % SPAN + distance < SPAN]
        sent = grad_nearby[:, distance * row_count : (distance + 1) * row_count].astype(BF16)
        owned = owned + lax.ppermute(sent, "dp", route).astype(F32)
    grad_query_raw, part_query_gain = normalize_back(
        query_raw, query_inverse, query_gain, rotate_back(grad_query, cosine, sine_table)
    )
    grad_key_raw, part_key_gain = normalize_back(
        key_raw, key_inverse, key_gain, rotate_back(owned[0], cosine, sine_table)
    )
    grad_query_b = grad_query_raw.reshape(row_count, local_heads * HEAD).astype(BF16)
    grad_joined_b = jnp.concatenate(
        [
            grad_key_raw.reshape(row_count, local_kv * HEAD),
            owned[1].reshape(row_count, local_kv * HEAD),
        ],
        axis=1,
    ).astype(BF16)
    grad_qkv_b = jnp.concatenate([grad_query_b, grad_joined_b], axis=1)
    attn_grads = jnp.concatenate([grad_attn_out, outer_sum(normed_attn_b, grad_qkv_b)], axis=1)
    sum_attn = ring.sum_scatter(attn_grads.astype(BF16))
    partial_normed = inner_back(grad_query_b, query_weight) + inner_back(grad_joined_b, kv_flat)
    grad_normed = scatter_rows(partial_normed.astype(BF16))
    grad_inner, grad_norm_attn = normalize_back(two_own, inverse_attn, norm_attn, grad_normed)
    grad_two = grad_three + grad_inner

    grad_two_b = gather_rows(grad_two.astype(BF16))
    sum_down_one = ring.sum_scatter(outer_sum(grad_two_b, active_one).astype(BF16))
    grad_gate, grad_up = mlp_back_hidden(grad_two_b, down_one, gate_a, up_a)
    sum_gate_one = ring.sum_scatter(outer_sum(norm_one_b, grad_gate).astype(BF16))
    sum_up_one = ring.sum_scatter(outer_sum(norm_one_b, grad_up).astype(BF16))
    partial_normed = inner_back(grad_gate, gate_one) + inner_back(grad_up, up_one)
    grad_normed = scatter_rows(partial_normed.astype(BF16))
    grad_inner, grad_norm_mlp_one = normalize_back(one_own, inverse_one, norm_mlp_one, grad_normed)
    grad_one = grad_two + grad_inner

    grad_one_b = gather_rows(grad_one.astype(BF16))
    grad_conv_out = outer_sum(grad_one_b, gated_b)
    grad_gated = to_true(inner_back(grad_one_b, conv_out), index)
    grad_after = grad_gated * convolved
    grad_convolved = grad_gated * after
    grad_kernel = jnp.stack(
        [
            jnp.sum(grad_convolved * padded[offset : offset + row_count], axis=0)
            for offset in range(KW)
        ]
    )
    grad_padded = jnp.pad(kernel[0] * grad_convolved, ((0, rim_rows), (0, 0)))
    for offset in range(1, KW):
        grad_padded = grad_padded + jnp.pad(
            kernel[offset] * grad_convolved, ((offset, rim_rows - offset), (0, 0))
        )
    rim_back = lax.ppermute(grad_padded[:rim_rows], "dp", backward_route)
    grad_mixed = grad_padded[rim_rows:] + jnp.pad(rim_back, ((row_count - rim_rows, 0), (0, 0)))
    grad_projected = jnp.concatenate(
        [grad_mixed * signal, grad_after, grad_mixed * before], axis=1
    ).astype(BF16)
    conv_grads = jnp.concatenate([grad_conv_out, outer_sum(normed_conv_b, grad_projected)], axis=1)
    sum_conv = ring.sum_scatter(conv_grads.astype(BF16))
    partial_normed = inner_back(to_local(grad_projected, index), weight_in)
    grad_normed = scatter_rows(partial_normed.astype(BF16))
    norm_input_own, inverse_own = normalize(inputs_own, norm_conv)
    grad_inner, grad_norm_conv = normalize_back(inputs_own, inverse_own, norm_conv, grad_normed)
    grad_inputs = to_true(gather_rows(grad_one + grad_inner), index)

    small = jnp.concatenate(
        [
            grad_norm_conv,
            grad_norm_mlp_one,
            grad_norm_attn,
            grad_norm_mlp_two,
            part_query_gain,
            part_key_gain,
        ]
    )
    for bit in (1, 2):
        small = small + swap(small, "tensor", bit)
    small = jnp.concatenate([small, grad_kernel.reshape(-1)])
    bit = 1
    while bit < devices:
        small = small + swap(small, "dp", bit)
        bit *= 2
    tap_sums = small[4 * width + 2 * HEAD :].reshape(KW, channels)

    out_rows = width // devices
    return (
        output,
        grad_inputs,
        small[:width],
        sum_conv[:, channels:].reshape(out_rows, 3, channels),
        tap_sums,
        sum_conv[:, :channels].T,
        small[width : 2 * width],
        jnp.stack([sum_gate_one, sum_up_one], axis=1),
        sum_down_one.T,
        small[2 * width : 3 * width],
        sum_attn[:, local_heads * HEAD : 2 * local_heads * HEAD],
        sum_attn[:, 2 * local_heads * HEAD :].reshape(out_rows, 2, local_kv * HEAD),
        small[4 * width : 4 * width + HEAD],
        small[4 * width + HEAD : 4 * width + 2 * HEAD],
        sum_attn[:, : local_heads * HEAD].T,
        small[3 * width : 4 * width],
        jnp.stack([sum_gate_two, sum_up_two], axis=1),
        sum_down_two.T,
    )


def solution(mesh):
    in_specs = (
        P("dp", None),
        P(),
        P(),
        P(None, None, "tensor"),
        P(None, "tensor"),
        P("tensor", None),
        P(),
        P(None, None, "tensor"),
        P("tensor", None),
        P(),
        P(None, "tensor"),
        P(None, None, "tensor"),
        P(),
        P(),
        P("tensor", None),
        P(),
        P(None, None, "tensor"),
        P("tensor", None),
        P("dp", None),
    )
    out_specs = (
        P("dp", None),
        P("dp", None),
        P(),
        P("dp", None, "tensor"),
        P(None, "tensor"),
        P("tensor", "dp"),
        P(),
        P("dp", None, "tensor"),
        P("tensor", "dp"),
        P(),
        P("dp", "tensor"),
        P("dp", None, "tensor"),
        P(),
        P(),
        P("tensor", "dp"),
        P(),
        P("dp", None, "tensor"),
        P("tensor", "dp"),
    )
    return jax.shard_map(local, mesh=mesh, in_specs=in_specs, out_specs=out_specs, check_vma=False)
```

```python
import jax
import jax.numpy as jnp
from jax import lax
from jax.experimental import pallas as pl
from jax.experimental.pallas import tpu as pltpu
from jax.sharding import PartitionSpec as P

HEAD = 64
KW = 3
SPAN = 4
GROUP = 3


EPSILON = 1e-05
THETA = 1000000.0
BF16 = jnp.bfloat16
F32 = jnp.float32


def matmul(left, right):
    return jnp.dot(left, right, preferred_element_type=F32)


def outer_sum(left, right):
    return lax.dot_general(left, right, (((0,), (0,)), ((), ())), preferred_element_type=F32)


def inner_back(left, right):
    return lax.dot_general(left, right, (((1,), (1,)), ((), ())), preferred_element_type=F32)


def normalize(values, gain):
    inverse = lax.rsqrt(jnp.mean(values * values, axis=-1, keepdims=True) + EPSILON)
    return (values * inverse * gain, inverse)


def normalize_back(values, inverse, gain, grad_result):
    weighted = grad_result * gain
    grad_gain = jnp.sum(grad_result * values * inverse, axis=tuple(range(values.ndim - 1)))
    inner = jnp.mean(weighted * values, axis=-1, keepdims=True)
    grad_values = inverse * (weighted - values * inverse * inverse * inner)
    return (grad_values, grad_gain)


def rotate(values, cosine, sine_table):
    middle = values.shape[-1] // 2
    turned = jnp.concatenate([-values[..., middle:], values[..., :middle]], axis=-1)
    return values * cosine + turned * sine_table


def rotate_back(grads, cosine, sine_table):
    middle = grads.shape[-1] // 2
    scaled = grads * sine_table
    turned = jnp.concatenate([scaled[..., middle:], -scaled[..., :middle]], axis=-1)
    return grads * cosine + turned


def swap(block, axis, bit):
    route = [(i, i ^ bit) for i in range(lax.axis_size(axis))]
    return lax.ppermute(block, axis, route)


CHUNKS = 4
MESH = pl.DeviceIdType.MESH


def greet(peers):
    barrier = pltpu.get_barrier_semaphore()
    for peer in peers:
        pl.semaphore_signal(barrier, inc=1, device_id=peer, device_id_type=MESH)
    pl.semaphore_wait(barrier, len(peers))


def tensor_peers():
    me = lax.axis_index("tensor")
    return [{"tensor": me ^ 1}, {"tensor": me ^ 2}]


def sum_and_gather(partial, gathered, gathered_t, near, across, far, send, recv, compute):
    core, other = tensor_peers()
    quarter = partial.shape[0] // 4
    size = quarter // CHUNKS
    copies = {}

    def copy(kind, at, src, dst, peer):
        number = kind * CHUNKS + at
        made = pltpu.make_async_remote_copy(
            src_ref=src,
            dst_ref=dst,
            send_sem=send.at[number],
            recv_sem=recv.at[number],
            device_id=peer,
            device_id_type=MESH,
        )
        made.start()
        copies[kind, at] = made

    def part(block, at):
        return pl.ds(block * quarter + at * size, size)

    def turn(block):
        if gathered_t is not None:
            rows = slice(block * quarter, (block + 1) * quarter)
            gathered_t[:, rows] = gathered[rows, :].T

    for at in range(CHUNKS):
        copy(0, at, partial.at[part(3, at)], near.at[part(1, at)], core)
    for at in range(CHUNKS):
        copy(1, at, partial.at[part(2, at)], near.at[part(0, at)], core)
    for at in range(CHUNKS):
        copies[0, at].wait_recv()
        far[part(0, at), :] = (
            partial[part(1, at), :].astype(F32) + near[part(1, at), :].astype(F32)
        ).astype(BF16)
        copy(2, at, far.at[part(0, at)], across.at[part(0, at)], other)
    for at in range(CHUNKS):
        copies[1, at].wait_recv()
        copies[2, at].wait_recv()
        total = (
            partial[part(0, at), :].astype(F32)
            + near[part(0, at), :].astype(F32)
            + across[part(0, at), :].astype(F32)
        )
        gathered[part(0, at), :] = compute(total, part(0, at), at == 0)
        copy(3, at, gathered.at[part(0, at)], gathered.at[part(1, at)], other)
        copy(4, at, gathered.at[part(0, at)], gathered.at[part(2, at)], core)
    turn(0)
    for at in range(CHUNKS):
        copies[3, at].wait_recv()
        copy(5, at, gathered.at[part(1, at)], gathered.at[part(3, at)], core)
    turn(1)
    for at in range(CHUNKS):
        copies[4, at].wait_recv()
    turn(2)
    for at in range(CHUNKS):
        copies[5, at].wait_recv()
    turn(3)
    for made in copies.values():
        made.wait_send()


def exchange_scratch(rows, width):
    quarter = rows // 4
    return [
        pltpu.VMEM((2 * quarter, width), BF16),
        pltpu.VMEM((quarter, width), BF16),
        pltpu.VMEM((quarter, width), BF16),
        pltpu.SemaphoreType.DMA((6 * CHUNKS,)),
        pltpu.SemaphoreType.DMA((6 * CHUNKS,)),
    ]


def spread(partial_b, extras, out_shapes, compute, collective_id):
    rows, width = partial_b.shape
    quarter = rows // 4

    def body(*refs):
        partial = refs[0]
        extra_refs = refs[1 : 1 + len(extras)]
        gathered, gathered_t = refs[1 + len(extras) : 3 + len(extras)]
        out_refs = refs[3 + len(extras) : 3 + len(extras) + len(out_shapes)]
        scratch = refs[3 + len(extras) + len(out_shapes) :]
        greet(tensor_peers())
        sum_and_gather(
            partial, gathered, gathered_t, *scratch,
            lambda total, at, first: compute(total, at, extra_refs, out_refs, first),
        )

    vmem = pl.BlockSpec(memory_space=pltpu.VMEM)
    return pl.pallas_call(
        body,
        in_specs=[vmem] * (1 + len(extras)),
        out_specs=[vmem] * (2 + len(out_shapes)),
        out_shape=[
            jax.ShapeDtypeStruct((rows, width), BF16),
            jax.ShapeDtypeStruct((width, rows), BF16),
        ]
        + [jax.ShapeDtypeStruct(shape, F32) for shape in out_shapes],
        scratch_shapes=exchange_scratch(rows, width),
        compiler_params=pltpu.CompilerParams(
            collective_id=collective_id, has_side_effects=True, vmem_limit_bytes=32 * 2**20
        ),
        cost_estimate=pl.CostEstimate(
            flops=20 * quarter * width, bytes_accessed=8 * rows * width, transcendentals=0
        ),
    )(partial_b, *extras)


def norm_spread(partial_b, residual, gain):
    def compute(total, rows, extra_refs, out_refs, first):
        hidden = extra_refs[0][rows, :] + total
        out_refs[0][rows, :] = hidden
        return normalize(hidden, extra_refs[1][...])[0].astype(BF16)

    return spread(partial_b, [residual, gain.reshape(1, -1)], [residual.shape], compute, 1)


def row_back(total, rows, first, hidden, gain, incoming, own, grad_gain):
    values = hidden[rows, :]
    inverse = lax.rsqrt(jnp.mean(values * values, axis=-1, keepdims=True) + EPSILON)
    made, term = normalize_back(values, inverse, gain[...], total)
    made = made + incoming[rows, :]
    if own is not None:
        own[rows, :] = made
    term = term.reshape(1, -1)
    grad_gain[...] = term if first else grad_gain[...] + term
    return made.astype(BF16)


def back_spread(partial_b, hidden, gain, incoming):
    def compute(total, rows, extra_refs, out_refs, first):
        return row_back(total, rows, first, *extra_refs, *out_refs)

    gathered, gathered_t, own, grad_gain = spread(
        partial_b,
        [hidden, gain.reshape(1, -1), incoming],
        [hidden.shape, (1, hidden.shape[1])],
        compute,
        3,
    )
    return gathered, gathered_t, own, grad_gain


def ring_peers(count):
    me = lax.axis_index("dp")
    even = lax.rem(me, 2) == 0
    place = jnp.where(even, me // 2, count - 1 - me // 2)

    def at(position):
        position = lax.rem(position + count, count)
        return jnp.where(position < count // 2, 2 * position, 2 * (count - 1 - position) + 1)

    return at(place + 1), at(place - 1), lambda distance: at(place + distance)


def finish(segments, small, last_partial, hidden, gain, incoming, out_partial, out_hidden, devices, sides):
    width, tokens = segments[0][0][0].shape
    rows = width // devices
    half = rows // sides
    steps = devices - 1
    row_count = last_partial.shape[0]
    lefts, rights = [], []
    plan = []
    for pairs in segments:
        entry = []
        for left, right in pairs:
            if not any(left is o for o in lefts):
                lefts.append(left)
            rights.append(right)
            entry.append(([o is left for o in lefts].index(True), len(rights) - 1))
        plan.append(entry)
    widths = [sum(right.shape[1] for _, right in pairs) for pairs in segments]
    count = len(segments)
    bits = []
    bit = 1
    while bit < devices:
        bits.append(bit)
        bit *= 2
    stages = 2 + len(bits)
    inputs = lefts + rights + [small, last_partial, hidden, gain.reshape(1, -1), incoming, out_partial, out_hidden]

    def body(*refs):
        left_refs = refs[: len(lefts)]
        right_refs = refs[len(lefts) : len(lefts) + len(rights)]
        refs = refs[len(lefts) + len(rights) :]
        small_ref, last_ref, hidden_ref, gain_ref, incoming_ref, outp_ref, outh_ref = refs[:7]
        sums = refs[7 : 7 + count]
        input_grad, output, small_out = refs[7 + count : 10 + count]
        held = refs[10 + count : 10 + 2 * count]
        (send, recv, near, across, far, x_send, x_recv, near2, across2, far2, y_send, y_recv,
         gain_term, slots, s_send, s_recv) = refs[10 + 2 * count :]
        following, previous, owner_at = ring_peers(devices)
        me = lax.axis_index("dp")
        small_peers = tensor_peers() + [{"dp": me ^ bit} for bit in bits]
        greet([{"dp": following}, {"dp": previous}] + small_peers)

        def copy(seg, side, step):
            number = (seg * sides + side) * steps + step
            return pltpu.make_async_remote_copy(
                src_ref=held[seg].at[side, step],
                dst_ref=held[seg].at[side, step + 1],
                send_sem=send.at[number],
                recv_sem=recv.at[number],
                device_id={"dp": following if side == 0 else previous},
                device_id_type=MESH,
            )

        def unit(seg, step, first=False, last=False):
            starts = []
            for side in range(sides):
                if last:
                    owner = me
                else:
                    owner = owner_at(-1 - step if side == 0 else 1 + step)
                starts.append(pl.multiple_of(owner * rows + side * half, 16))
            if not first:
                for side in range(sides):
                    copy(seg, side, step - 1).wait_recv()
            column = 0
            for left, right in plan[seg]:
                pieces = [left_refs[left][pl.ds(start, half), :] for start in starts]
                piece = pieces[0] if sides == 1 else jnp.concatenate(pieces, axis=0)
                made = jnp.dot(piece, right_refs[right][...], preferred_element_type=F32)
                at = slice(column, column + made.shape[1])
                for side in range(sides):
                    value = made[side * half : (side + 1) * half]
                    if not first:
                        value = value + held[seg][side, step, :, at].astype(F32)
                    if last:
                        sums[seg][side * half : (side + 1) * half, at] = value
                    else:
                        held[seg][side, step, :, at] = value.astype(BF16)
                column += made.shape[1]
            if not last:
                for side in range(sides):
                    copy(seg, side, step).start()

        for seg in range(count):
            unit(seg, 0, first=True)
        sum_and_gather(
            last_ref, input_grad, None, near, across, far, x_send, x_recv,
            lambda total, at, first: row_back(
                total, at, first, hidden_ref, gain_ref, incoming_ref, None, gain_term
            ),
        )
        if steps > 1:
            for seg in range(count):
                unit(seg, 1)
        sum_and_gather(
            outp_ref, output, None, near2, across2, far2, y_send, y_recv,
            lambda total, at, first: (outh_ref[at, :] + total).astype(BF16),
        )
        if steps > 2:
            for seg in range(count):
                unit(seg, 2)
        small_out[...] = small_ref[...]
        small_out[0:1, :] = gain_term[...]
        row = lax.broadcasted_iota(jnp.int32, small.shape, 0)
        for stage in range(stages):
            made = pltpu.make_async_remote_copy(
                src_ref=small_out,
                dst_ref=slots.at[stage],
                send_sem=s_send.at[stage],
                recv_sem=s_recv.at[stage],
                device_id=small_peers[stage],
                device_id_type=MESH,
            )
            made.start()
            made.wait()
            if stage < 2:
                small_out[...] += jnp.where(row < 5, slots[stage], 0.0)
            else:
                small_out[...] += slots[stage]

        @pl.loop(3, steps)
        def _(step):
            for seg in range(count):
                unit(seg, step)

        for seg in range(count):
            unit(seg, steps, last=True)

        @pl.loop(0, steps)
        def _(step):
            for seg in range(count):
                for side in range(sides):
                    copy(seg, side, step).wait_send()

    vmem = pl.BlockSpec(memory_space=pltpu.VMEM)
    copies = count * sides * steps
    return pl.pallas_call(
        body,
        in_specs=[vmem] * len(inputs),
        out_specs=[vmem] * (count + 3),
        out_shape=[jax.ShapeDtypeStruct((rows, w), F32) for w in widths]
        + [jax.ShapeDtypeStruct((row_count, width), BF16)] * 2
        + [jax.ShapeDtypeStruct(small.shape, F32)],
        scratch_shapes=[pltpu.VMEM((sides, devices, half, w), BF16) for w in widths]
        + [pltpu.SemaphoreType.DMA((copies,)), pltpu.SemaphoreType.DMA((copies,))]
        + exchange_scratch(row_count, width)
        + exchange_scratch(row_count, width)
        + [
            pltpu.VMEM((1, width), F32),
            pltpu.VMEM((stages,) + small.shape, F32),
            pltpu.SemaphoreType.DMA((stages,)),
            pltpu.SemaphoreType.DMA((stages,)),
        ],
        compiler_params=pltpu.CompilerParams(
            collective_id=4, has_side_effects=True, vmem_limit_bytes=62 * 2**20
        ),
    )(*inputs)


def block_owners(index):
    return [index, index ^ 2, index ^ 1, index ^ 3]


def to_local(values, index):
    quarter = values.shape[0] // 4
    return jnp.concatenate(
        [lax.dynamic_slice_in_dim(values, o * quarter, quarter) for o in block_owners(index)]
    )


def to_true(values, index):
    quarter = values.shape[0] // 4
    places = []
    for block in range(4):
        shift = block ^ index
        place = ((shift & 1) << 1) | (shift >> 1)
        places.append(lax.dynamic_slice_in_dim(values, place * quarter, quarter))
    return jnp.concatenate(places)


def ring_order(count):
    return list(range(0, count, 2)) + [i for i in range(count - 1, -1, -1) if i % 2 == 1]


class Ring:
    def __init__(self, count):
        self.count = count
        self.order = ring_order(count)
        place = [0] * count
        for at, device in enumerate(self.order):
            place[device] = at
        self.place = jnp.array(place, jnp.int32)[lax.axis_index("dp")]
        self.table = jnp.array(self.order, jnp.int32)
        pairs = [(self.order[i], self.order[(i + 1) % count]) for i in range(count)]
        self.routes = (pairs, [(b, a) for a, b in pairs])

    def owner(self, distance):
        return self.table[lax.rem(self.place + distance + self.count, self.count)]


def piece_plan(width, devices):
    rows = width // devices
    return (2, 2) if rows % 64 == 0 else (1, 1)


def outer_pieces(pairs, devices, parts, sides, stack):
    tokens, width = pairs[0][0].shape
    rows = width // devices
    pieces = parts * sides
    size = rows // pieces
    step = max(rows, 384 // rows * rows)
    while width % step:
        step -= rows
    owners = step // rows
    lefts = []
    for left, _ in pairs:
        if not any(left is o for o in lefts):
            lefts.append(left)
    which = [[o is left for o in lefts].index(True) for left, _ in pairs]
    widths = [right.shape[1] for _, right in pairs]
    count = len(pairs)
    if stack:
        shape = (devices * pieces, size * count, widths[0])
    else:
        shape = (devices * pieces, size, sum(widths))

    def body(*refs):
        left_refs, right_refs, out = refs[: len(lefts)], refs[len(lefts) : -1], refs[-1]
        column = 0
        for at in range(count):
            made = lax.dot_general(
                left_refs[which[at]][...],
                right_refs[at][...],
                (((0,), (0,)), ((), ())),
                preferred_element_type=F32,
            ).astype(BF16)
            for piece in range(owners * pieces):
                value = made[piece * size : (piece + 1) * size]
                if stack:
                    out[piece, at * size : (at + 1) * size, :] = value
                else:
                    out[piece, :, column : column + widths[at]] = value
            column += widths[at]

    block = (owners * pieces,) + shape[1:]
    return pl.pallas_call(
        body,
        grid=(width // step,),
        in_specs=[pl.BlockSpec((tokens, step), lambda i: (0, i)) for _ in lefts]
        + [pl.BlockSpec((tokens, w), lambda i: (0, 0)) for w in widths],
        out_specs=pl.BlockSpec(block, lambda i: (i, 0, 0)),
        out_shape=jax.ShapeDtypeStruct(shape, BF16),
        compiler_params=pltpu.CompilerParams(vmem_limit_bytes=56 * 2**20),
        cost_estimate=pl.CostEstimate(
            flops=2 * tokens * width * sum(widths),
            bytes_accessed=2 * width * sum(widths) + 2 * tokens * (width + sum(widths)),
            transcendentals=0,
        ),
    )(*lefts, *[right for _, right in pairs])


class Job:
    def __init__(self, ring, arrays, part, parts, sides):
        self.ring, self.arrays = ring, arrays
        self.part, self.parts, self.sides = part, parts, sides
        self.step = 0
        self.held = None
        self.sums = None

    def terms(self, side):
        ring = self.ring
        if self.step < ring.count - 1:
            owner = ring.owner((self.step + 1) * (-1 if side == 0 else 1))
        else:
            owner = lax.axis_index("dp")
        at = (owner * self.parts + self.part) * self.sides + side
        return [lax.dynamic_index_in_dim(g, at, keepdims=False) for g in self.arrays]

    def advance(self, tied):
        last = self.step == self.ring.count - 1
        if self.held is not None:
            self.held, tied = lax.optimization_barrier((self.held, tied))
        totals = []
        for side in range(self.sides):
            terms = self.terms(side)
            if self.held is not None:
                terms = [h.astype(F32) + t.astype(F32) for h, t in zip(self.held[side], terms)]
            totals.append(terms)
        self.step += 1
        if last:
            self.sums = totals
            return tied
        totals = [[t.astype(BF16) for t in side] for side in totals]
        totals, tied = lax.optimization_barrier((totals, tied))
        self.held = [
            [lax.ppermute(t, "dp", self.ring.routes[side]) for t in totals[side]]
            for side in range(self.sides)
        ]
        return tied

    def result(self, at, stacked=1):
        found = []
        for number in range(stacked):
            pieces = []
            for side in range(self.sides):
                value = self.sums[side][at]
                size = value.shape[0] // stacked
                pieces.append(value[number * size : (number + 1) * size])
            found.append(jnp.concatenate(pieces, axis=0))
        return found


def drive(main):
    jobs, turn, tied = [], 0, None
    running = True
    while running or jobs:
        if running:
            try:
                made = main.send(tied)
            except StopIteration as stop:
                outcome, running, tied = stop.value, False, None
            else:
                tied = made
                if isinstance(made, Job):
                    jobs.append(made)
                    continue
        if jobs:
            job = jobs[turn % len(jobs)]
            tied = job.advance(tied)
            if job.sums is None:
                turn += 1
            else:
                jobs.remove(job)
    return outcome


def split_gate_up(weight):
    return weight[:, 0, :], weight[:, 1, :]


def head_columns(ref, head):
    return ref[:, head * HEAD : (head + 1) * HEAD]


def cross(left, right):
    return lax.dot_general(left, right, (((1,), (1,)), ((), ())), preferred_element_type=F32)


def fill_bias(bias, length_ref, row_positions, column_positions):
    keys = column_positions[...]
    allowed = (keys <= row_positions[...]) & (keys < length_ref[0])
    bias[...] = jnp.where(allowed, 0.0, -1e30)


def attention_forward(query, pieces, place, length, positions):
    rows, columns = query.shape
    heads = columns // HEAD
    kv_columns = heads // GROUP * HEAD
    count = len(pieces)

    def body(place_ref, length_ref, row_pos, column_pos, q_ref, *refs):
        piece_refs, (out, out_t, log_total, near, bias, total_ref) = refs[:count], refs[count:]
        for at in range(1, count):
            near[at] = piece_refs[at][...]
        fill_bias(bias, length_ref, row_pos, column_pos)

        def part(q, keys, values_t, masked):
            scores = cross(keys, q)
            if masked:
                scores = scores + bias[...]
            expo = jnp.exp(scores)
            return (
                jnp.dot(values_t, expo.astype(BF16), preferred_element_type=F32),
                jnp.sum(expo, axis=0, keepdims=True),
            )

        for head in range(heads):
            first = head // GROUP * HEAD
            q = head_columns(q_ref, head)
            keys = piece_refs[0][:, first : first + HEAD]
            values = piece_refs[0][:, kv_columns + first : kv_columns + first + HEAD]
            made, total = part(q, keys, values.T, True)
            out_t[head * HEAD : (head + 1) * HEAD, :] = made
            total_ref[...] = total

            @pl.loop(1, place_ref[0] + 1)
            def _(at):
                keys = near[at, :, first : first + HEAD]
                values = near[at, :, kv_columns + first : kv_columns + first + HEAD]
                made, total = part(q, keys, values.T, False)
                out_t[head * HEAD : (head + 1) * HEAD, :] += made
                total_ref[...] += total

            total = total_ref[...]
            made = out_t[head * HEAD : (head + 1) * HEAD, :] / total
            out_t[head * HEAD : (head + 1) * HEAD, :] = made
            out[:, head * HEAD : (head + 1) * HEAD] = made.T.astype(BF16)
            log_total[head : head + 1, :] = jnp.log(total)

    vmem = pl.BlockSpec(memory_space=pltpu.VMEM)
    smem = pl.BlockSpec(memory_space=pltpu.SMEM)
    return pl.pallas_call(
        body,
        in_specs=[smem, smem] + [vmem] * (3 + count),
        out_specs=[vmem] * 3,
        out_shape=[
            jax.ShapeDtypeStruct((rows, columns), BF16),
            jax.ShapeDtypeStruct((columns, rows), F32),
            jax.ShapeDtypeStruct((heads, rows), F32),
        ],
        scratch_shapes=[
            pltpu.VMEM((count, rows, 2 * kv_columns), BF16),
            pltpu.VMEM((rows, rows), F32),
            pltpu.VMEM((1, rows), F32),
        ],
        compiler_params=pltpu.CompilerParams(vmem_limit_bytes=48 * 2**20),
        cost_estimate=pl.CostEstimate(
            flops=4 * rows * rows * count * columns * 4,
            bytes_accessed=10 * rows * columns,
            transcendentals=rows * rows * count * heads,
        ),
    )(
        place.reshape(1),
        length.reshape(1),
        positions.reshape(1, rows),
        positions.reshape(rows, 1),
        query,
        *pieces,
    )


def attention_backward(query, pieces, out_t, log_total, grad, place, length, positions):
    rows, columns = query.shape
    heads = columns // HEAD
    kv_heads = heads // GROUP
    kv_columns = kv_heads * HEAD
    count = len(pieces)

    def body(place_ref, length_ref, row_pos, column_pos, q_ref, o_ref, log_ref, g_ref, *refs):
        piece_refs, (grad_q, own, far, near, bias, grad_q_t, delta) = refs[:count], refs[count:]
        for at in range(1, count):
            near[at] = piece_refs[at][...]
        fill_bias(bias, length_ref, row_pos, column_pos)
        grad_q_t[...] = jnp.zeros_like(grad_q_t)
        for head in range(heads):
            at = slice(head * HEAD, (head + 1) * HEAD)
            grad_t = g_ref[:, at].astype(F32).T
            delta[head : head + 1, :] = jnp.sum(grad_t * o_ref[at, :], axis=0, keepdims=True)

        def part(read, write, masked):
            for group in range(kv_heads):
                first = group * HEAD
                keys = read(first)
                values = read(kv_columns + first)
                keys_t = keys.T
                grad_k = grad_v = None
                for head in range(group * GROUP, (group + 1) * GROUP):
                    at = slice(head * HEAD, (head + 1) * HEAD)
                    q, grads = q_ref[:, at], g_ref[:, at]
                    scores = cross(keys, q) - log_ref[head : head + 1, :]
                    if masked:
                        scores = scores + bias[...]
                    probs = jnp.exp(scores)
                    made = jnp.dot(probs.astype(BF16), grads, preferred_element_type=F32)
                    grad_v = made if grad_v is None else grad_v + made
                    grad_probs = cross(values, grads)
                    grad_scores = (probs * (grad_probs - delta[head : head + 1, :])).astype(BF16)
                    made = jnp.dot(grad_scores, q, preferred_element_type=F32)
                    grad_k = made if grad_k is None else grad_k + made
                    grad_q_t[at, :] += jnp.dot(keys_t, grad_scores, preferred_element_type=F32)
                write(first, grad_k)
                write(kv_columns + first, grad_v)

        def write_own(column, value):
            own[:, column : column + HEAD] = value

        part(lambda column: piece_refs[0][:, column : column + HEAD], write_own, True)

        @pl.loop(1, place_ref[0] + 1)
        def _(at):
            def write_far(column, value):
                far[at - 1, :, column : column + HEAD] = value.astype(BF16)

            part(lambda column: near[at, :, column : column + HEAD], write_far, False)

        for head in range(heads):
            at = slice(head * HEAD, (head + 1) * HEAD)
            grad_q[:, at] = grad_q_t[at, :].T * HEAD ** (-0.5)

    vmem = pl.BlockSpec(memory_space=pltpu.VMEM)
    smem = pl.BlockSpec(memory_space=pltpu.SMEM)
    return pl.pallas_call(
        body,
        in_specs=[smem, smem] + [vmem] * (6 + count),
        out_specs=[vmem] * 3,
        out_shape=[
            jax.ShapeDtypeStruct((rows, columns), F32),
            jax.ShapeDtypeStruct((rows, 2 * kv_columns), F32),
            jax.ShapeDtypeStruct((count - 1, rows, 2 * kv_columns), BF16),
        ],
        scratch_shapes=[
            pltpu.VMEM((count, rows, 2 * kv_columns), BF16),
            pltpu.VMEM((rows, rows), F32),
            pltpu.VMEM((columns, rows), F32),
            pltpu.VMEM((heads, rows), F32),
        ],
        compiler_params=pltpu.CompilerParams(vmem_limit_bytes=48 * 2**20),
        cost_estimate=pl.CostEstimate(
            flops=10 * rows * rows * count * columns * 4,
            bytes_accessed=20 * rows * columns,
            transcendentals=rows * rows * count * heads,
        ),
    )(
        place.reshape(1),
        length.reshape(1),
        positions.reshape(1, rows),
        positions.reshape(rows, 1),
        query,
        out_t,
        log_total,
        grad,
        *pieces,
    )


def mlp_hidden(normed_b, gate_w, up_w):
    gate = matmul(normed_b, gate_w)
    upward = matmul(normed_b, up_w)
    active_b = (jax.nn.silu(gate) * upward).astype(BF16)
    return gate, upward, active_b


def mlp_back_hidden(grad_b, down, gate, upward):
    grad_active = inner_back(grad_b, down)
    sigma = jax.nn.sigmoid(gate)
    grad_gate = (grad_active * upward * sigma * (1.0 + gate * (1.0 - sigma))).astype(BF16)
    grad_upward = (grad_active * gate * sigma).astype(BF16)
    return grad_gate, grad_upward


def local(
    tokens,
    lengths,
    norm_conv,
    conv_in,
    conv_kernel,
    conv_out,
    norm_mlp_one,
    gate_up_one,
    down_one,
    norm_attn,
    query_weight,
    kv_weight,
    query_gain,
    key_gain,
    attn_out,
    norm_mlp_two,
    gate_up_two,
    down_two,
    cotangent,
):
    row_count = tokens.shape[0]
    width = tokens.shape[1]
    quarter = row_count // 4
    channels = conv_out.shape[0]
    local_heads = query_weight.shape[1] // HEAD
    local_kv = kv_weight.shape[2] // HEAD
    device = lax.axis_index("dp")
    devices = lax.axis_size("dp")
    index = lax.axis_index("tensor")
    sequence = device // SPAN
    place_index = device % SPAN
    length = lengths[sequence]
    ring = Ring(devices)
    offsets = jnp.concatenate(
        [o * quarter + jnp.arange(quarter, dtype=jnp.int32) for o in block_owners(index)]
    )
    positions = place_index * row_count + offsets
    is_valid = positions < length
    frequency = THETA ** (-2.0 * jnp.arange(HEAD // 2, dtype=jnp.float32) / HEAD)
    angles = positions.astype(jnp.float32)[:, None] * frequency[None, :]
    angles = jnp.concatenate([angles, angles], axis=-1)[:, None, :]
    cosine = jnp.cos(angles)
    sine_table = jnp.sin(angles)
    factor = HEAD ** (-0.5)
    kernel = conv_kernel.astype(jnp.float32)
    rim_rows = KW - 1
    gate_one, up_one = split_gate_up(gate_up_one)
    gate_two, up_two = split_gate_up(gate_up_two)
    forward_route = [(i, i + 1) for i in range(devices - 1) if (i + 1) % SPAN]
    backward_route = [(b, a) for a, b in forward_route]

    inputs = tokens.astype(F32)
    normed_conv, inverse_conv = normalize(inputs, norm_conv)
    normed_conv_b = normed_conv.astype(BF16)
    weight_in = conv_in.reshape(width, 3 * channels)
    projected = matmul(normed_conv_b, weight_in)
    before = projected[:, :channels]
    after = projected[:, channels : 2 * channels]
    signal = projected[:, 2 * channels :]
    mixed = before * signal
    rim_in = lax.ppermute(mixed[row_count - rim_rows :], "dp", forward_route)
    padded = jnp.concatenate([rim_in, mixed], axis=0)
    convolved = kernel[0] * padded[0:row_count]
    for offset in range(1, KW):
        convolved = convolved + kernel[offset] * padded[offset : offset + row_count]
    gated_b = to_local((after * convolved).astype(BF16), index)
    inputs_own = lax.dynamic_slice_in_dim(tokens, index * quarter, quarter).astype(F32)

    norm_one_b, norm_one_t, one_own = norm_spread(
        matmul(gated_b, conv_out).astype(BF16), inputs_own, norm_mlp_one
    )
    gate_a, up_a, active_one = mlp_hidden(norm_one_b, gate_one, up_one)

    normed_attn_b, normed_attn_t, two_own = norm_spread(
        matmul(active_one, down_one).astype(BF16), one_own, norm_attn
    )
    kv_flat = kv_weight.reshape(width, 2 * local_kv * HEAD)
    joined = matmul(normed_attn_b, kv_flat)
    key_raw = joined[:, : local_kv * HEAD].reshape(row_count, local_kv, HEAD)
    value_rows = joined[:, local_kv * HEAD :].reshape(row_count, local_kv, HEAD).astype(BF16)
    key_norm, key_inverse = normalize(key_raw, key_gain)
    key_rot = rotate(key_norm, cosine, sine_table).astype(BF16)
    stacked = jnp.concatenate(
        [key_rot.reshape(row_count, -1), value_rows.reshape(row_count, -1)], axis=1
    )
    pieces = [stacked]
    for distance in range(1, SPAN):
        route = [(i, i + distance) for i in range(devices) if i % SPAN + distance < SPAN]
        pieces.append(lax.ppermute(stacked, "dp", route))
    query_raw = matmul(normed_attn_b, query_weight).reshape(row_count, local_heads, HEAD)
    query_norm, query_inverse = normalize(query_raw, query_gain)
    query_rot = rotate(query_norm, cosine, sine_table).astype(BF16)
    query_b = (query_rot * factor).astype(BF16).reshape(row_count, local_heads * HEAD)
    attended_b, attended_t, log_total = attention_forward(
        query_b, pieces, place_index, length, positions
    )
    norm_two_b, _, three_own = norm_spread(
        matmul(attended_b, attn_out).astype(BF16), two_own, norm_mlp_two
    )
    gate_b, up_b, active_two = mlp_hidden(norm_two_b, gate_two, up_two)
    grad_result = to_local(cotangent, index).astype(F32) * is_valid[:, None].astype(F32)
    grad_result_b = grad_result.astype(BF16)

    def backward():
        grad_gate, grad_up = mlp_back_hidden(grad_result_b, down_two, gate_b, up_b)
        parts, sides = 1, piece_plan(width, devices)[1]
        two_grads = outer_pieces(
            [(grad_result_b, active_two), (norm_two_b, grad_gate), (norm_two_b, grad_up)],
            devices, parts, sides, True,
        )
        jobs_two = [Job(ring, [two_grads], part, parts, sides) for part in range(parts)]
        for job in jobs_two:
            yield job
        grad_gate, grad_up = yield (grad_gate, grad_up)
        partial_normed = inner_back(grad_gate, gate_two) + inner_back(grad_up, up_two)

        partial_b = yield partial_normed.astype(BF16)
        grad_branch, grad_branch_t, grad_three, grad_norm_mlp_two = back_spread(
            partial_b, three_own, norm_mlp_two, grad_result[:quarter]
        )
        grad_branch = yield grad_branch

        grad_attended = inner_back(grad_branch, attn_out).astype(BF16)
        grad_attended = yield grad_attended
        grad_query, owned, grad_far = attention_backward(
            query_b, pieces, attended_t, log_total, grad_attended, place_index, length, positions
        )
        grad_query, owned, grad_far = yield (grad_query, owned, grad_far)
        grad_query = grad_query.reshape(row_count, local_heads, HEAD)
        arrived = []
        for distance in range(1, SPAN):
            route = [(i + distance, i) for i in range(devices) if i % SPAN + distance < SPAN]
            arrived.append(lax.ppermute(grad_far[distance - 1], "dp", route))
        grad_query_raw, part_query_gain = normalize_back(
            query_raw, query_inverse, query_gain, rotate_back(grad_query, cosine, sine_table)
        )
        yield ()
        for piece in arrived:
            owned = owned + piece.astype(F32)
        grad_key = owned[:, : local_kv * HEAD].reshape(row_count, local_kv, HEAD)
        grad_key_raw, part_key_gain = normalize_back(
            key_raw, key_inverse, key_gain, rotate_back(grad_key, cosine, sine_table)
        )
        grad_query_b = grad_query_raw.reshape(row_count, local_heads * HEAD).astype(BF16)
        grad_joined_b = jnp.concatenate(
            [
                grad_key_raw.reshape(row_count, local_kv * HEAD),
                owned[:, local_kv * HEAD :],
            ],
            axis=1,
        ).astype(BF16)
        grad_query_b, grad_joined_b = yield (grad_query_b, grad_joined_b)
        partial_normed = inner_back(grad_query_b, query_weight) + inner_back(grad_joined_b, kv_flat)

        partial_b = yield partial_normed.astype(BF16)
        grad_two_b, grad_two_t, grad_two, grad_norm_attn = back_spread(
            partial_b, two_own, norm_attn, grad_three
        )
        grad_two_b = yield grad_two_b

        grad_gate, grad_up = mlp_back_hidden(grad_two_b, down_one, gate_a, up_a)
        grad_gate, grad_up = yield (grad_gate, grad_up)
        grad_gate, grad_up = yield (grad_gate, grad_up)
        partial_normed = inner_back(grad_gate, gate_one) + inner_back(grad_up, up_one)
        partial_b = yield partial_normed.astype(BF16)
        grad_one_b, grad_one_t, grad_one, grad_norm_mlp_one = back_spread(
            partial_b, one_own, norm_mlp_one, grad_two
        )
        grad_one_b = yield grad_one_b

        grad_gated = to_true(inner_back(grad_one_b, conv_out), index)
        grad_after = grad_gated * convolved
        grad_convolved = grad_gated * after
        grad_kernel = jnp.stack(
            [
                jnp.sum(grad_convolved * padded[offset : offset + row_count], axis=0)
                for offset in range(KW)
            ]
        )
        grad_padded = jnp.pad(kernel[0] * grad_convolved, ((0, rim_rows), (0, 0)))
        for offset in range(1, KW):
            grad_padded = grad_padded + jnp.pad(
                kernel[offset] * grad_convolved, ((offset, rim_rows - offset), (0, 0))
            )
        rim_back = lax.ppermute(grad_padded[:rim_rows], "dp", backward_route)
        yield ()
        grad_mixed = grad_padded[rim_rows:] + jnp.pad(rim_back, ((row_count - rim_rows, 0), (0, 0)))
        grad_projected = jnp.concatenate(
            [grad_mixed * signal, grad_after, grad_mixed * before], axis=1
        ).astype(BF16)
        partial_b = inner_back(to_local(grad_projected, index), weight_in).astype(BF16)
        partial_b = yield partial_b
        while jobs_two[0].sums is None:
            yield ()
        small = jnp.concatenate(
            [
                jnp.zeros((1, width), F32),
                grad_norm_mlp_one,
                grad_norm_attn,
                grad_norm_mlp_two,
                jnp.pad(
                    jnp.concatenate([part_query_gain, part_key_gain]), (0, width - 2 * HEAD)
                ).reshape(1, width),
                jnp.pad(grad_kernel, ((0, 0), (0, width - channels))),
            ],
            axis=0,
        )
        late_active, partial_b = lax.optimization_barrier((active_two, partial_b))
        out_partial = matmul(late_active, down_two).astype(BF16)
        made = finish(
            [
                [
                    (grad_branch_t, attended_b),
                    (normed_attn_t, grad_query_b),
                    (normed_attn_t, grad_joined_b),
                ],
                [(grad_two_t, active_one)],
                [(norm_one_t, grad_gate)],
                [(norm_one_t, grad_up)],
                [(grad_one_t, gated_b), (normed_conv_b.T, grad_projected)],
            ],
            small,
            partial_b,
            inputs_own,
            norm_conv,
            grad_one,
            out_partial,
            three_own,
            devices,
            sides,
        )
        return made, jobs_two[0].result(0, 3)

    made, sums_two = drive(backward())
    sum_attn, sum_down_one, sum_gate_one, sum_up_one, sum_conv, grad_inputs, output, small = made
    sum_down_two, sum_gate_two, sum_up_two = sums_two
    grad_inputs = to_true(grad_inputs, index).astype(F32)
    output = to_true(output, index)

    out_rows = width // devices
    return (
        output,
        grad_inputs,
        small[0],
        sum_conv[:, channels:].reshape(out_rows, 3, channels),
        small[5:, :channels],
        sum_conv[:, :channels].T,
        small[1],
        jnp.stack([sum_gate_one, sum_up_one], axis=1),
        sum_down_one.T,
        small[2],
        sum_attn[:, local_heads * HEAD : 2 * local_heads * HEAD],
        sum_attn[:, 2 * local_heads * HEAD :].reshape(out_rows, 2, local_kv * HEAD),
        small[4, :HEAD],
        small[4, HEAD : 2 * HEAD],
        sum_attn[:, : local_heads * HEAD].T,
        small[3],
        jnp.stack([sum_gate_two, sum_up_two], axis=1),
        sum_down_two.T,
    )


def solution(mesh):
    in_specs = (
        P("dp", None),
        P(),
        P(),
        P(None, None, "tensor"),
        P(None, "tensor"),
        P("tensor", None),
        P(),
        P(None, None, "tensor"),
        P("tensor", None),
        P(),
        P(None, "tensor"),
        P(None, None, "tensor"),
        P(),
        P(),
        P("tensor", None),
        P(),
        P(None, None, "tensor"),
        P("tensor", None),
        P("dp", None),
    )
    out_specs = (
        P("dp", None),
        P("dp", None),
        P(),
        P("dp", None, "tensor"),
        P(None, "tensor"),
        P("tensor", "dp"),
        P(),
        P("dp", None, "tensor"),
        P("tensor", "dp"),
        P(),
        P("dp", "tensor"),
        P("dp", None, "tensor"),
        P(),
        P(),
        P("tensor", "dp"),
        P(),
        P("dp", None, "tensor"),
        P("tensor", "dp"),
    )
    return jax.shard_map(local, mesh=mesh, in_specs=in_specs, out_specs=out_specs, check_vma=False)
```

```python
import jax
import jax.numpy as jnp
from jax import lax
from jax.experimental import pallas as pl
from jax.experimental.pallas import tpu as pltpu
from jax.sharding import PartitionSpec as P

HEAD = 64
KW = 3
SPAN = 4
GROUP = 3


EPSILON = 1e-05
THETA = 1000000.0
BF16 = jnp.bfloat16
F32 = jnp.float32


def matmul(left, right):
    return jnp.dot(left, right, preferred_element_type=F32)


def inner_back(left, right):
    return lax.dot_general(left, right, (((1,), (1,)), ((), ())), preferred_element_type=F32)


def normalize(values, gain):
    inverse = lax.rsqrt(jnp.mean(values * values, axis=-1, keepdims=True) + EPSILON)
    return (values * inverse * gain, inverse)


def normalize_back(values, inverse, gain, grad_result):
    weighted = grad_result * gain
    grad_gain = jnp.sum(grad_result * values * inverse, axis=tuple(range(values.ndim - 1)))
    inner = jnp.mean(weighted * values, axis=-1, keepdims=True)
    grad_values = inverse * (weighted - values * inverse * inverse * inner)
    return (grad_values, grad_gain)


CHUNKS = 4
SLOTS = 3
MESH = pl.DeviceIdType.MESH


class Refs:
    def __init__(self, names, refs):
        self.__dict__.update(zip(names, refs))


def run_kernel(body, inputs, outputs, scratch, collective_id, limit, flops):
    arrays, specs = [], []
    for value in inputs.values():
        array, space = value if isinstance(value, tuple) else (value, pltpu.VMEM)
        arrays.append(array)
        specs.append(pl.BlockSpec(memory_space=space))
    names = list(inputs) + list(outputs) + list(scratch)
    return pl.pallas_call(
        lambda *refs: body(Refs(names, refs)),
        in_specs=specs,
        out_specs=[pl.BlockSpec(memory_space=pltpu.VMEM)] * len(outputs),
        out_shape=[jax.ShapeDtypeStruct(*value) for value in outputs.values()],
        scratch_shapes=list(scratch.values()),
        compiler_params=pltpu.CompilerParams(
            collective_id=collective_id, has_side_effects=True, vmem_limit_bytes=limit * 2**20
        ),
        cost_estimate=pl.CostEstimate(
            flops=flops,
            bytes_accessed=sum(a.size * a.dtype.itemsize for a in arrays),
            transcendentals=0,
        ),
    )(*arrays)


def greet(peers):
    barrier = pltpu.get_barrier_semaphore()
    for peer in peers:
        pl.semaphore_signal(barrier, inc=1, device_id=peer, device_id_type=MESH)
    pl.semaphore_wait(barrier, len(peers))


def tensor_peers():
    me = lax.axis_index("tensor")
    return [dict(tensor=me ^ 1), dict(tensor=me ^ 2)]


def span_peers():
    me = lax.axis_index("dp")
    place = lax.rem(me, SPAN)
    return [dict(dp=me - place + lax.rem(place + k, SPAN)) for k in range(1, SPAN)]


def remote(src, dst, send, recv, peer):
    return pltpu.make_async_remote_copy(
        src_ref=src, dst_ref=dst, send_sem=send, recv_sem=recv, device_id=peer, device_id_type=MESH
    )


def exchange_scratch(rows, width):
    quarter = rows // 4
    return dict(
        near_rows=pltpu.VMEM((2 * quarter, width), BF16),
        across_rows=pltpu.VMEM((quarter, width), BF16),
        far_rows=pltpu.VMEM((quarter, width), BF16),
        x_send=pltpu.SemaphoreType.DMA((6 * CHUNKS,)),
        x_recv=pltpu.SemaphoreType.DMA((6 * CHUNKS,)),
    )


def sum_and_gather(r, partial, gathered, gathered_t, compute):
    near, across, far = r.near_rows, r.across_rows, r.far_rows
    core, other = tensor_peers()
    quarter = partial.shape[0] // 4
    size = quarter // CHUNKS
    copies = {}

    def copy(kind, at, src, dst, peer):
        number = kind * CHUNKS + at
        copies[kind, at] = remote(src, dst, r.x_send.at[number], r.x_recv.at[number], peer)
        copies[kind, at].start()

    def part(block, at):
        return pl.ds(block * quarter + at * size, size)

    def turn(block):
        if gathered_t is not None:
            rows = slice(block * quarter, (block + 1) * quarter)
            gathered_t[:, rows] = gathered[rows, :].T

    for at in range(CHUNKS):
        copy(0, at, partial.at[part(3, at)], near.at[part(1, at)], core)
    for at in range(CHUNKS):
        copy(1, at, partial.at[part(2, at)], near.at[part(0, at)], core)
    for at in range(CHUNKS):
        copies[0, at].wait_recv()
        far[part(0, at), :] = (
            partial[part(1, at), :].astype(F32) + near[part(1, at), :].astype(F32)
        ).astype(BF16)
        copy(2, at, far.at[part(0, at)], across.at[part(0, at)], other)
    yield 1
    for at in range(CHUNKS):
        copies[1, at].wait_recv()
        copies[2, at].wait_recv()
        total = (
            partial[part(0, at), :].astype(F32)
            + near[part(0, at), :].astype(F32)
            + across[part(0, at), :].astype(F32)
        )
        gathered[part(0, at), :] = compute(total, part(0, at), at == 0)
        copy(3, at, gathered.at[part(0, at)], gathered.at[part(1, at)], other)
        copy(4, at, gathered.at[part(0, at)], gathered.at[part(2, at)], core)
    turn(0)
    yield 1
    for at in range(CHUNKS):
        copies[3, at].wait_recv()
        copy(5, at, gathered.at[part(1, at)], gathered.at[part(3, at)], core)
    turn(1)
    for at in range(CHUNKS):
        copies[4, at].wait_recv()
    turn(2)
    for at in range(CHUNKS):
        copies[5, at].wait_recv()
    turn(3)
    for made in copies.values():
        made.wait_send()
    yield 1


def exhaust(main):
    for _ in main:
        pass


def spread(partial_b, extras, out_shapes, compute, collective_id):
    rows, width = partial_b.shape

    def body(r):
        greet(tensor_peers())
        exhaust(
            sum_and_gather(
                r, r.partial, r.gathered, r.gathered_t, lambda *values: compute(r, *values)
            )
        )

    outputs = dict(gathered=((rows, width), BF16), gathered_t=((width, rows), BF16))
    outputs.update({name: (shape, F32) for name, shape in out_shapes.items()})
    return run_kernel(
        body,
        dict(partial=partial_b, **extras),
        outputs,
        exchange_scratch(rows, width),
        collective_id,
        32,
        10 * rows * width,
    )


def norm_rows(total, rows, residual, gain, hidden):
    values = residual[rows, :] + total
    hidden[rows, :] = values
    return normalize(values, gain[...])[0].astype(BF16)


def norm_spread(partial_b, residual, gain):
    def compute(r, total, rows, first):
        return norm_rows(total, rows, r.residual, r.gain, r.hidden)

    return spread(
        partial_b,
        dict(residual=residual, gain=gain.reshape(1, -1)),
        dict(hidden=residual.shape),
        compute,
        1,
    )


def back_rows(total, rows, first, hidden, gain, incoming, own, grad_gain):
    values = hidden[rows, :]
    inverse = lax.rsqrt(jnp.mean(values * values, axis=-1, keepdims=True) + EPSILON)
    made, term = normalize_back(values, inverse, gain[...], total)
    made = made + incoming[rows, :]
    if own is not None:
        own[rows, :] = made
    term = term.reshape(1, -1)
    grad_gain[...] = term if first else grad_gain[...] + term
    return made.astype(BF16)


def back_spread(partial_b, hidden, gain, incoming):
    def compute(r, total, rows, first):
        return back_rows(total, rows, first, r.hidden, r.gain, r.incoming, r.own, r.grad_gain)

    return spread(
        partial_b,
        dict(hidden=hidden, gain=gain.reshape(1, -1), incoming=incoming),
        dict(own=hidden.shape, grad_gain=(1, hidden.shape[1])),
        compute,
        3,
    )


def ring_peers(count):
    me = lax.axis_index("dp")
    even = lax.rem(me, 2) == 0
    place = jnp.where(even, me // 2, count - 1 - me // 2)

    def at(position):
        position = lax.rem(position + count, count)
        return jnp.where(position < count // 2, 2 * position, 2 * (count - 1 - position) + 1)

    return at(place + 1), at(place - 1), lambda distance: at(place + distance)


class Rings:
    def __init__(self, devices, sides, segments, held, send, recv, credit, store):
        self.devices, self.sides, self.segments, self.held = devices, sides, segments, held
        self.send, self.recv, self.credit, self.store = send, recv, credit, store
        self.rows = segments[0][0][0].shape[0] // devices
        self.half = self.rows // sides
        self.steps = devices - 1
        self.following, self.previous, self.owner_at = ring_peers(devices)

    def peers(self):
        return [dict(dp=self.following), dict(dp=self.previous)]

    def copy(self, seg, side, step):
        number = (seg * self.sides + side) * self.steps + step
        return remote(
            self.held[seg].at[side, step % SLOTS],
            self.held[seg].at[side, (step + 1) % SLOTS],
            self.send.at[number],
            self.recv.at[number],
            dict(dp=self.following if side == 0 else self.previous),
        )

    def unit(self, seg, step):
        sides, half, steps = self.sides, self.half, self.steps
        last = step == steps
        slot = step % SLOTS
        starts = []
        for side in range(sides):
            if last:
                owner = lax.axis_index("dp")
            else:
                owner = self.owner_at(-1 - step if side == 0 else 1 + step)
            starts.append(pl.multiple_of(owner * self.rows + side * half, 16))
        if step:
            for side in range(sides):
                self.copy(seg, side, step - 1).wait_send()
                if step <= steps + 1 - SLOTS:
                    pl.semaphore_signal(
                        self.credit.at[seg * sides + side],
                        inc=1,
                        device_id=dict(dp=self.previous if side == 0 else self.following),
                        device_id_type=MESH,
                    )
                self.copy(seg, side, step - 1).wait_recv()
        column = 0
        for left, right in self.segments[seg]:
            pieces = [left[pl.ds(start, half), :] for start in starts]
            piece = pieces[0] if sides == 1 else jnp.concatenate(pieces, axis=0)
            made = jnp.dot(piece, right[...], preferred_element_type=F32)
            at = slice(column, column + made.shape[1])
            values = []
            for side in range(sides):
                value = made[side * half : (side + 1) * half]
                if step:
                    value = value + self.held[seg][side, slot, :, at].astype(F32)
                if last:
                    values.append(value)
                else:
                    self.held[seg][side, slot, :, at] = value.astype(BF16)
            if last:
                self.store(seg, column, values[0] if sides == 1 else jnp.concatenate(values, axis=0))
            column += made.shape[1]
        if not last:
            for side in range(sides):
                if step >= SLOTS - 1:
                    pl.semaphore_wait(self.credit.at[seg * sides + side], 1)
                self.copy(seg, side, step).start()


def ring_scratch(devices, sides, rows, widths):
    copies = len(widths) * sides * (devices - 1)
    made = {
        f"held{at}": pltpu.VMEM((sides, SLOTS, rows // sides, w), BF16)
        for at, w in enumerate(widths)
    }
    made["r_send"] = pltpu.SemaphoreType.DMA((copies,))
    made["r_recv"] = pltpu.SemaphoreType.DMA((copies,))
    made["r_credit"] = pltpu.SemaphoreType.REGULAR((len(widths) * sides,))
    return made


def interleave(main, units, first):
    units = iter(units)

    def some(number):
        for _ in range(number):
            unit = next(units, None)
            if unit is not None:
                unit()

    some(first)
    for number in main:
        some(number)
    for unit in units:
        unit()


def piece_sides(width, devices):
    return 2 if width // devices % 32 == 0 else 1


def block_owners(index):
    return [index, index ^ 2, index ^ 1, index ^ 3]


def to_local(values, index):
    quarter = values.shape[0] // 4
    return jnp.concatenate(
        [lax.dynamic_slice_in_dim(values, o * quarter, quarter) for o in block_owners(index)]
    )


def to_true(values, index):
    quarter = values.shape[0] // 4
    places = []
    for block in range(4):
        shift = block ^ index
        place = ((shift & 1) << 1) | (shift >> 1)
        places.append(lax.dynamic_slice_in_dim(values, place * quarter, quarter))
    return jnp.concatenate(places)


def cross(left, right):
    return lax.dot_general(left, right, (((1,), (1,)), ((), ())), preferred_element_type=F32)


def turn_t(values, cosine, sine, back):
    middle = HEAD // 2
    low, high = values[:middle], values[middle:]
    if back:
        return jnp.concatenate([low * cosine + high * sine, high * cosine - low * sine], axis=0)
    return jnp.concatenate([low * cosine - high * sine, high * cosine + low * sine], axis=0)


def head_norm_t(values, gain):
    inverse = lax.rsqrt(jnp.mean(values * values, axis=0, keepdims=True) + EPSILON)
    return values * inverse * gain


def head_back_t(values, gain, grad):
    inverse = lax.rsqrt(jnp.mean(values * values, axis=0, keepdims=True) + EPSILON)
    weighted = grad * gain
    inner = jnp.mean(weighted * values, axis=0, keepdims=True)
    return inverse * (weighted - values * inverse * inverse * inner), grad * values * inverse


def fill_bias(r):
    keys = r.column_positions[...]
    allowed = (keys <= r.row_positions[...]) & (keys < r.length[0])
    r.bias[...] = jnp.where(allowed, 0.0, -1e30)


def head_rows(head):
    return slice(head * HEAD, (head + 1) * HEAD)


def position_inputs(positions, length):
    rows = positions.shape[0]
    return dict(
        length=(length.reshape(1), pltpu.SMEM),
        row_positions=positions.reshape(1, rows),
        column_positions=positions.reshape(rows, 1),
    )


def attention_forward(
    normed_b, query_weight, kv_weight, query_gain, key_gain, attn_out, residual, gain, tables, where
):
    rows, width = normed_b.shape
    columns = query_weight.shape[1]
    kv_columns = kv_weight.shape[1] // 2
    heads, kv_heads = columns // HEAD, kv_columns // HEAD

    def body(r):
        me = lax.axis_index("dp")
        place = lax.rem(me, SPAN)
        greet(tensor_peers() + span_peers())

        def pass_on(distance):
            return remote(
                r.own, r.near.at[distance - 1], r.p_send.at[distance - 1], r.p_recv.at[distance - 1],
                dict(dp=me + distance),
            )

        cosine, sine = r.cosine[...], r.sine[...]
        made = jnp.dot(r.normed[...], r.kv_weight[...], preferred_element_type=F32)
        r.key_raw[...] = made[:, :kv_columns].T
        r.own[:, kv_columns:] = made[:, kv_columns:].astype(BF16)
        for group in range(kv_heads):
            keys = head_norm_t(r.key_raw[head_rows(group), :], r.key_gain[...])
            r.keys_t[head_rows(group), :] = turn_t(keys, cosine, sine, False).astype(BF16)
        r.own[:, :kv_columns] = r.keys_t[...].T
        for distance in range(1, SPAN):

            @pl.when(place + distance < SPAN)
            def _():
                pass_on(distance).start()

        made = jnp.dot(r.normed[...], r.query_weight[...], preferred_element_type=F32)
        r.query_raw[...] = made.T
        for head in range(heads):
            query = head_norm_t(r.query_raw[head_rows(head), :], r.query_gain[...])
            query = turn_t(query, cosine, sine, False).astype(BF16)
            r.query[head_rows(head), :] = query * jnp.asarray(HEAD ** (-0.5), BF16)
        fill_bias(r)

        def part(piece, first):
            for group in range(kv_heads):
                keys = piece[:, head_rows(group)]
                values_t = piece[:, kv_columns + group * HEAD : kv_columns + (group + 1) * HEAD].T
                for head in range(group * GROUP, (group + 1) * GROUP):
                    at = head_rows(head)
                    scores = jnp.dot(keys, r.query[at, :], preferred_element_type=F32)
                    if first:
                        scores = scores + r.bias[...]
                    expo = jnp.exp(scores)
                    total = jnp.sum(expo, axis=0, keepdims=True)
                    made = jnp.dot(values_t, expo.astype(BF16), preferred_element_type=F32)
                    if first:
                        r.total[head : head + 1, :] = total
                        r.attended_t[at, :] = made
                    else:
                        r.total[head : head + 1, :] += total
                        r.attended_t[at, :] += made

        part(r.own[...], True)
        for distance in range(1, SPAN):

            @pl.when(place >= distance)
            def _():
                pass_on(distance).wait_recv()
                part(r.near[distance - 1], False)

        for head in range(heads):
            at = head_rows(head)
            made = r.attended_t[at, :] / r.total[head : head + 1, :]
            r.attended_t[at, :] = made
            r.attended[:, at] = made.T.astype(BF16)
        r.log_total[...] = jnp.log(r.total[...])
        r.partial[...] = jnp.dot(
            r.attended[...], r.attn_out[...], preferred_element_type=F32
        ).astype(BF16)
        exhaust(
            sum_and_gather(
                r, r.partial, r.gathered, r.gathered_t,
                lambda total, at, first: norm_rows(total, at, r.residual, r.gain, r.hidden),
            )
        )
        for distance in range(1, SPAN):

            @pl.when(place + distance < SPAN)
            def _():
                pass_on(distance).wait_send()

    return run_kernel(
        body,
        dict(
            normed=normed_b,
            query_weight=query_weight,
            kv_weight=kv_weight,
            query_gain=query_gain.reshape(HEAD, 1),
            key_gain=key_gain.reshape(HEAD, 1),
            attn_out=attn_out,
            residual=residual,
            gain=gain.reshape(1, -1),
            cosine=tables[0],
            sine=tables[1],
            **where,
        ),
        dict(
            gathered=((rows, width), BF16),
            gathered_t=((width, rows), BF16),
            hidden=(residual.shape, F32),
            query_raw=((columns, rows), F32),
            key_raw=((kv_columns, rows), F32),
            query=((columns, rows), BF16),
            own=((rows, 2 * kv_columns), BF16),
            near=((SPAN - 1, rows, 2 * kv_columns), BF16),
            attended=((rows, columns), BF16),
            attended_t=((columns, rows), F32),
            log_total=((heads, rows), F32),
        ),
        dict(
            keys_t=pltpu.VMEM((kv_columns, rows), BF16),
            bias=pltpu.VMEM((rows, rows), F32),
            total=pltpu.VMEM((heads, rows), F32),
            partial=pltpu.VMEM((rows, width), BF16),
            p_send=pltpu.SemaphoreType.DMA((SPAN - 1,)),
            p_recv=pltpu.SemaphoreType.DMA((SPAN - 1,)),
            **exchange_scratch(rows, width),
        ),
        2,
        48,
        16 * rows * rows * SPAN * columns,
    )


def stream_product(r, lefts, weights, out):
    width = weights.shape[2]
    size = r.tile.shape[3]
    tiles = width // size

    def fetch(j):
        return [
            pltpu.make_async_copy(
                weights.at[k, :, pl.ds(j * size, size)], r.tile.at[j % 2, k], r.tile_sem.at[j % 2, k]
            )
            for k in range(len(lefts))
        ]

    for copy in fetch(0):
        copy.start()
    for j in range(tiles):
        if j + 1 < tiles:
            for copy in fetch(j + 1):
                copy.start()
        for copy in fetch(j):
            copy.wait()
        made = None
        for k, left in enumerate(lefts):
            term = jnp.dot(left[...], r.tile[j % 2, k], preferred_element_type=F32)
            made = term if made is None else made + term
        out[:, j * size : (j + 1) * size] = made.astype(BF16)
        if j % 2:
            yield 1


def stream_scratch(count, depth, size):
    return dict(
        tile=pltpu.VMEM((2, count, depth, size), BF16),
        tile_sem=pltpu.SemaphoreType.DMA((2, count)),
    )


def attention_backward(
    grad_b_t, norm_two_t, active, grad_gate, grad_up, gate_up_t, down, three, norm_mlp, incoming,
    kept, attn_out, query_weight, kv_weight, query_gain, key_gain, two, norm_attn, tables, where, devices,
):
    units, tokens_width = gate_up_t.shape[1:]
    query_raw, key_raw, query, own, near, attended_t, log_total = kept
    rows, width = active.shape[0], tokens_width
    columns = query_weight.shape[1]
    kv_columns = kv_weight.shape[1] // 2
    heads, kv_heads = columns // HEAD, kv_columns // HEAD
    sides = piece_sides(width, devices)
    block = width // devices
    segment_widths = [units] * 3

    def body(r):
        me = lax.axis_index("dp")
        place = lax.rem(me, SPAN)

        def store(seg, column, value):
            (r.sum_down, r.sum_gate, r.sum_up)[seg][...] = value

        rings = Rings(
            devices, sides,
            [[(r.grad_b_t, r.active)], [(r.norm_two_t, r.grad_gate)], [(r.norm_two_t, r.grad_up)]],
            [r.held0, r.held1, r.held2], r.r_send, r.r_recv, r.r_credit, store,
        )
        greet(rings.peers() + tensor_peers() + span_peers())

        def pass_back(distance):
            return remote(
                r.far.at[distance - 1], r.arrived.at[distance - 1],
                r.p_send.at[distance - 1], r.p_recv.at[distance - 1], dict(dp=me - distance),
            )

        def part(piece, write, masked):
            for group in range(kv_heads):
                keys = piece[:, head_rows(group)]
                value_at = slice(kv_columns + group * HEAD, kv_columns + (group + 1) * HEAD)
                values = piece[:, value_at]
                keys_t = keys.T
                grad_k = grad_v = None
                for head in range(group * GROUP, (group + 1) * GROUP):
                    at = head_rows(head)
                    q, grads = r.query[at, :], r.grads[:, at]
                    scores = jnp.dot(keys, q, preferred_element_type=F32)
                    scores = scores - r.log_total[head : head + 1, :]
                    if masked:
                        scores = scores + r.bias[...]
                    probs = jnp.exp(scores)
                    made = jnp.dot(probs.astype(BF16), grads, preferred_element_type=F32)
                    grad_v = made if grad_v is None else grad_v + made
                    grad_probs = cross(values, grads)
                    grad_scores = (probs * (grad_probs - r.delta[head : head + 1, :])).astype(BF16)
                    made = cross(grad_scores, q)
                    grad_k = made if grad_k is None else grad_k + made
                    made = jnp.dot(keys_t, grad_scores, preferred_element_type=F32)
                    if masked:
                        r.grad_q_t[at, :] = made
                    else:
                        r.grad_q_t[at, :] += made
                write(head_rows(group), grad_k)
                write(value_at, grad_v)

        def main():
            yield from stream_product(r, [r.grad_gate, r.grad_up], r.gate_up_t, r.partial)
            fill_bias(r)
            yield from sum_and_gather(
                r, r.partial, r.gathered, r.grad_three_t,
                lambda total, at, first: back_rows(
                    total, at, first, r.three, r.norm_mlp, r.incoming, r.grad_three, r.grad_norm_mlp
                ),
            )
            r.grads[...] = cross(r.gathered[...], r.attn_out[...]).astype(BF16)
            for head in range(heads):
                at = head_rows(head)
                grads_t = r.grads[:, at].astype(F32).T
                r.delta[head : head + 1, :] = jnp.sum(
                    grads_t * r.attended_t[at, :], axis=0, keepdims=True
                )
            yield 1

            def write_own(at, value):
                r.grad_own[:, at] = value

            part(r.own[...], write_own, True)
            yield 1
            for distance in range(1, SPAN):

                @pl.when(place >= distance)
                def _():
                    def write_far(at, value):
                        r.far[distance - 1, :, at] = value.astype(BF16)

                    part(r.near[distance - 1], write_far, False)
                    pass_back(distance).start()

                yield 1
            cosine, sine = r.cosine[...], r.sine[...]
            terms = None
            for head in range(heads):
                at = head_rows(head)
                grad = turn_t(r.grad_q_t[at, :] * HEAD ** (-0.5), cosine, sine, True)
                made, term = head_back_t(r.query_raw[at, :], r.query_gain[...], grad)
                terms = term if terms is None else terms + term
                r.grad_query[:, at] = made.T.astype(BF16)
            r.grad_query_gain[...] = jnp.sum(terms, axis=1, keepdims=True)
            yield 1
            for distance in range(1, SPAN):

                @pl.when(place + distance < SPAN)
                def _():
                    pass_back(distance).wait_recv()
                    r.grad_own[...] += r.arrived[distance - 1].astype(F32)

            terms = None
            for group in range(kv_heads):
                at = head_rows(group)
                grad = turn_t(r.grad_own[:, at].T, cosine, sine, True)
                made, term = head_back_t(r.key_raw[at, :], r.key_gain[...], grad)
                terms = term if terms is None else terms + term
                r.grad_kv[:, at] = made.T.astype(BF16)
            r.grad_key_gain[...] = jnp.sum(terms, axis=1, keepdims=True)
            r.grad_kv[:, kv_columns:] = r.grad_own[:, kv_columns:].astype(BF16)
            r.partial[...] = (
                cross(r.grad_query[...], r.query_weight[...]) + cross(r.grad_kv[...], r.kv_weight[...])
            ).astype(BF16)
            yield 1
            yield from sum_and_gather(
                r, r.partial, r.grad_two_b, r.grad_two_t,
                lambda total, at, first: back_rows(
                    total, at, first, r.two, r.norm_attn, r.grad_three, r.grad_two, r.grad_norm_attn
                ),
            )
            for distance in range(1, SPAN):

                @pl.when(place >= distance)
                def _():
                    pass_back(distance).wait_send()

            yield from stream_product(r, [r.active], r.down, r.partial)
            yield from sum_and_gather(
                r, r.partial, r.output, None,
                lambda total, at, first: (r.three[at, :] + total).astype(BF16),
            )

        order = [(seg, step) for step in range(devices) for seg in range(3)]
        interleave(main(), [lambda u=u: rings.unit(*u) for u in order], 3)

    quarter = rows // 4
    return run_kernel(
        body,
        dict(
            grad_b_t=grad_b_t,
            norm_two_t=norm_two_t,
            active=active,
            grad_gate=grad_gate,
            grad_up=grad_up,
            gate_up_t=(gate_up_t, pl.ANY),
            down=(down.reshape((1,) + down.shape), pl.ANY),
            three=three,
            norm_mlp=norm_mlp.reshape(1, -1),
            incoming=incoming,
            query_raw=query_raw,
            key_raw=key_raw,
            query=query,
            own=own,
            near=near,
            attended_t=attended_t,
            log_total=log_total,
            attn_out=attn_out,
            query_weight=query_weight,
            kv_weight=kv_weight,
            query_gain=query_gain.reshape(HEAD, 1),
            key_gain=key_gain.reshape(HEAD, 1),
            two=two,
            norm_attn=norm_attn.reshape(1, -1),
            cosine=tables[0],
            sine=tables[1],
            **where,
        ),
        dict(
            grad_three_t=((width, rows), BF16),
            grad_query=((rows, columns), BF16),
            grad_kv=((rows, 2 * kv_columns), BF16),
            grad_two_b=((rows, width), BF16),
            grad_two_t=((width, rows), BF16),
            grad_two=((quarter, width), F32),
            grad_norm_mlp=((1, width), F32),
            grad_norm_attn=((1, width), F32),
            grad_query_gain=((HEAD, 1), F32),
            grad_key_gain=((HEAD, 1), F32),
            sum_down=((block, units), F32),
            sum_gate=((block, units), F32),
            sum_up=((block, units), F32),
            output=((rows, width), BF16),
        ),
        dict(
            partial=pltpu.VMEM((rows, width), BF16),
            gathered=pltpu.VMEM((rows, width), BF16),
            grad_three=pltpu.VMEM((quarter, width), F32),
            grads=pltpu.VMEM((rows, columns), BF16),
            delta=pltpu.VMEM((heads, rows), F32),
            bias=pltpu.VMEM((rows, rows), F32),
            grad_q_t=pltpu.VMEM((columns, rows), F32),
            grad_own=pltpu.VMEM((rows, 2 * kv_columns), F32),
            far=pltpu.VMEM((SPAN - 1, rows, 2 * kv_columns), BF16),
            arrived=pltpu.VMEM((SPAN - 1, rows, 2 * kv_columns), BF16),
            p_send=pltpu.SemaphoreType.DMA((SPAN - 1,)),
            p_recv=pltpu.SemaphoreType.DMA((SPAN - 1,)),
            **stream_scratch(2, units, 256),
            **exchange_scratch(rows, width),
            **ring_scratch(devices, sides, block, segment_widths),
        ),
        3 + 2,
        61,
        2 * rows * width * units * 10,
    )


class Pump:
    def __init__(self, rings, ready):
        self.rings, self.ready = rings, list(ready)
        self.step = [0] * len(rings.segments)
        self.before = None

    def run(self, number):
        for _ in range(number):
            left = [s for s in self.ready if self.step[s] <= self.rings.steps]
            if not left:
                return
            seg = min(left, key=lambda s: (s == self.before, self.step[s], s))
            self.rings.unit(seg, self.step[seg])
            self.step[seg] += 1
            self.before = seg

    def rest(self):
        self.run(len(self.step) * (self.rings.steps + 1))


def first_backward(
    lefts, rights, grad_two_b, down, gate_up_t, gate, upward, one, norm_mlp, grad_two, conv_out,
    conv_in_t, projected, rim, kernel, inputs, norm_conv, small, devices,
):
    rows, width = grad_two_b.shape
    units = down.shape[0]
    channels = conv_out.shape[0]
    quarter = rows // 4
    block = width // devices
    sides = piece_sides(width, devices)
    grad_three_t, normed_attn_t, grad_two_t, norm_one_t, normed_conv_t = lefts
    attended, grad_query, grad_kv, active, gated = rights
    columns, kv_columns = grad_query.shape[1], grad_kv.shape[1]
    widths = [channels + columns + kv_columns, units, units, units, 4 * channels]
    bits = []
    bit = 1
    while bit < devices:
        bits.append(bit)
        bit *= 2
    stages = 2 + len(bits)
    size = TILE
    tiles = [(at, min(size, units - at)) for at in range(0, units, size)]

    def body(r):
        me = lax.axis_index("dp")
        index = lax.axis_index("tensor")
        place = lax.rem(me, SPAN)

        def store(seg, column, value):
            if seg == 0:
                at = (0, channels, channels + columns).index(column)
                (r.sum_attn_out, r.sum_query, r.sum_kv)[at][...] = value
            elif seg < 4:
                (r.sum_down, r.sum_gate, r.sum_up)[seg - 1][...] = value
            elif column == 0:
                r.sum_conv_out[...] = value
            else:
                for at in range(3):
                    r.sum_conv_in[at] = value[:, at * channels : (at + 1) * channels]

        rings = Rings(
            devices, sides,
            [
                [
                    (r.grad_three_t, r.attended),
                    (r.normed_attn_t, r.grad_query),
                    (r.normed_attn_t, r.grad_kv),
                ],
                [(r.grad_two_t, r.active)],
                [(r.norm_one_t, r.grad_gate)],
                [(r.norm_one_t, r.grad_up)],
                [(r.grad_one_t, r.gated), (r.normed_conv_t, r.grad_projected)],
            ],
            [r.held0, r.held1, r.held2, r.held3, r.held4], r.r_send, r.r_recv, r.r_credit, store,
        )
        pump = Pump(rings, [0, 1])
        small_peers = tensor_peers() + [dict(dp=me ^ bit) for bit in bits]
        greet(rings.peers() + small_peers + span_peers())

        def fetch(number):
            at, wide = tiles[number]
            slot = number % 2
            pairs = [
                (r.down.at[at : at + wide, :], r.down_tile.at[slot, 0:wide, :]),
                (r.gate.at[number], r.gate_tile.at[slot]),
                (r.upward.at[number], r.up_tile.at[slot]),
            ]
            return [
                pltpu.make_async_copy(a, b, r.h_sem.at[slot, k]) for k, (a, b) in enumerate(pairs)
            ]

        def fetch_conv(number):
            slot = number % 2
            return [
                pltpu.make_async_copy(
                    r.conv_in_t.at[k, pl.ds(number * size, size), :],
                    r.conv_tile.at[slot, k],
                    r.c_sem.at[slot, k],
                )
                for k in range(3)
            ]

        def main():
            first = pltpu.make_async_copy(r.grad_two_b, r.gathered, r.e_sem)
            first.start()
            for copy in fetch(0):
                copy.start()
            first.wait()
            for number, (at, wide) in enumerate(tiles):
                if number + 1 < len(tiles):
                    for copy in fetch(number + 1):
                        copy.start()
                for copy in fetch(number):
                    copy.wait()
                slot = number % 2
                grad = cross(r.gathered[...], r.down_tile[slot, 0:wide, :])
                gates, ups = r.gate_tile[slot, :, 0:wide], r.up_tile[slot, :, 0:wide]
                sigma = jax.nn.sigmoid(gates)
                r.grad_gate[:, at : at + wide] = (
                    grad * ups * sigma * (1.0 + gates * (1.0 - sigma))
                ).astype(BF16)
                r.grad_up[:, at : at + wide] = (grad * gates * sigma).astype(BF16)
                if number % 3 == 2:
                    yield 1
            pump.ready += [2, 3]
            yield 2
            yield from stream_product(r, [r.grad_gate, r.grad_up], r.gate_up_t, r.partial)
            yield from sum_and_gather(
                r, r.partial, r.gathered, r.grad_one_t,
                lambda total, at, first: back_rows(
                    total, at, first, r.one, r.norm_mlp, r.grad_two, r.grad_one, r.gain_term
                ),
            )
            r.small_out[...] = r.small[...]
            r.small_out[1:2, :] = r.gain_term[...]

            made = cross(r.gathered[...], r.conv_out[...])
            for at, owner in enumerate(block_owners(index)):
                start = pl.multiple_of(owner * quarter, quarter)
                r.grad_gated[pl.ds(start, quarter), :] = made[at * quarter : (at + 1) * quarter]
            before = r.projected[:, :channels]
            signal = r.projected[:, 2 * channels :]
            taps = r.kernel[...].astype(F32)
            pad = 8
            r.mixed[pad:, :] = before * signal
            r.mixed[pad - KW + 1 : pad, :] = r.rim[...]
            grad_gated = r.grad_gated[...]
            r.grad_conv[0:rows, :] = grad_gated * r.projected[:, channels : 2 * channels]
            r.grad_conv[rows:, :] = jnp.zeros_like(r.grad_conv[rows:, :])
            r.rim_out[...] = r.grad_conv[0:pad, :]
            rim_copy = remote(r.rim_out, r.rim_in, r.m_sem.at[0], r.m_sem.at[1], dict(dp=me - 1))

            @pl.when(place > 0)
            def _():
                rim_copy.start()

            yield 1
            convolved = None
            for k in range(KW):
                shifted = r.mixed[pad - KW + 1 + k : pad - KW + 1 + k + rows, :]
                term = taps[k : k + 1, :] * shifted
                convolved = term if convolved is None else convolved + term
                term = jnp.sum(r.grad_conv[0:rows, :] * shifted, axis=0, keepdims=True)
                r.small_out[5 + k : 6 + k, 0:channels] = term
            r.grad_projected[:, channels : 2 * channels] = (grad_gated * convolved).astype(BF16)

            @pl.when(place < SPAN - 1)
            def _():
                rim_copy.wait_recv()
                r.grad_conv[rows:, :] = r.rim_in[...]

            grad_mixed = None
            for k in range(KW):
                term = taps[k : k + 1, :] * r.grad_conv[KW - 1 - k : KW - 1 - k + rows, :]
                grad_mixed = term if grad_mixed is None else grad_mixed + term
            r.grad_projected[:, :channels] = (grad_mixed * signal).astype(BF16)
            r.grad_projected[:, 2 * channels :] = (grad_mixed * before).astype(BF16)

            @pl.when(place > 0)
            def _():
                rim_copy.wait_send()

            pump.ready += [4]
            yield 2
            for copy in fetch_conv(0):
                copy.start()
            for number in range(width // size):
                if number + 1 < width // size:
                    for copy in fetch_conv(number + 1):
                        copy.start()
                for copy in fetch_conv(number):
                    copy.wait()
                for at, owner in enumerate(block_owners(index)):
                    start = pl.multiple_of(owner * quarter, quarter)
                    made = None
                    for k in range(3):
                        piece = r.grad_projected[
                            pl.ds(start, quarter), k * channels : (k + 1) * channels
                        ]
                        term = cross(piece, r.conv_tile[number % 2, k])
                        made = term if made is None else made + term
                    r.partial[
                        at * quarter : (at + 1) * quarter, number * size : (number + 1) * size
                    ] = made.astype(BF16)
                if number % 2:
                    yield 1
            yield from sum_and_gather(
                r, r.partial, r.input_grad, None,
                lambda total, at, first: back_rows(
                    total, at, first, r.inputs, r.norm_conv, r.grad_one, None, r.gain_term
                ),
            )
            r.small_out[0:1, :] = r.gain_term[...]
            row = lax.broadcasted_iota(jnp.int32, small.shape, 0)
            for stage in range(stages):
                copy = remote(
                    r.small_out, r.slots.at[stage], r.s_send.at[stage], r.s_recv.at[stage],
                    small_peers[stage],
                )
                copy.start()
                yield 1
                copy.wait()
                if stage < 2:
                    r.small_out[...] += jnp.where(row < 5, r.slots[stage], 0.0)
                else:
                    r.small_out[...] += r.slots[stage]

        pump.run(2)
        for number in main():
            pump.run(number)
        pump.rest()

    return run_kernel(
        body,
        dict(
            grad_three_t=grad_three_t,
            normed_attn_t=normed_attn_t,
            grad_two_t=grad_two_t,
            norm_one_t=norm_one_t,
            normed_conv_t=normed_conv_t,
            attended=attended,
            grad_query=grad_query,
            grad_kv=grad_kv,
            active=active,
            gated=gated,
            grad_two_b=(grad_two_b, pl.ANY),
            down=(down, pl.ANY),
            gate_up_t=(gate_up_t, pl.ANY),
            gate=(gate, pl.ANY),
            upward=(upward, pl.ANY),
            one=one,
            norm_mlp=norm_mlp.reshape(1, -1),
            grad_two=grad_two,
            conv_out=conv_out,
            conv_in_t=(conv_in_t, pl.ANY),
            projected=projected,
            rim=rim,
            kernel=kernel,
            inputs=inputs,
            norm_conv=norm_conv.reshape(1, -1),
            small=small,
        ),
        dict(
            input_grad=((rows, width), BF16),
            small_out=(small.shape, F32),
            sum_attn_out=((block, channels), F32),
            sum_query=((block, columns), F32),
            sum_kv=((block, kv_columns), F32),
            sum_down=((block, units), F32),
            sum_gate=((block, units), F32),
            sum_up=((block, units), F32),
            sum_conv_out=((block, channels), F32),
            sum_conv_in=((3, block, channels), F32),
        ),
        dict(
            gathered=pltpu.VMEM((rows, width), BF16),
            partial=pltpu.VMEM((rows, width), BF16),
            grad_one_t=pltpu.VMEM((width, rows), BF16),
            grad_one=pltpu.VMEM((quarter, width), F32),
            grad_gate=pltpu.VMEM((rows, units), BF16),
            grad_up=pltpu.VMEM((rows, units), BF16),
            grad_projected=pltpu.VMEM((rows, 3 * channels), BF16),
            grad_gated=pltpu.VMEM((rows, channels), F32),
            mixed=pltpu.VMEM((rows + 8, channels), F32),
            grad_conv=pltpu.VMEM((rows + 8, channels), F32),
            rim_out=pltpu.VMEM((8, channels), F32),
            rim_in=pltpu.VMEM((8, channels), F32),
            m_sem=pltpu.SemaphoreType.DMA((2,)),
            e_sem=pltpu.SemaphoreType.DMA,
            down_tile=pltpu.VMEM((2, size, width), BF16),
            gate_tile=pltpu.VMEM((2, rows, size), F32),
            up_tile=pltpu.VMEM((2, rows, size), F32),
            h_sem=pltpu.SemaphoreType.DMA((2, 3)),
            conv_tile=pltpu.VMEM((2, 3, size, channels), BF16),
            c_sem=pltpu.SemaphoreType.DMA((2, 3)),
            gain_term=pltpu.VMEM((1, width), F32),
            slots=pltpu.VMEM((stages,) + small.shape, F32),
            s_send=pltpu.SemaphoreType.DMA((stages,)),
            s_recv=pltpu.SemaphoreType.DMA((stages,)),
            **stream_scratch(2, units, 128),
            **exchange_scratch(rows, width),
            **ring_scratch(devices, sides, block, widths),
        ),
        4,
        62,
        2 * rows * width * sum(widths) * 3,
    )


TILE = 256


def hidden_forward(normed_b, gate_up_t, down):
    rows, width = normed_b.shape
    units = down.shape[0]
    tiles = pl.cdiv(units, TILE)
    rest = units - (tiles - 1) * TILE

    def body(normed, weight, down_ref, partial, active, gate, upward, total):
        at = pl.program_id(0)
        a = cross(normed[...], weight[0])
        z = cross(normed[...], weight[1])
        gate[0] = a
        upward[0] = z
        s = (a * jax.nn.sigmoid(a) * z).astype(BF16)
        active[...] = s

        @pl.when(at == 0)
        def _():
            total[...] = jnp.dot(s, down_ref[...], preferred_element_type=F32)

        @pl.when((at > 0) & (at < tiles - 1))
        def _():
            total[...] += jnp.dot(s, down_ref[...], preferred_element_type=F32)

        @pl.when(at == tiles - 1)
        def _():
            last = jnp.dot(s[:, :rest], down_ref[0:rest, :], preferred_element_type=F32)
            partial[...] = (total[...] + last).astype(BF16)

    return pl.pallas_call(
        body,
        grid=(tiles,),
        in_specs=[
            pl.BlockSpec((rows, width), lambda i: (0, 0)),
            pl.BlockSpec((2, TILE, width), lambda i: (0, i, 0)),
            pl.BlockSpec((TILE, width), lambda i: (i, 0)),
        ],
        out_specs=[
            pl.BlockSpec((rows, width), lambda i: (0, 0)),
            pl.BlockSpec((rows, TILE), lambda i: (0, i)),
            pl.BlockSpec((1, rows, TILE), lambda i: (i, 0, 0)),
            pl.BlockSpec((1, rows, TILE), lambda i: (i, 0, 0)),
        ],
        out_shape=[
            jax.ShapeDtypeStruct((rows, width), BF16),
            jax.ShapeDtypeStruct((rows, units), BF16),
            jax.ShapeDtypeStruct((tiles, rows, TILE), F32),
            jax.ShapeDtypeStruct((tiles, rows, TILE), F32),
        ],
        scratch_shapes=[pltpu.VMEM((rows, width), F32)],
        compiler_params=pltpu.CompilerParams(vmem_limit_bytes=40 * 2**20),
    )(normed_b, gate_up_t, down)


def hidden_both(normed_b, gate_up_t, down, grad_b):
    rows, width = normed_b.shape
    units = down.shape[0]

    def body(normed, weight, down_ref, grad_ref, active, grad_gate, grad_up):
        a = cross(normed[...], weight[0])
        z = cross(normed[...], weight[1])
        grad = cross(grad_ref[...], down_ref[...])
        sigma = jax.nn.sigmoid(a)
        active[...] = (a * sigma * z).astype(BF16)
        grad_gate[...] = (grad * z * sigma * (1.0 + a * (1.0 - sigma))).astype(BF16)
        grad_up[...] = (grad * a * sigma).astype(BF16)

    whole = pl.BlockSpec((rows, width), lambda i: (0, 0))
    tile = pl.BlockSpec((rows, TILE), lambda i: (0, i))
    return pl.pallas_call(
        body,
        grid=(pl.cdiv(units, TILE),),
        in_specs=[
            whole,
            pl.BlockSpec((2, TILE, width), lambda i: (0, i, 0)),
            pl.BlockSpec((TILE, width), lambda i: (i, 0)),
            whole,
        ],
        out_specs=[tile] * 3,
        out_shape=[jax.ShapeDtypeStruct((rows, units), BF16)] * 3,
        compiler_params=pltpu.CompilerParams(vmem_limit_bytes=40 * 2**20),
    )(normed_b, gate_up_t, down, grad_b)


def local(
    tokens,
    lengths,
    norm_conv,
    conv_in,
    conv_kernel,
    conv_out,
    norm_mlp_one,
    gate_up_one,
    down_one,
    norm_attn,
    query_weight,
    kv_weight,
    query_gain,
    key_gain,
    attn_out,
    norm_mlp_two,
    gate_up_two,
    down_two,
    cotangent,
):
    row_count = tokens.shape[0]
    width = tokens.shape[1]
    quarter = row_count // 4
    channels = conv_out.shape[0]
    local_heads = query_weight.shape[1] // HEAD
    local_kv = kv_weight.shape[2] // HEAD
    device = lax.axis_index("dp")
    devices = lax.axis_size("dp")
    index = lax.axis_index("tensor")
    sequence = device // SPAN
    place_index = device % SPAN
    length = lengths[sequence]
    offsets = jnp.concatenate(
        [o * quarter + jnp.arange(quarter, dtype=jnp.int32) for o in block_owners(index)]
    )
    positions = place_index * row_count + offsets
    is_valid = positions < length
    frequency = THETA ** (-2.0 * jnp.arange(HEAD // 2, dtype=jnp.float32) / HEAD)
    angles = frequency[:, None] * positions.astype(jnp.float32)[None, :]
    tables = (jnp.cos(angles), jnp.sin(angles))
    where = position_inputs(positions, length)
    kernel = conv_kernel.astype(jnp.float32)
    rim_rows = KW - 1
    gate_up_one_t = jnp.transpose(gate_up_one, (1, 2, 0))
    gate_up_two_t = jnp.transpose(gate_up_two, (1, 2, 0))
    forward_route = [(i, i + 1) for i in range(devices - 1) if (i + 1) % SPAN]
    backward_route = [(b, a) for a, b in forward_route]

    inputs = tokens.astype(F32)
    normed_conv, inverse_conv = normalize(inputs, norm_conv)
    normed_conv_b = normed_conv.astype(BF16)
    weight_in = conv_in.reshape(width, 3 * channels)
    projected = matmul(normed_conv_b, weight_in)
    before = projected[:, :channels]
    after = projected[:, channels : 2 * channels]
    signal = projected[:, 2 * channels :]
    mixed = before * signal
    rim_in = lax.ppermute(mixed[row_count - rim_rows :], "dp", forward_route)
    padded = jnp.concatenate([rim_in, mixed], axis=0)
    convolved = kernel[0] * padded[0:row_count]
    for offset in range(1, KW):
        convolved = convolved + kernel[offset] * padded[offset : offset + row_count]
    gated_b = to_local((after * convolved).astype(BF16), index)
    inputs_own = lax.dynamic_slice_in_dim(tokens, index * quarter, quarter).astype(F32)

    norm_one_b, norm_one_t, one_own = norm_spread(
        matmul(gated_b, conv_out).astype(BF16), inputs_own, norm_mlp_one
    )
    partial_b, active_one, gate_a, up_a = hidden_forward(norm_one_b, gate_up_one_t, down_one)

    normed_attn_b, normed_attn_t, two_own = norm_spread(
        partial_b, one_own, norm_attn
    )
    kv_flat = kv_weight.reshape(width, 2 * local_kv * HEAD)
    (
        norm_two_b,
        norm_two_t,
        three_own,
        *kept,
        attended_b,
        attended_t,
        log_total,
    ) = attention_forward(
        normed_attn_b,
        query_weight,
        kv_flat,
        query_gain,
        key_gain,
        attn_out,
        two_own,
        norm_mlp_two,
        tables,
        where,
    )
    kept = (*kept, attended_t, log_total)

    grad_result = to_local(cotangent, index).astype(F32) * is_valid[:, None].astype(F32)
    grad_result_b = grad_result.astype(BF16)
    active_two, grad_gate_two, grad_up_two = hidden_both(
        norm_two_b, gate_up_two_t, down_two, grad_result_b
    )
    (
        grad_three_t,
        grad_query,
        grad_kv,
        grad_two_b,
        grad_two_t,
        grad_two,
        grad_norm_mlp_two,
        grad_norm_attn,
        part_query_gain,
        part_key_gain,
        sum_down_two,
        sum_gate_two,
        sum_up_two,
        output,
    ) = attention_backward(
        grad_result_b.T,
        norm_two_t,
        active_two,
        grad_gate_two,
        grad_up_two,
        gate_up_two_t,
        down_two,
        three_own,
        norm_mlp_two,
        grad_result[:quarter],
        kept,
        attn_out,
        query_weight,
        kv_flat,
        query_gain,
        key_gain,
        two_own,
        norm_attn,
        tables,
        where,
        devices,
    )

    small = jnp.concatenate(
        [
            jnp.zeros((2, width), F32),
            grad_norm_attn,
            grad_norm_mlp_two,
            jnp.pad(
                jnp.concatenate([part_query_gain[:, 0], part_key_gain[:, 0]]), (0, width - 2 * HEAD)
            ).reshape(1, width),
            jnp.zeros((KW, width), F32),
        ],
        axis=0,
    )
    (
        grad_inputs,
        small,
        sum_attn_out,
        sum_query,
        sum_kv,
        sum_down_one,
        sum_gate_one,
        sum_up_one,
        sum_conv_out,
        sum_conv_in,
    ) = first_backward(
        [grad_three_t, normed_attn_t, grad_two_t, norm_one_t, normed_conv_b.T],
        [attended_b, grad_query, grad_kv, active_one, gated_b],
        grad_two_b,
        down_one,
        gate_up_one_t,
        gate_a,
        up_a,
        one_own,
        norm_mlp_one,
        grad_two,
        conv_out,
        jnp.transpose(conv_in, (1, 0, 2)),
        projected,
        rim_in,
        conv_kernel,
        inputs_own,
        norm_conv,
        small,
        devices,
    )
    grad_inputs = to_true(grad_inputs, index).astype(F32)
    output = to_true(output, index)

    out_rows = width // devices
    return (
        output,
        grad_inputs,
        small[0],
        jnp.transpose(sum_conv_in, (1, 0, 2)),
        small[5:, :channels],
        sum_conv_out.T,
        small[1],
        jnp.stack([sum_gate_one, sum_up_one], axis=1),
        sum_down_one.T,
        small[2],
        sum_query,
        sum_kv.reshape(out_rows, 2, local_kv * HEAD),
        small[4, :HEAD],
        small[4, HEAD : 2 * HEAD],
        sum_attn_out.T,
        small[3],
        jnp.stack([sum_gate_two, sum_up_two], axis=1),
        sum_down_two.T,
    )


def solution(mesh):
    in_specs = (
        P("dp", None),
        P(),
        P(),
        P(None, None, "tensor"),
        P(None, "tensor"),
        P("tensor", None),
        P(),
        P(None, None, "tensor"),
        P("tensor", None),
        P(),
        P(None, "tensor"),
        P(None, None, "tensor"),
        P(),
        P(),
        P("tensor", None),
        P(),
        P(None, None, "tensor"),
        P("tensor", None),
        P("dp", None),
    )
    out_specs = (
        P("dp", None),
        P("dp", None),
        P(),
        P("dp", None, "tensor"),
        P(None, "tensor"),
        P("tensor", "dp"),
        P(),
        P("dp", None, "tensor"),
        P("tensor", "dp"),
        P(),
        P("dp", "tensor"),
        P("dp", None, "tensor"),
        P(),
        P(),
        P("tensor", "dp"),
        P(),
        P("dp", None, "tensor"),
        P("tensor", "dp"),
    )
    return jax.shard_map(local, mesh=mesh, in_specs=in_specs, out_specs=out_specs, check_vma=False)
```

```python
import jax
import jax.numpy as jnp
from jax import lax
from jax.experimental import pallas as pl
from jax.experimental.pallas import tpu as pltpu
from jax.sharding import PartitionSpec as P

HEAD = 64
KW = 3
SPAN = 4
GROUP = 3


EPSILON = 1e-05
THETA = 1000000.0
BF16 = jnp.bfloat16
F32 = jnp.float32


def matmul(left, right):
    return jnp.dot(left, right, preferred_element_type=F32)


def inner_back(left, right):
    return lax.dot_general(left, right, (((1,), (1,)), ((), ())), preferred_element_type=F32)


def normalize(values, gain):
    inverse = lax.rsqrt(jnp.mean(values * values, axis=-1, keepdims=True) + EPSILON)
    return (values * inverse * gain, inverse)


def normalize_back(values, inverse, gain, grad_result):
    weighted = grad_result * gain
    grad_gain = jnp.sum(grad_result * values * inverse, axis=tuple(range(values.ndim - 1)))
    inner = jnp.mean(weighted * values, axis=-1, keepdims=True)
    grad_values = inverse * (weighted - values * inverse * inverse * inner)
    return (grad_values, grad_gain)


CHUNKS = 4
SLOTS = 3
MESH = pl.DeviceIdType.MESH


class Lazy:
    def __init__(self, value, dtype=None):
        self.value, self.dtype = value, dtype


class Refs:
    def __init__(self, names, refs):
        self.__dict__.update(zip(names, refs))

    def begin(self, inputs, outputs, refs):
        self.arriving, self.leaving, self.homes = {}, [], {}
        for at, name in enumerate(inputs):
            ref = self.__dict__[name]
            copy = pltpu.make_async_copy(refs[at], ref, self.lazy_in.at[at])
            copy.start()
            self.arriving[id(ref)] = copy
        for at, name in enumerate(outputs):
            self.homes[id(self.__dict__[name])] = (refs[len(inputs) + at], at)

    def need(self, *refs):
        for ref in refs:
            self.arriving.pop(id(ref)).wait()

    def flush(self, *refs):
        for ref in refs:
            home, at = self.homes.pop(id(ref))
            copy = pltpu.make_async_copy(ref, home, self.lazy_out.at[at, 0])
            copy.start()
            self.leaving.append(copy)

    def flush_blocks(self, ref, owners):
        home, at = self.homes.pop(id(ref))
        rows = ref.shape[0] // 4
        for block, owner in enumerate(owners):
            copy = pltpu.make_async_copy(
                ref.at[pl.ds(block * rows, rows)],
                home.at[pl.ds(pl.multiple_of(owner * rows, rows), rows)],
                self.lazy_out.at[at, block],
            )
            copy.start()
            self.leaving.append(copy)

    def end(self):
        assert not self.homes
        for copy in list(self.arriving.values()) + self.leaving:
            copy.wait()


def run_kernel(body, inputs, outputs, scratch, collective_id, limit, flops):
    arrays, specs, names, out_names = [], [], [], []
    scratch = dict(scratch)
    lazy_in = [name for name, value in inputs.items() if isinstance(value, Lazy)]
    lazy_out = [name for name, value in outputs.items() if isinstance(value, Lazy)]
    for name, value in inputs.items():
        if isinstance(value, Lazy):
            array, space = value.value, pl.ANY
            scratch[name] = pltpu.VMEM(array.shape, array.dtype)
            names.append(None)
        else:
            array, space = value if isinstance(value, tuple) else (value, pltpu.VMEM)
            names.append(name)
        arrays.append(array)
        specs.append(pl.BlockSpec(memory_space=space))
    shapes, out_specs = [], []
    for name, value in outputs.items():
        if isinstance(value, Lazy):
            shape, dtype, space = value.value, value.dtype, pl.ANY
            scratch[name] = pltpu.VMEM(shape, dtype)
            names.append(None)
        else:
            (shape, dtype), space = value, pltpu.VMEM
            names.append(name)
        shapes.append(jax.ShapeDtypeStruct(shape, dtype))
        out_specs.append(pl.BlockSpec(memory_space=space))
    scratch["lazy_in"] = pltpu.SemaphoreType.DMA((max(len(lazy_in), 1),))
    scratch["lazy_out"] = pltpu.SemaphoreType.DMA((max(len(lazy_out), 1), 4))
    names += list(scratch)

    def whole(*refs):
        r = Refs([n for n in names if n], [ref for n, ref in zip(names, refs) if n])
        r.begin(lazy_in, lazy_out, [ref for n, ref in zip(names, refs) if not n])
        body(r)
        r.end()

    return pl.pallas_call(
        whole,
        in_specs=specs,
        out_specs=out_specs,
        out_shape=shapes,
        scratch_shapes=list(scratch.values()),
        compiler_params=pltpu.CompilerParams(
            collective_id=collective_id, has_side_effects=True, vmem_limit_bytes=limit * 2**20
        ),
        cost_estimate=pl.CostEstimate(
            flops=flops,
            bytes_accessed=sum(a.size * a.dtype.itemsize for a in arrays),
            transcendentals=0,
        ),
    )(*arrays)


def greet(peers):
    barrier = pltpu.get_barrier_semaphore()
    for peer in peers:
        pl.semaphore_signal(barrier, inc=1, device_id=peer, device_id_type=MESH)
    pl.semaphore_wait(barrier, len(peers))


def tensor_peers():
    me = lax.axis_index("tensor")
    return [dict(tensor=me ^ 1), dict(tensor=me ^ 2)]


def span_peers():
    me = lax.axis_index("dp")
    place = lax.rem(me, SPAN)
    return [dict(dp=me - place + lax.rem(place + k, SPAN)) for k in range(1, SPAN)]


def remote(src, dst, send, recv, peer):
    return pltpu.make_async_remote_copy(
        src_ref=src, dst_ref=dst, send_sem=send, recv_sem=recv, device_id=peer, device_id_type=MESH
    )


def exchange_scratch(rows, width):
    quarter = rows // 4
    return dict(
        near_rows=pltpu.VMEM((2 * quarter, width), BF16),
        across_rows=pltpu.VMEM((quarter, width), BF16),
        far_rows=pltpu.VMEM((quarter, width), BF16),
        x_send=pltpu.SemaphoreType.DMA((6 * CHUNKS,)),
        x_recv=pltpu.SemaphoreType.DMA((6 * CHUNKS,)),
    )


def sum_and_gather(r, partial, gathered, gathered_t, compute):
    near, across, far = r.near_rows, r.across_rows, r.far_rows
    core, other = tensor_peers()
    quarter = partial.shape[0] // 4
    size = quarter // CHUNKS
    copies = {}

    def copy(kind, at, src, dst, peer):
        number = kind * CHUNKS + at
        copies[kind, at] = remote(src, dst, r.x_send.at[number], r.x_recv.at[number], peer)
        copies[kind, at].start()

    def part(block, at):
        return pl.ds(block * quarter + at * size, size)

    def turn(block):
        if gathered_t is not None:
            rows = slice(block * quarter, (block + 1) * quarter)
            gathered_t[:, rows] = gathered[rows, :].T

    for at in range(CHUNKS):
        copy(0, at, partial.at[part(3, at)], near.at[part(1, at)], core)
    for at in range(CHUNKS):
        copy(1, at, partial.at[part(2, at)], near.at[part(0, at)], core)
    for at in range(CHUNKS):
        copies[0, at].wait_recv()
        far[part(0, at), :] = (
            partial[part(1, at), :].astype(F32) + near[part(1, at), :].astype(F32)
        ).astype(BF16)
        copy(2, at, far.at[part(0, at)], across.at[part(0, at)], other)
    yield 1
    for at in range(CHUNKS):
        copies[1, at].wait_recv()
        copies[2, at].wait_recv()
        total = (
            partial[part(0, at), :].astype(F32)
            + near[part(0, at), :].astype(F32)
            + across[part(0, at), :].astype(F32)
        )
        gathered[part(0, at), :] = compute(total, part(0, at), at == 0)
        copy(3, at, gathered.at[part(0, at)], gathered.at[part(1, at)], other)
        copy(4, at, gathered.at[part(0, at)], gathered.at[part(2, at)], core)
    turn(0)
    yield 1
    for at in range(CHUNKS):
        copies[3, at].wait_recv()
        copy(5, at, gathered.at[part(1, at)], gathered.at[part(3, at)], core)
    turn(1)
    for at in range(CHUNKS):
        copies[4, at].wait_recv()
    turn(2)
    for at in range(CHUNKS):
        copies[5, at].wait_recv()
    turn(3)
    for made in copies.values():
        made.wait_send()
    yield 1


def exhaust(main):
    for _ in main:
        pass


def norm_rows(total, rows, residual, gain, hidden):
    values = residual[rows, :] + total
    hidden[rows, :] = values
    return normalize(values, gain[...])[0].astype(BF16)


def back_rows(total, rows, first, hidden, gain, incoming, own, grad_gain):
    values = hidden[rows, :]
    inverse = lax.rsqrt(jnp.mean(values * values, axis=-1, keepdims=True) + EPSILON)
    made, term = normalize_back(values, inverse, gain[...], total)
    made = made + incoming[rows, :]
    if own is not None:
        own[rows, :] = made
    term = term.reshape(1, -1)
    grad_gain[...] = term if first else grad_gain[...] + term
    return made.astype(BF16)


def ring_peers(count):
    me = lax.axis_index("dp")
    even = lax.rem(me, 2) == 0
    place = jnp.where(even, me // 2, count - 1 - me // 2)

    def at(position):
        position = lax.rem(position + count, count)
        return jnp.where(position < count // 2, 2 * position, 2 * (count - 1 - position) + 1)

    return at(place + 1), at(place - 1), lambda distance: at(place + distance)


class Rings:
    def __init__(self, devices, sides, segments, held, send, recv, credit, store):
        self.devices, self.sides, self.segments, self.held = devices, sides, segments, held
        self.send, self.recv, self.credit, self.store = send, recv, credit, store
        self.rows = segments[0][0][0].shape[0] // devices
        self.half = self.rows // sides
        self.steps = devices - 1
        self.following, self.previous, self.owner_at = ring_peers(devices)

    def peers(self):
        return [dict(dp=self.following), dict(dp=self.previous)]

    def copy(self, seg, side, step):
        number = (seg * self.sides + side) * self.steps + step
        return remote(
            self.held[seg].at[side, step % SLOTS],
            self.held[seg].at[side, (step + 1) % SLOTS],
            self.send.at[number],
            self.recv.at[number],
            dict(dp=self.following if side == 0 else self.previous),
        )

    def unit(self, seg, step):
        sides, half, steps = self.sides, self.half, self.steps
        last = step == steps
        slot = step % SLOTS
        starts = []
        for side in range(sides):
            if last:
                owner = lax.axis_index("dp")
            else:
                owner = self.owner_at(-1 - step if side == 0 else 1 + step)
            starts.append(pl.multiple_of(owner * self.rows + side * half, 16))
        if step:
            for side in range(sides):
                self.copy(seg, side, step - 1).wait_send()
                if step <= steps + 1 - SLOTS:
                    pl.semaphore_signal(
                        self.credit.at[seg * sides + side],
                        inc=1,
                        device_id=dict(dp=self.previous if side == 0 else self.following),
                        device_id_type=MESH,
                    )
                self.copy(seg, side, step - 1).wait_recv()
        column = 0
        for left, right in self.segments[seg]:
            pieces = [left[pl.ds(start, half), :] for start in starts]
            piece = pieces[0] if sides == 1 else jnp.concatenate(pieces, axis=0)
            made = jnp.dot(piece, right[...], preferred_element_type=F32)
            at = slice(column, column + made.shape[1])
            values = []
            for side in range(sides):
                value = made[side * half : (side + 1) * half]
                if step:
                    value = value + self.held[seg][side, slot, :, at].astype(F32)
                if last:
                    values.append(value)
                else:
                    self.held[seg][side, slot, :, at] = value.astype(BF16)
            if last:
                self.store(seg, column, values[0] if sides == 1 else jnp.concatenate(values, axis=0))
            column += made.shape[1]
        if not last:
            for side in range(sides):
                if step >= SLOTS - 1:
                    pl.semaphore_wait(self.credit.at[seg * sides + side], 1)
                self.copy(seg, side, step).start()


def ring_scratch(devices, sides, rows, widths):
    copies = len(widths) * sides * (devices - 1)
    made = {
        f"held{at}": pltpu.VMEM((sides, SLOTS, rows // sides, w), BF16)
        for at, w in enumerate(widths)
    }
    made["r_send"] = pltpu.SemaphoreType.DMA((copies,))
    made["r_recv"] = pltpu.SemaphoreType.DMA((copies,))
    made["r_credit"] = pltpu.SemaphoreType.REGULAR((len(widths) * sides,))
    return made


def interleave(main, units, first):
    units = iter(units)

    def some(number):
        for _ in range(number):
            unit = next(units, None)
            if unit is not None:
                unit()

    some(first)
    for number in main:
        some(number)
    for unit in units:
        unit()


def piece_sides(width, devices):
    return 2 if width // devices % 32 == 0 else 1


def block_owners(index):
    return [index, index ^ 2, index ^ 1, index ^ 3]


def cross(left, right):
    return lax.dot_general(left, right, (((1,), (1,)), ((), ())), preferred_element_type=F32)


def turn_t(values, cosine, sine, back):
    middle = HEAD // 2
    low, high = values[:middle], values[middle:]
    if back:
        return jnp.concatenate([low * cosine + high * sine, high * cosine - low * sine], axis=0)
    return jnp.concatenate([low * cosine - high * sine, high * cosine + low * sine], axis=0)


def head_norm_t(values, gain):
    inverse = lax.rsqrt(jnp.mean(values * values, axis=0, keepdims=True) + EPSILON)
    return values * inverse * gain


def head_back_t(values, gain, grad):
    inverse = lax.rsqrt(jnp.mean(values * values, axis=0, keepdims=True) + EPSILON)
    weighted = grad * gain
    inner = jnp.mean(weighted * values, axis=0, keepdims=True)
    return inverse * (weighted - values * inverse * inverse * inner), grad * values * inverse


def fill_bias(r):
    keys = r.column_positions[...]
    allowed = (keys <= r.row_positions[...]) & (keys < r.length[0])
    r.bias[...] = jnp.where(allowed, 0.0, -1e30)


def head_rows(head):
    return slice(head * HEAD, (head + 1) * HEAD)


def position_inputs(positions, length):
    rows = positions.shape[0]
    return dict(
        length=(length.reshape(1), pltpu.SMEM),
        row_positions=positions.reshape(1, rows),
        column_positions=positions.reshape(rows, 1),
    )


def attention_forward(
    normed_b, query_weight, kv_weight, query_gain, key_gain, attn_out, residual, gain, tables, where,
    gate_up_t, down, grad_b,
):
    rows, width = normed_b.shape
    columns = query_weight.shape[1]
    kv_columns = kv_weight.shape[1] // 2
    heads, kv_heads = columns // HEAD, kv_columns // HEAD
    units = down.shape[0]

    def body(r):
        me = lax.axis_index("dp")
        place = lax.rem(me, SPAN)
        greet(tensor_peers() + span_peers())
        for copy in hidden_fetch(r, 0, TILE):
            copy.start()

        def pass_on(distance):
            return remote(
                r.own, r.near.at[distance - 1], r.p_send.at[distance - 1], r.p_recv.at[distance - 1],
                dict(dp=me + distance),
            )

        r.need(r.normed, r.kv_weight, r.cosine, r.sine)
        cosine, sine = r.cosine[...], r.sine[...]
        made = jnp.dot(r.normed[...], r.kv_weight[...], preferred_element_type=F32)
        r.key_raw[...] = made[:, :kv_columns].T
        r.own[:, kv_columns:] = made[:, kv_columns:].astype(BF16)
        for group in range(kv_heads):
            keys = head_norm_t(r.key_raw[head_rows(group), :], r.key_gain[...])
            r.keys_t[head_rows(group), :] = turn_t(keys, cosine, sine, False).astype(BF16)
        r.own[:, :kv_columns] = r.keys_t[...].T
        for distance in range(1, SPAN):

            @pl.when(place + distance < SPAN)
            def _():
                pass_on(distance).start()

        r.need(r.query_weight)
        made = jnp.dot(r.normed[...], r.query_weight[...], preferred_element_type=F32)
        r.query_raw[...] = made.T
        for head in range(heads):
            query = head_norm_t(r.query_raw[head_rows(head), :], r.query_gain[...])
            query = turn_t(query, cosine, sine, False).astype(BF16)
            r.query[head_rows(head), :] = query * jnp.asarray(HEAD ** (-0.5), BF16)
        fill_bias(r)

        def part(piece, first):
            for group in range(kv_heads):
                keys = piece[:, head_rows(group)]
                values_t = piece[:, kv_columns + group * HEAD : kv_columns + (group + 1) * HEAD].T
                for head in range(group * GROUP, (group + 1) * GROUP):
                    at = head_rows(head)
                    scores = jnp.dot(keys, r.query[at, :], preferred_element_type=F32)
                    if first:
                        scores = scores + r.bias[...]
                    expo = jnp.exp(scores)
                    total = jnp.sum(expo, axis=0, keepdims=True)
                    made = jnp.dot(values_t, expo.astype(BF16), preferred_element_type=F32)
                    if first:
                        r.total[head : head + 1, :] = total
                        r.attended_t[at, :] = made
                    else:
                        r.total[head : head + 1, :] += total
                        r.attended_t[at, :] += made

        part(r.own[...], True)

        @pl.loop(1, place + 1)
        def _(distance):
            pass_on(distance).wait_recv()
            part(r.near[distance - 1], False)

        for head in range(heads):
            at = head_rows(head)
            made = r.attended_t[at, :] / r.total[head : head + 1, :]
            r.attended_t[at, :] = made
            r.attended[:, at] = made.T.astype(BF16)
        r.log_total[...] = jnp.log(r.total[...])
        r.need(r.attn_out, r.residual, r.grad_b)
        r.flush(r.query_raw, r.key_raw, r.query, r.own, r.near, r.attended, r.attended_t, r.log_total)
        r.partial[...] = jnp.dot(
            r.attended[...], r.attn_out[...], preferred_element_type=F32
        ).astype(BF16)
        exhaust(
            sum_and_gather(
                r, r.partial, r.gathered, r.gathered_t,
                lambda total, at, first: norm_rows(total, at, r.residual, r.gain, r.hidden),
            )
        )
        r.flush(r.gathered_t, r.hidden)
        for distance in range(1, SPAN):

            @pl.when(place + distance < SPAN)
            def _():
                pass_on(distance).wait_send()

        def tile(number, wide, gate_w, up_w, down_w):
            lanes = tile_lanes(number, wide)
            a = cross(r.gathered[...], gate_w)
            z = cross(r.gathered[...], up_w)
            grad = cross(r.grad_b[...], down_w)
            sigma = jax.nn.sigmoid(a)
            r.active[:, lanes] = (a * sigma * z).astype(BF16)
            r.grad_gate[:, lanes] = (grad * z * sigma * (1.0 + a * (1.0 - sigma))).astype(BF16)
            r.grad_up[:, lanes] = (grad * a * sigma).astype(BF16)

        hidden_tiles(r, units, tile)
        r.flush(r.active, r.grad_gate, r.grad_up)

    return run_kernel(
        body,
        dict(
            normed=Lazy(normed_b),
            query_weight=Lazy(query_weight),
            kv_weight=Lazy(kv_weight),
            query_gain=query_gain.reshape(HEAD, 1),
            key_gain=key_gain.reshape(HEAD, 1),
            attn_out=Lazy(attn_out),
            residual=Lazy(residual),
            gain=gain.reshape(1, -1),
            cosine=Lazy(tables[0]),
            sine=Lazy(tables[1]),
            gate_up_t=(gate_up_t, pl.ANY),
            down=(down, pl.ANY),
            grad_b=Lazy(grad_b),
            **where,
        ),
        dict(
            active=Lazy((rows, units), BF16),
            grad_gate=Lazy((rows, units), BF16),
            grad_up=Lazy((rows, units), BF16),
            gathered_t=Lazy((width, rows), BF16),
            hidden=Lazy(residual.shape, F32),
            query_raw=Lazy((columns, rows), F32),
            key_raw=Lazy((kv_columns, rows), F32),
            query=Lazy((columns, rows), BF16),
            own=Lazy((rows, 2 * kv_columns), BF16),
            near=Lazy((SPAN - 1, rows, 2 * kv_columns), BF16),
            attended=Lazy((rows, columns), BF16),
            attended_t=Lazy((columns, rows), F32),
            log_total=Lazy((heads, rows), F32),
        ),
        dict(
            keys_t=pltpu.VMEM((kv_columns, rows), BF16),
            bias=pltpu.VMEM((rows, rows), F32),
            total=pltpu.VMEM((heads, rows), F32),
            partial=pltpu.VMEM((rows, width), BF16),
            gathered=pltpu.VMEM((rows, width), BF16),
            **hidden_scratch(width),
            p_send=pltpu.SemaphoreType.DMA((SPAN - 1,)),
            p_recv=pltpu.SemaphoreType.DMA((SPAN - 1,)),
            **exchange_scratch(rows, width),
        ),
        2,
        58,
        16 * rows * rows * SPAN * columns,
    )


def stream_product(r, lefts, weights, out):
    width = weights.shape[2]
    size = r.tile.shape[3]
    tiles = width // size

    def fetch(j):
        return [
            pltpu.make_async_copy(
                weights.at[k, :, pl.ds(j * size, size)], r.tile.at[j % 2, k], r.tile_sem.at[j % 2, k]
            )
            for k in range(len(lefts))
        ]

    for copy in fetch(0):
        copy.start()
    for j in range(tiles):
        if j + 1 < tiles:
            for copy in fetch(j + 1):
                copy.start()
        for copy in fetch(j):
            copy.wait()
        made = None
        for k, left in enumerate(lefts):
            term = jnp.dot(left[...], r.tile[j % 2, k], preferred_element_type=F32)
            made = term if made is None else made + term
        out[:, j * size : (j + 1) * size] = made.astype(BF16)
        if j % 2:
            yield 1


def stream_scratch(count, depth, size):
    return dict(
        tile=pltpu.VMEM((2, count, depth, size), BF16),
        tile_sem=pltpu.SemaphoreType.DMA((2, count)),
    )


def attention_backward(
    grad_b_t, norm_two_t, active, grad_gate, grad_up, gate_up_t, down, three, norm_mlp, incoming,
    kept, attn_out, query_weight, kv_weight, query_gain, key_gain, two, norm_attn, tables, where, devices,
):
    units, tokens_width = gate_up_t.shape[1:]
    query_raw, key_raw, query, own, near, attended_t, log_total = kept
    rows, width = active.shape[0], tokens_width
    columns = query_weight.shape[1]
    kv_columns = kv_weight.shape[1] // 2
    heads, kv_heads = columns // HEAD, kv_columns // HEAD
    sides = piece_sides(width, devices)
    block = width // devices
    segment_widths = [units] * 3

    def body(r):
        me = lax.axis_index("dp")
        place = lax.rem(me, SPAN)

        def store(seg, column, value):
            if seg == 0:
                r.sum_down[...] = value
                r.flush(r.sum_down)
            else:
                r.sum_gate_up[:, seg - 1, :] = value
                if seg == 2:
                    r.flush(r.sum_gate_up)

        rings = Rings(
            devices, sides,
            [[(r.grad_b_t, r.active)], [(r.norm_two_t, r.grad_gate)], [(r.norm_two_t, r.grad_up)]],
            [r.held0, r.held1, r.held2], r.r_send, r.r_recv, r.r_credit, store,
        )
        greet(rings.peers() + tensor_peers() + span_peers())

        def pass_back(distance):
            return remote(
                r.far.at[distance - 1], r.arrived.at[distance - 1],
                r.p_send.at[distance - 1], r.p_recv.at[distance - 1], dict(dp=me - distance),
            )

        def part(piece, write, masked):
            for group in range(kv_heads):
                keys = piece[:, head_rows(group)]
                value_at = slice(kv_columns + group * HEAD, kv_columns + (group + 1) * HEAD)
                values = piece[:, value_at]
                keys_t = keys.T
                grad_k = grad_v = None
                for head in range(group * GROUP, (group + 1) * GROUP):
                    at = head_rows(head)
                    q, grads = r.query[at, :], r.grads[:, at]
                    scores = jnp.dot(keys, q, preferred_element_type=F32)
                    scores = scores - r.log_total[head : head + 1, :]
                    if masked:
                        scores = scores + r.bias[...]
                    probs = jnp.exp(scores)
                    made = jnp.dot(probs.astype(BF16), grads, preferred_element_type=F32)
                    grad_v = made if grad_v is None else grad_v + made
                    grad_probs = cross(values, grads)
                    grad_scores = (probs * (grad_probs - r.delta[head : head + 1, :])).astype(BF16)
                    made = cross(grad_scores, q)
                    grad_k = made if grad_k is None else grad_k + made
                    made = jnp.dot(keys_t, grad_scores, preferred_element_type=F32)
                    if masked:
                        r.grad_q_t[at, :] = made
                    else:
                        r.grad_q_t[at, :] += made
                write(head_rows(group), grad_k)
                write(value_at, grad_v)

        def main():
            yield from stream_product(r, [r.grad_gate, r.grad_up], r.gate_up_t, r.partial)
            fill_bias(r)
            r.need(r.three, r.incoming)
            yield from sum_and_gather(
                r, r.partial, r.gathered, r.grad_three_t,
                lambda total, at, first: back_rows(
                    total, at, first, r.three, r.norm_mlp, r.incoming, r.grad_three, r.grad_norm_mlp
                ),
            )
            r.flush(r.grad_three_t)
            r.need(r.attn_out, r.attended_t, r.own, r.near, r.query, r.log_total)
            r.grads[...] = cross(r.gathered[...], r.attn_out[...]).astype(BF16)
            for head in range(heads):
                at = head_rows(head)
                grads_t = r.grads[:, at].astype(F32).T
                r.delta[head : head + 1, :] = jnp.sum(
                    grads_t * r.attended_t[at, :], axis=0, keepdims=True
                )
            yield 1

            def write_own(at, value):
                r.grad_own[:, at] = value

            part(r.own[...], write_own, True)
            yield 1

            @pl.loop(1, place + 1)
            def _(distance):
                def write_far(at, value):
                    r.far[distance - 1, :, at] = value.astype(BF16)

                part(r.near[distance - 1], write_far, False)
                pass_back(distance).start()

            yield 2
            r.need(r.cosine, r.sine, r.query_raw, r.key_raw, r.query_weight, r.kv_weight, r.two)
            cosine, sine = r.cosine[...], r.sine[...]
            terms = None
            for head in range(heads):
                at = head_rows(head)
                grad = turn_t(r.grad_q_t[at, :] * HEAD ** (-0.5), cosine, sine, True)
                made, term = head_back_t(r.query_raw[at, :], r.query_gain[...], grad)
                terms = term if terms is None else terms + term
                r.grad_query[:, at] = made.T.astype(BF16)
            r.grad_query_gain[...] = jnp.sum(terms, axis=1, keepdims=True)
            yield 1
            for distance in range(1, SPAN):

                @pl.when(place + distance < SPAN)
                def _():
                    pass_back(distance).wait_recv()
                    r.grad_own[...] += r.arrived[distance - 1].astype(F32)

            terms = None
            for group in range(kv_heads):
                at = head_rows(group)
                grad = turn_t(r.grad_own[:, at].T, cosine, sine, True)
                made, term = head_back_t(r.key_raw[at, :], r.key_gain[...], grad)
                terms = term if terms is None else terms + term
                r.grad_kv[:, at] = made.T.astype(BF16)
            r.grad_key_gain[...] = jnp.sum(terms, axis=1, keepdims=True)
            r.grad_kv[:, kv_columns:] = r.grad_own[:, kv_columns:].astype(BF16)
            r.flush(r.grad_query, r.grad_kv)
            r.partial[...] = (
                cross(r.grad_query[...], r.query_weight[...]) + cross(r.grad_kv[...], r.kv_weight[...])
            ).astype(BF16)
            yield 1
            yield from sum_and_gather(
                r, r.partial, r.grad_two_b, r.grad_two_t,
                lambda total, at, first: back_rows(
                    total, at, first, r.two, r.norm_attn, r.grad_three, r.grad_two, r.grad_norm_attn
                ),
            )
            r.flush(r.grad_two_b, r.grad_two_t, r.grad_two)
            for distance in range(1, SPAN):

                @pl.when(place >= distance)
                def _():
                    pass_back(distance).wait_send()

            yield from stream_product(r, [r.active], r.down, r.partial)
            yield from sum_and_gather(
                r, r.partial, r.output, None,
                lambda total, at, first: (r.three[at, :] + total).astype(BF16),
            )
            r.flush_blocks(r.output, block_owners(lax.axis_index("tensor")))

        def first(seg):
            r.need(*((r.grad_b_t, r.active), (r.norm_two_t, r.grad_gate), (r.grad_up,))[seg])
            rings.unit(seg, 0)

        order = [(seg, step) for step in range(1, devices) for seg in range(3)]
        units_left = [lambda s=seg: first(s) for seg in range(3)]
        units_left += [lambda u=u: rings.unit(*u) for u in order]
        interleave(main(), units_left, 3)

    quarter = rows // 4
    return run_kernel(
        body,
        dict(
            grad_b_t=Lazy(grad_b_t),
            active=Lazy(active),
            norm_two_t=Lazy(norm_two_t),
            grad_gate=Lazy(grad_gate),
            grad_up=Lazy(grad_up),
            gate_up_t=(gate_up_t, pl.ANY),
            down=(down.reshape((1,) + down.shape), pl.ANY),
            three=Lazy(three),
            norm_mlp=norm_mlp.reshape(1, -1),
            incoming=Lazy(incoming),
            query_raw=Lazy(query_raw),
            key_raw=Lazy(key_raw),
            query=Lazy(query),
            own=Lazy(own),
            near=Lazy(near),
            attended_t=Lazy(attended_t),
            log_total=Lazy(log_total),
            attn_out=Lazy(attn_out),
            query_weight=Lazy(query_weight),
            kv_weight=Lazy(kv_weight),
            query_gain=query_gain.reshape(HEAD, 1),
            key_gain=key_gain.reshape(HEAD, 1),
            two=Lazy(two),
            norm_attn=norm_attn.reshape(1, -1),
            cosine=Lazy(tables[0]),
            sine=Lazy(tables[1]),
            **where,
        ),
        dict(
            grad_three_t=Lazy((width, rows), BF16),
            grad_query=Lazy((rows, columns), BF16),
            grad_kv=Lazy((rows, 2 * kv_columns), BF16),
            grad_two_b=Lazy((rows, width), BF16),
            grad_two_t=Lazy((width, rows), BF16),
            grad_two=Lazy((quarter, width), F32),
            grad_norm_mlp=((1, width), F32),
            grad_norm_attn=((1, width), F32),
            grad_query_gain=((HEAD, 1), F32),
            grad_key_gain=((HEAD, 1), F32),
            sum_down=Lazy((block, units), F32),
            sum_gate_up=Lazy((block, 2, units), F32),
            output=Lazy((rows, width), BF16),
        ),
        dict(
            partial=pltpu.VMEM((rows, width), BF16),
            gathered=pltpu.VMEM((rows, width), BF16),
            grad_three=pltpu.VMEM((quarter, width), F32),
            grads=pltpu.VMEM((rows, columns), BF16),
            delta=pltpu.VMEM((heads, rows), F32),
            bias=pltpu.VMEM((rows, rows), F32),
            grad_q_t=pltpu.VMEM((columns, rows), F32),
            grad_own=pltpu.VMEM((rows, 2 * kv_columns), F32),
            far=pltpu.VMEM((SPAN - 1, rows, 2 * kv_columns), BF16),
            arrived=pltpu.VMEM((SPAN - 1, rows, 2 * kv_columns), BF16),
            p_send=pltpu.SemaphoreType.DMA((SPAN - 1,)),
            p_recv=pltpu.SemaphoreType.DMA((SPAN - 1,)),
            **stream_scratch(2, units, 256),
            **exchange_scratch(rows, width),
            **ring_scratch(devices, sides, block, segment_widths),
        ),
        3 + 2,
        61,
        2 * rows * width * units * 10,
    )


TILE = 256


def unit_tiles(units):
    return [(at, min(TILE, units - at)) for at in range(0, units, TILE)]


def hidden_fetch(r, number, wide):
    slot = lax.rem(number, 2)
    rows = pl.ds(number * TILE, wide)
    pairs = [
        (r.gate_up_t.at[:, rows, :], r.gate_up_tile.at[slot, :, 0:wide, :]),
        (r.down.at[rows, :], r.down_tile.at[slot, 0:wide, :]),
    ]
    return [pltpu.make_async_copy(a, b, r.h_sem.at[slot, k]) for k, (a, b) in enumerate(pairs)]


def hidden_tiles(r, units, tile):
    count = pl.cdiv(units, TILE)
    rest = units - (count - 1) * TILE

    def run(number, wide):
        for copy in hidden_fetch(r, number, wide):
            copy.wait()
        slot = lax.rem(number, 2)
        tile(
            number, wide,
            r.gate_up_tile[slot, 0, 0:wide, :],
            r.gate_up_tile[slot, 1, 0:wide, :],
            r.down_tile[slot, 0:wide, :],
        )

    @pl.loop(0, count - 1)
    def _(number):
        @pl.when(number + 1 < count - 1)
        def _():
            for copy in hidden_fetch(r, number + 1, TILE):
                copy.start()

        @pl.when(number + 1 == count - 1)
        def _():
            for copy in hidden_fetch(r, number + 1, rest):
                copy.start()

        run(number, TILE)

    run(count - 1, rest)


def tile_lanes(number, wide):
    start = number * TILE
    return pl.ds(start if isinstance(start, int) else pl.multiple_of(start, TILE), wide)


def hidden_scratch(width):
    return dict(
        gate_up_tile=pltpu.VMEM((2, 2, TILE, width), BF16),
        down_tile=pltpu.VMEM((2, TILE, width), BF16),
        h_sem=pltpu.SemaphoreType.DMA((2, 2)),
    )


def first_forward(
    tokens, cotangent, norm_conv, conv_in_t, kernel, conv_out, norm_mlp, gate_up_t, down, norm_attn, where
):
    rows, width = tokens.shape
    channels = conv_out.shape[0]
    units = down.shape[0]
    quarter = rows // 4
    count = len(unit_tiles(units))

    def body(r):
        me = lax.axis_index("dp")
        index = lax.axis_index("tensor")
        place = lax.rem(me, SPAN)
        greet(tensor_peers() + span_peers())
        for copy in hidden_fetch(r, 0, TILE):
            copy.start()
        r.need(r.tokens)
        for at in range(4):
            part = slice(at * quarter, (at + 1) * quarter)
            values = r.tokens[part, :].astype(F32)
            r.normed[part, :] = normalize(values, r.norm_conv[...])[0].astype(BF16)
        r.need(r.conv_in_t)
        for at in range(3):
            made = jnp.dot(r.normed[...], r.conv_in_t[at], preferred_element_type=F32)
            r.projected[:, at * channels : (at + 1) * channels] = made
        r.flush(r.projected)
        pad = 8
        r.mixed[0:pad, :] = jnp.zeros((pad, channels), F32)
        r.mixed[pad:, :] = r.projected[:, :channels] * r.projected[:, 2 * channels :]
        r.rim_out[...] = r.mixed[rows : rows + pad, :]
        rim_copy = remote(r.rim_out, r.rim_in, r.m_sem.at[0], r.m_sem.at[1], dict(dp=me + 1))

        @pl.when(place < SPAN - 1)
        def _():
            rim_copy.start()

        start = pl.multiple_of(index * quarter, quarter)
        r.inputs_own[...] = r.tokens[pl.ds(start, quarter), :].astype(F32)
        r.flush(r.inputs_own)

        @pl.when(place > 0)
        def _():
            rim_copy.wait_recv()
            r.mixed[0:pad, :] = r.rim_in[...]

        r.rim[...] = r.mixed[0:pad, :]
        r.flush(r.rim)
        taps = r.kernel[...].astype(F32)
        convolved = None
        for k in range(KW):
            term = taps[k : k + 1, :] * r.mixed[pad - KW + 1 + k : pad - KW + 1 + k + rows, :]
            convolved = term if convolved is None else convolved + term
        r.gated_true[...] = (r.projected[:, channels : 2 * channels] * convolved).astype(BF16)
        for at, owner in enumerate(block_owners(index)):
            start = pl.multiple_of(owner * quarter, quarter)
            r.gated[at * quarter : (at + 1) * quarter, :] = r.gated_true[pl.ds(start, quarter), :]
        r.need(r.conv_out)
        r.partial[...] = jnp.dot(r.gated[...], r.conv_out[...], preferred_element_type=F32).astype(BF16)
        r.flush(r.gated)
        waits = sum_and_gather(
            r, r.partial, r.gathered_one, r.norm_one_t,
            lambda total, at, first: norm_rows(total, at, r.inputs_own, r.norm_mlp, r.one),
        )
        next(waits)
        r.need(r.cotangent)
        for at, owner in enumerate(block_owners(index)):
            part = slice(at * quarter, (at + 1) * quarter)
            start = pl.multiple_of(owner * quarter, quarter)
            live = r.column_positions[part, :] < r.length[0]
            values = jnp.where(live, r.cotangent[pl.ds(start, quarter), :].astype(F32), 0.0)
            if at == 0:
                r.incoming[...] = values
            r.grad_b[part, :] = values.astype(BF16)
        next(waits)
        r.normed_t[...] = r.normed[...].T
        r.grad_b_t[...] = r.grad_b[...].T
        r.flush(r.normed_t, r.grad_b, r.grad_b_t, r.incoming)
        exhaust(waits)
        r.flush(r.one, r.norm_one_t)
        r.total[...] = jnp.zeros_like(r.total)

        def tile(number, wide, gate_w, up_w, down_w):
            a = cross(r.gathered_one[...], gate_w)
            z = cross(r.gathered_one[...], up_w)
            r.gate[number, :, 0:wide] = a
            r.upward[number, :, 0:wide] = z
            s = (a * jax.nn.sigmoid(a) * z).astype(BF16)
            r.active[:, tile_lanes(number, wide)] = s
            r.total[...] += jnp.dot(s, down_w, preferred_element_type=F32)

        hidden_tiles(r, units, tile)
        r.partial[...] = r.total[...].astype(BF16)
        r.flush(r.active, r.gate, r.upward)
        exhaust(
            sum_and_gather(
                r, r.partial, r.gathered, r.normed_attn_t,
                lambda total, at, first: norm_rows(total, at, r.one, r.norm_attn, r.two),
            )
        )
        r.flush(r.gathered, r.normed_attn_t, r.two)

        @pl.when(place < SPAN - 1)
        def _():
            rim_copy.wait_send()

    return run_kernel(
        body,
        dict(
            tokens=Lazy(tokens),
            cotangent=Lazy(cotangent),
            norm_conv=norm_conv.reshape(1, -1),
            conv_in_t=Lazy(conv_in_t),
            kernel=kernel,
            conv_out=Lazy(conv_out),
            norm_mlp=norm_mlp.reshape(1, -1),
            gate_up_t=(gate_up_t, pl.ANY),
            down=(down, pl.ANY),
            norm_attn=norm_attn.reshape(1, -1),
            **where,
        ),
        dict(
            gathered=Lazy((rows, width), BF16),
            normed_attn_t=Lazy((width, rows), BF16),
            two=Lazy((quarter, width), F32),
            one=Lazy((quarter, width), F32),
            inputs_own=Lazy((quarter, width), F32),
            norm_one_t=Lazy((width, rows), BF16),
            normed_t=Lazy((width, rows), BF16),
            active=Lazy((rows, units), BF16),
            gate=Lazy((count, rows, TILE), F32),
            upward=Lazy((count, rows, TILE), F32),
            gated=Lazy((rows, channels), BF16),
            projected=Lazy((rows, 3 * channels), F32),
            rim=Lazy((8, channels), F32),
            grad_b=Lazy((rows, width), BF16),
            grad_b_t=Lazy((width, rows), BF16),
            incoming=Lazy((quarter, width), F32),
        ),
        dict(
            normed=pltpu.VMEM((rows, width), BF16),
            partial=pltpu.VMEM((rows, width), BF16),
            gathered_one=pltpu.VMEM((rows, width), BF16),
            total=pltpu.VMEM((rows, width), F32),
            gated_true=pltpu.VMEM((rows, channels), BF16),
            mixed=pltpu.VMEM((rows + 8, channels), F32),
            rim_out=pltpu.VMEM((8, channels), F32),
            rim_in=pltpu.VMEM((8, channels), F32),
            m_sem=pltpu.SemaphoreType.DMA((2,)),
            **hidden_scratch(width),
            **exchange_scratch(rows, width),
        ),
        1,
        60,
        6 * rows * width * units,
    )


class Pump:
    def __init__(self, rings, ready):
        self.rings, self.ready = rings, list(ready)
        self.step = [0] * len(rings.segments)
        self.before = None

    def run(self, number):
        for _ in range(number):
            left = [s for s in self.ready if self.step[s] <= self.rings.steps]
            if not left:
                return
            seg = min(left, key=lambda s: (s == self.before, self.step[s], s))
            self.rings.unit(seg, self.step[seg])
            self.step[seg] += 1
            self.before = seg

    def rest(self):
        self.run(len(self.step) * (self.rings.steps + 1))


def first_backward(
    lefts, rights, grad_two_b, down, gate_up_t, gate, upward, one, norm_mlp, grad_two, conv_out,
    conv_in_t, projected, rim, kernel, inputs, norm_conv, small, devices,
):
    rows, width = grad_two_b.shape
    units = down.shape[0]
    channels = conv_out.shape[0]
    quarter = rows // 4
    block = width // devices
    sides = piece_sides(width, devices)
    grad_three_t, normed_attn_t, grad_two_t, norm_one_t, normed_conv_t = lefts
    attended, grad_query, grad_kv, active, gated = rights
    columns, kv_columns = grad_query.shape[1], grad_kv.shape[1]
    widths = [channels + columns + kv_columns, units, units, units, 4 * channels]
    bits = []
    bit = 1
    while bit < devices:
        bits.append(bit)
        bit *= 2
    stages = 2 + len(bits)
    size = TILE
    tiles = [(at, min(size, units - at)) for at in range(0, units, size)]

    def body(r):
        me = lax.axis_index("dp")
        index = lax.axis_index("tensor")
        place = lax.rem(me, SPAN)

        done = []

        def store(seg, column, value):
            if seg == 0:
                at = (0, channels, channels + columns).index(column)
                ref = (r.sum_attn_out, r.sum_query, r.sum_kv)[at]
                ref[...] = value
                r.flush(ref)
            elif seg == 1:
                r.sum_down[...] = value
                r.flush(r.sum_down)
            elif seg < 4:
                r.sum_gate_up[:, seg - 2, :] = value
                done.append(seg)
                if len(done) == 2:
                    r.flush(r.sum_gate_up)
            elif column == 0:
                r.sum_conv_out[...] = value
                r.flush(r.sum_conv_out)
            else:
                for at in range(3):
                    r.sum_conv_in[at] = value[:, at * channels : (at + 1) * channels]
                r.flush(r.sum_conv_in)

        rings = Rings(
            devices, sides,
            [
                [
                    (r.grad_three_t, r.attended),
                    (r.normed_attn_t, r.grad_query),
                    (r.normed_attn_t, r.grad_kv),
                ],
                [(r.grad_two_t, r.active)],
                [(r.norm_one_t, r.grad_gate)],
                [(r.norm_one_t, r.grad_up)],
                [(r.grad_one_t, r.gated), (r.normed_conv_t, r.grad_projected)],
            ],
            [r.held0, r.held1, r.held2, r.held3, r.held4], r.r_send, r.r_recv, r.r_credit, store,
        )
        pump = Pump(rings, [0, 1])
        small_peers = tensor_peers() + [dict(dp=me ^ bit) for bit in bits]
        greet(rings.peers() + small_peers + span_peers())

        def fetch(number):
            at, wide = tiles[number]
            slot = number % 2
            pairs = [
                (r.down.at[at : at + wide, :], r.down_tile.at[slot, 0:wide, :]),
                (r.gate.at[number], r.gate_tile.at[slot]),
                (r.upward.at[number], r.up_tile.at[slot]),
            ]
            return [
                pltpu.make_async_copy(a, b, r.h_sem.at[slot, k]) for k, (a, b) in enumerate(pairs)
            ]

        def fetch_conv(number):
            slot = number % 2
            return [
                pltpu.make_async_copy(
                    r.conv_in_t.at[k, pl.ds(number * size, size), :],
                    r.conv_tile.at[slot, k],
                    r.c_sem.at[slot, k],
                )
                for k in range(3)
            ]

        def main():
            first = pltpu.make_async_copy(r.grad_two_b, r.gathered, r.e_sem)
            first.start()
            for copy in fetch(0):
                copy.start()
            first.wait()
            for number, (at, wide) in enumerate(tiles):
                if number + 1 < len(tiles):
                    for copy in fetch(number + 1):
                        copy.start()
                for copy in fetch(number):
                    copy.wait()
                slot = number % 2
                grad = cross(r.gathered[...], r.down_tile[slot, 0:wide, :])
                gates, ups = r.gate_tile[slot, :, 0:wide], r.up_tile[slot, :, 0:wide]
                sigma = jax.nn.sigmoid(gates)
                r.grad_gate[:, at : at + wide] = (
                    grad * ups * sigma * (1.0 + gates * (1.0 - sigma))
                ).astype(BF16)
                r.grad_up[:, at : at + wide] = (grad * gates * sigma).astype(BF16)
                if number % 3 == 2:
                    yield 1
            r.need(r.norm_one_t, r.one, r.grad_two)
            pump.ready += [2, 3]
            yield 2
            yield from stream_product(r, [r.grad_gate, r.grad_up], r.gate_up_t, r.partial)
            yield from sum_and_gather(
                r, r.partial, r.gathered, r.grad_one_t,
                lambda total, at, first: back_rows(
                    total, at, first, r.one, r.norm_mlp, r.grad_two, r.grad_one, r.gain_term
                ),
            )
            r.small_out[...] = r.small[...]
            r.small_out[1:2, :] = r.gain_term[...]

            r.need(r.conv_out, r.projected, r.rim, r.gated, r.normed_conv_t, r.inputs)
            made = cross(r.gathered[...], r.conv_out[...])
            for at, owner in enumerate(block_owners(index)):
                start = pl.multiple_of(owner * quarter, quarter)
                r.grad_gated[pl.ds(start, quarter), :] = made[at * quarter : (at + 1) * quarter]
            before = r.projected[:, :channels]
            signal = r.projected[:, 2 * channels :]
            taps = r.kernel[...].astype(F32)
            pad = 8
            r.mixed[pad:, :] = before * signal
            r.mixed[0:pad, :] = r.rim[...]
            grad_gated = r.grad_gated[...]
            r.grad_conv[0:rows, :] = grad_gated * r.projected[:, channels : 2 * channels]
            r.grad_conv[rows:, :] = jnp.zeros_like(r.grad_conv[rows:, :])
            r.rim_out[...] = r.grad_conv[0:pad, :]
            rim_copy = remote(r.rim_out, r.rim_in, r.m_sem.at[0], r.m_sem.at[1], dict(dp=me - 1))

            @pl.when(place > 0)
            def _():
                rim_copy.start()

            yield 1
            convolved = None
            for k in range(KW):
                shifted = r.mixed[pad - KW + 1 + k : pad - KW + 1 + k + rows, :]
                term = taps[k : k + 1, :] * shifted
                convolved = term if convolved is None else convolved + term
                term = jnp.sum(r.grad_conv[0:rows, :] * shifted, axis=0, keepdims=True)
                r.small_out[5 + k : 6 + k, 0:channels] = term
            r.grad_projected[:, channels : 2 * channels] = (grad_gated * convolved).astype(BF16)

            @pl.when(place < SPAN - 1)
            def _():
                rim_copy.wait_recv()
                r.grad_conv[rows:, :] = r.rim_in[...]

            grad_mixed = None
            for k in range(KW):
                term = taps[k : k + 1, :] * r.grad_conv[KW - 1 - k : KW - 1 - k + rows, :]
                grad_mixed = term if grad_mixed is None else grad_mixed + term
            r.grad_projected[:, :channels] = (grad_mixed * signal).astype(BF16)
            r.grad_projected[:, 2 * channels :] = (grad_mixed * before).astype(BF16)

            @pl.when(place > 0)
            def _():
                rim_copy.wait_send()

            pump.ready += [4]
            yield 2
            for copy in fetch_conv(0):
                copy.start()
            for number in range(width // size):
                if number + 1 < width // size:
                    for copy in fetch_conv(number + 1):
                        copy.start()
                for copy in fetch_conv(number):
                    copy.wait()
                for at, owner in enumerate(block_owners(index)):
                    start = pl.multiple_of(owner * quarter, quarter)
                    made = None
                    for k in range(3):
                        piece = r.grad_projected[
                            pl.ds(start, quarter), k * channels : (k + 1) * channels
                        ]
                        term = cross(piece, r.conv_tile[number % 2, k])
                        made = term if made is None else made + term
                    r.partial[
                        at * quarter : (at + 1) * quarter, number * size : (number + 1) * size
                    ] = made.astype(BF16)
                if number % 2:
                    yield 1
            yield from sum_and_gather(
                r, r.partial, r.input_grad, None,
                lambda total, at, first: back_rows(
                    total, at, first, r.inputs, r.norm_conv, r.grad_one, None, r.gain_term
                ),
            )
            r.flush_blocks(r.input_grad, block_owners(index))
            r.small_out[0:1, :] = r.gain_term[...]
            row = lax.broadcasted_iota(jnp.int32, small.shape, 0)
            for stage in range(stages):
                copy = remote(
                    r.small_out, r.slots.at[stage], r.s_send.at[stage], r.s_recv.at[stage],
                    small_peers[stage],
                )
                copy.start()
                yield 1
                copy.wait()
                if stage < 2:
                    r.small_out[...] += jnp.where(row < 5, r.slots[stage], 0.0)
                else:
                    r.small_out[...] += r.slots[stage]
            r.flush(r.small_out)

        r.need(r.grad_three_t, r.attended, r.normed_attn_t, r.grad_query, r.grad_kv)
        pump.run(1)
        r.need(r.grad_two_t, r.active)
        pump.run(1)
        for number in main():
            pump.run(number)
        pump.rest()

    return run_kernel(
        body,
        dict(
            grad_three_t=Lazy(grad_three_t),
            attended=Lazy(attended),
            normed_attn_t=Lazy(normed_attn_t),
            grad_query=Lazy(grad_query),
            grad_kv=Lazy(grad_kv),
            grad_two_t=Lazy(grad_two_t),
            active=Lazy(active),
            norm_one_t=Lazy(norm_one_t),
            one=Lazy(one),
            grad_two=Lazy(grad_two),
            conv_out=Lazy(conv_out),
            projected=Lazy(projected),
            rim=Lazy(rim),
            gated=Lazy(gated),
            normed_conv_t=Lazy(normed_conv_t),
            inputs=Lazy(inputs),
            grad_two_b=(grad_two_b, pl.ANY),
            down=(down, pl.ANY),
            gate_up_t=(gate_up_t, pl.ANY),
            gate=(gate, pl.ANY),
            upward=(upward, pl.ANY),
            norm_mlp=norm_mlp.reshape(1, -1),
            conv_in_t=(conv_in_t, pl.ANY),
            kernel=kernel,
            norm_conv=norm_conv.reshape(1, -1),
            small=small,
        ),
        dict(
            input_grad=Lazy((rows, width), BF16),
            small_out=Lazy(small.shape, F32),
            sum_attn_out=Lazy((block, channels), F32),
            sum_query=Lazy((block, columns), F32),
            sum_kv=Lazy((block, kv_columns), F32),
            sum_down=Lazy((block, units), F32),
            sum_gate_up=Lazy((block, 2, units), F32),
            sum_conv_out=Lazy((block, channels), F32),
            sum_conv_in=Lazy((3, block, channels), F32),
        ),
        dict(
            gathered=pltpu.VMEM((rows, width), BF16),
            partial=pltpu.VMEM((rows, width), BF16),
            grad_one_t=pltpu.VMEM((width, rows), BF16),
            grad_one=pltpu.VMEM((quarter, width), F32),
            grad_gate=pltpu.VMEM((rows, units), BF16),
            grad_up=pltpu.VMEM((rows, units), BF16),
            grad_projected=pltpu.VMEM((rows, 3 * channels), BF16),
            grad_gated=pltpu.VMEM((rows, channels), F32),
            mixed=pltpu.VMEM((rows + 8, channels), F32),
            grad_conv=pltpu.VMEM((rows + 8, channels), F32),
            rim_out=pltpu.VMEM((8, channels), F32),
            rim_in=pltpu.VMEM((8, channels), F32),
            m_sem=pltpu.SemaphoreType.DMA((2,)),
            e_sem=pltpu.SemaphoreType.DMA,
            down_tile=pltpu.VMEM((2, size, width), BF16),
            gate_tile=pltpu.VMEM((2, rows, size), F32),
            up_tile=pltpu.VMEM((2, rows, size), F32),
            h_sem=pltpu.SemaphoreType.DMA((2, 3)),
            conv_tile=pltpu.VMEM((2, 3, size, channels), BF16),
            c_sem=pltpu.SemaphoreType.DMA((2, 3)),
            gain_term=pltpu.VMEM((1, width), F32),
            slots=pltpu.VMEM((stages,) + small.shape, F32),
            s_send=pltpu.SemaphoreType.DMA((stages,)),
            s_recv=pltpu.SemaphoreType.DMA((stages,)),
            **stream_scratch(2, units, 128),
            **exchange_scratch(rows, width),
            **ring_scratch(devices, sides, block, widths),
        ),
        4,
        62,
        2 * rows * width * sum(widths) * 3,
    )


def local(
    tokens,
    lengths,
    norm_conv,
    conv_in,
    conv_kernel,
    conv_out,
    norm_mlp_one,
    gate_up_one,
    down_one,
    norm_attn,
    query_weight,
    kv_weight,
    query_gain,
    key_gain,
    attn_out,
    norm_mlp_two,
    gate_up_two,
    down_two,
    cotangent,
):
    row_count = tokens.shape[0]
    width = tokens.shape[1]
    quarter = row_count // 4
    local_kv = kv_weight.shape[2] // HEAD
    device = lax.axis_index("dp")
    devices = lax.axis_size("dp")
    index = lax.axis_index("tensor")
    sequence = device // SPAN
    place_index = device % SPAN
    length = lengths[sequence]
    offsets = jnp.concatenate(
        [o * quarter + jnp.arange(quarter, dtype=jnp.int32) for o in block_owners(index)]
    )
    positions = place_index * row_count + offsets
    frequency = THETA ** (-2.0 * jnp.arange(HEAD // 2, dtype=jnp.float32) / HEAD)
    angles = frequency[:, None] * positions.astype(jnp.float32)[None, :]
    tables = (jnp.cos(angles), jnp.sin(angles))
    where = position_inputs(positions, length)
    gate_up_one_t = jnp.transpose(gate_up_one, (1, 2, 0))
    gate_up_two_t = jnp.transpose(gate_up_two, (1, 2, 0))
    conv_in_t = jnp.transpose(conv_in, (1, 0, 2))
    kv_flat = kv_weight.reshape(width, 2 * local_kv * HEAD)

    (
        normed_attn_b,
        normed_attn_t,
        two_own,
        one_own,
        inputs_own,
        norm_one_t,
        normed_conv_t,
        active_one,
        gate_one,
        up_one,
        gated_b,
        projected,
        rim,
        grad_b,
        grad_b_t,
        incoming,
    ) = first_forward(
        tokens,
        cotangent,
        norm_conv,
        conv_in_t,
        conv_kernel,
        conv_out,
        norm_mlp_one,
        gate_up_one_t,
        down_one,
        norm_attn,
        where,
    )
    (
        active_two,
        grad_gate_two,
        grad_up_two,
        norm_two_t,
        three_own,
        *kept,
        attended_b,
        attended_t,
        log_total,
    ) = attention_forward(
        normed_attn_b,
        query_weight,
        kv_flat,
        query_gain,
        key_gain,
        attn_out,
        two_own,
        norm_mlp_two,
        tables,
        where,
        gate_up_two_t,
        down_two,
        grad_b,
    )
    kept = (*kept, attended_t, log_total)
    (
        grad_three_t,
        grad_query,
        grad_kv,
        grad_two_b,
        grad_two_t,
        grad_two,
        grad_norm_mlp_two,
        grad_norm_attn,
        part_query_gain,
        part_key_gain,
        sum_down_two,
        sum_gate_up_two,
        output,
    ) = attention_backward(
        grad_b_t,
        norm_two_t,
        active_two,
        grad_gate_two,
        grad_up_two,
        gate_up_two_t,
        down_two,
        three_own,
        norm_mlp_two,
        incoming,
        kept,
        attn_out,
        query_weight,
        kv_flat,
        query_gain,
        key_gain,
        two_own,
        norm_attn,
        tables,
        where,
        devices,
    )

    small = jnp.concatenate(
        [
            jnp.zeros((2, width), F32),
            grad_norm_attn,
            grad_norm_mlp_two,
            jnp.pad(
                jnp.concatenate([part_query_gain[:, 0], part_key_gain[:, 0]]), (0, width - 2 * HEAD)
            ).reshape(1, width),
            jnp.zeros((KW, width), F32),
        ],
        axis=0,
    )
    (
        grad_inputs,
        small,
        sum_attn_out,
        sum_query,
        sum_kv,
        sum_down_one,
        sum_gate_up_one,
        sum_conv_out,
        sum_conv_in,
    ) = first_backward(
        [grad_three_t, normed_attn_t, grad_two_t, norm_one_t, normed_conv_t],
        [attended_b, grad_query, grad_kv, active_one, gated_b],
        grad_two_b,
        down_one,
        gate_up_one_t,
        gate_one,
        up_one,
        one_own,
        norm_mlp_one,
        grad_two,
        conv_out,
        conv_in_t,
        projected,
        rim,
        conv_kernel,
        inputs_own,
        norm_conv,
        small,
        devices,
    )
    grad_inputs = grad_inputs.astype(F32)

    out_rows = width // devices
    return (
        output,
        grad_inputs,
        small[0],
        jnp.transpose(sum_conv_in, (1, 0, 2)),
        small[5:, : conv_out.shape[0]],
        sum_conv_out.T,
        small[1],
        sum_gate_up_one,
        sum_down_one.T,
        small[2],
        sum_query,
        sum_kv.reshape(out_rows, 2, local_kv * HEAD),
        small[4, :HEAD],
        small[4, HEAD : 2 * HEAD],
        sum_attn_out.T,
        small[3],
        sum_gate_up_two,
        sum_down_two.T,
    )


def solution(mesh):
    in_specs = (
        P("dp", None),
        P(),
        P(),
        P(None, None, "tensor"),
        P(None, "tensor"),
        P("tensor", None),
        P(),
        P(None, None, "tensor"),
        P("tensor", None),
        P(),
        P(None, "tensor"),
        P(None, None, "tensor"),
        P(),
        P(),
        P("tensor", None),
        P(),
        P(None, None, "tensor"),
        P("tensor", None),
        P("dp", None),
    )
    out_specs = (
        P("dp", None),
        P("dp", None),
        P(),
        P("dp", None, "tensor"),
        P(None, "tensor"),
        P("tensor", "dp"),
        P(),
        P("dp", None, "tensor"),
        P("tensor", "dp"),
        P(),
        P("dp", "tensor"),
        P("dp", None, "tensor"),
        P(),
        P(),
        P("tensor", "dp"),
        P(),
        P("dp", None, "tensor"),
        P("tensor", "dp"),
    )
    return jax.shard_map(local, mesh=mesh, in_specs=in_specs, out_specs=out_specs, check_vma=False)
```

```python
import jax
import jax.numpy as jnp
from jax import lax
from jax.experimental import pallas as pl
from jax.experimental.pallas import tpu as pltpu
from jax.sharding import PartitionSpec as P

HEAD = 64
KW = 3
SPAN = 4
GROUP = 3


EPSILON = 1e-05
THETA = 1000000.0
BF16 = jnp.bfloat16
F32 = jnp.float32


def matmul(left, right):
    return jnp.dot(left, right, preferred_element_type=F32)


def inner_back(left, right):
    return lax.dot_general(left, right, (((1,), (1,)), ((), ())), preferred_element_type=F32)


def normalize(values, gain):
    inverse = lax.rsqrt(jnp.mean(values * values, axis=-1, keepdims=True) + EPSILON)
    return (values * inverse * gain, inverse)


def normalize_back(values, inverse, gain, grad_result):
    weighted = grad_result * gain
    grad_gain = jnp.sum(grad_result * values * inverse, axis=tuple(range(values.ndim - 1)))
    inner = jnp.mean(weighted * values, axis=-1, keepdims=True)
    grad_values = inverse * (weighted - values * inverse * inverse * inner)
    return (grad_values, grad_gain)


CHUNKS = 4
SLOTS = 3
MESH = pl.DeviceIdType.MESH


class Lazy:
    def __init__(self, value, dtype=None):
        self.value, self.dtype = value, dtype


class Refs:
    def __init__(self, names, refs):
        self.__dict__.update(zip(names, refs))

    def begin(self, inputs, outputs, refs):
        self.arriving, self.leaving, self.homes = {}, [], {}
        for at, name in enumerate(inputs):
            ref = self.__dict__[name]
            copy = pltpu.make_async_copy(refs[at], ref, self.lazy_in.at[at])
            copy.start()
            self.arriving[id(ref)] = copy
        for at, name in enumerate(outputs):
            self.homes[id(self.__dict__[name])] = (refs[len(inputs) + at], at)

    def need(self, *refs):
        for ref in refs:
            self.arriving.pop(id(ref)).wait()

    def flush(self, *refs):
        for ref in refs:
            home, at = self.homes.pop(id(ref))
            copy = pltpu.make_async_copy(ref, home, self.lazy_out.at[at, 0])
            copy.start()
            self.leaving.append(copy)

    def flush_blocks(self, ref, owners):
        home, at = self.homes.pop(id(ref))
        rows = ref.shape[0] // 4
        for block, owner in enumerate(owners):
            copy = pltpu.make_async_copy(
                ref.at[pl.ds(block * rows, rows)],
                home.at[pl.ds(pl.multiple_of(owner * rows, rows), rows)],
                self.lazy_out.at[at, block],
            )
            copy.start()
            self.leaving.append(copy)

    def end(self):
        assert not self.homes
        for copy in list(self.arriving.values()) + self.leaving:
            copy.wait()


def run_kernel(body, inputs, outputs, scratch, collective_id, limit, flops):
    arrays, specs, names, out_names = [], [], [], []
    scratch = dict(scratch)
    lazy_in = [name for name, value in inputs.items() if isinstance(value, Lazy)]
    lazy_out = [name for name, value in outputs.items() if isinstance(value, Lazy)]
    for name, value in inputs.items():
        if isinstance(value, Lazy):
            array, space = value.value, pl.ANY
            scratch[name] = pltpu.VMEM(array.shape, array.dtype)
            names.append(None)
        else:
            array, space = value if isinstance(value, tuple) else (value, pltpu.VMEM)
            names.append(name)
        arrays.append(array)
        specs.append(pl.BlockSpec(memory_space=space))
    shapes, out_specs = [], []
    for name, value in outputs.items():
        if isinstance(value, Lazy):
            shape, dtype, space = value.value, value.dtype, pl.ANY
            scratch[name] = pltpu.VMEM(shape, dtype)
            names.append(None)
        else:
            shape, dtype, space = value if len(value) == 3 else (*value, pltpu.VMEM)
            names.append(name)
        shapes.append(jax.ShapeDtypeStruct(shape, dtype))
        out_specs.append(pl.BlockSpec(memory_space=space))
    scratch["lazy_in"] = pltpu.SemaphoreType.DMA((max(len(lazy_in), 1),))
    scratch["lazy_out"] = pltpu.SemaphoreType.DMA((max(len(lazy_out), 1), 4))
    names += list(scratch)

    def whole(*refs):
        r = Refs([n for n in names if n], [ref for n, ref in zip(names, refs) if n])
        r.begin(lazy_in, lazy_out, [ref for n, ref in zip(names, refs) if not n])
        body(r)
        r.end()

    return pl.pallas_call(
        whole,
        in_specs=specs,
        out_specs=out_specs,
        out_shape=shapes,
        scratch_shapes=list(scratch.values()),
        compiler_params=pltpu.CompilerParams(
            collective_id=collective_id, has_side_effects=True, vmem_limit_bytes=limit * 2**20
        ),
        cost_estimate=pl.CostEstimate(
            flops=flops,
            bytes_accessed=sum(a.size * a.dtype.itemsize for a in arrays),
            transcendentals=0,
        ),
    )(*arrays)


def greet(peers):
    barrier = pltpu.get_barrier_semaphore()
    for peer in peers:
        pl.semaphore_signal(barrier, inc=1, device_id=peer, device_id_type=MESH)
    pl.semaphore_wait(barrier, len(peers))


def tensor_peers():
    me = lax.axis_index("tensor")
    return [dict(tensor=me ^ 1), dict(tensor=me ^ 2)]


def span_peers():
    me = lax.axis_index("dp")
    place = lax.rem(me, SPAN)
    return [dict(dp=me - place + lax.rem(place + k, SPAN)) for k in range(1, SPAN)]


def remote(src, dst, send, recv, peer):
    return pltpu.make_async_remote_copy(
        src_ref=src, dst_ref=dst, send_sem=send, recv_sem=recv, device_id=peer, device_id_type=MESH
    )


def exchange_scratch(rows, width):
    quarter = rows // 4
    return dict(
        near_rows=pltpu.VMEM((2 * quarter, width), BF16),
        across_rows=pltpu.VMEM((quarter, width), BF16),
        far_rows=pltpu.VMEM((quarter, width), BF16),
        x_send=pltpu.SemaphoreType.DMA((6 * CHUNKS,)),
        x_recv=pltpu.SemaphoreType.DMA((6 * CHUNKS,)),
    )


def sum_and_gather(r, partial, gathered, gathered_t, compute):
    near, across, far = r.near_rows, r.across_rows, r.far_rows
    core, other = tensor_peers()
    quarter = partial.shape[0] // 4
    size = quarter // CHUNKS
    copies = {}

    def copy(kind, at, src, dst, peer):
        number = kind * CHUNKS + at
        copies[kind, at] = remote(src, dst, r.x_send.at[number], r.x_recv.at[number], peer)
        copies[kind, at].start()

    def part(block, at):
        return pl.ds(block * quarter + at * size, size)

    def turn(block):
        if gathered_t is not None:
            rows = slice(block * quarter, (block + 1) * quarter)
            gathered_t[:, rows] = gathered[rows, :].T

    for at in range(CHUNKS):
        copy(0, at, partial.at[part(3, at)], near.at[part(1, at)], core)
    for at in range(CHUNKS):
        copy(1, at, partial.at[part(2, at)], near.at[part(0, at)], core)
    for at in range(CHUNKS):
        copies[0, at].wait_recv()
        far[part(0, at), :] = (
            partial[part(1, at), :].astype(F32) + near[part(1, at), :].astype(F32)
        ).astype(BF16)
        copy(2, at, far.at[part(0, at)], across.at[part(0, at)], other)
    yield 1
    for at in range(CHUNKS):
        copies[1, at].wait_recv()
        copies[2, at].wait_recv()
        total = (
            partial[part(0, at), :].astype(F32)
            + near[part(0, at), :].astype(F32)
            + across[part(0, at), :].astype(F32)
        )
        gathered[part(0, at), :] = compute(total, part(0, at), at == 0)
        copy(3, at, gathered.at[part(0, at)], gathered.at[part(1, at)], other)
        copy(4, at, gathered.at[part(0, at)], gathered.at[part(2, at)], core)
    turn(0)
    yield 1
    for at in range(CHUNKS):
        copies[3, at].wait_recv()
        copy(5, at, gathered.at[part(1, at)], gathered.at[part(3, at)], core)
    turn(1)
    for at in range(CHUNKS):
        copies[4, at].wait_recv()
    turn(2)
    for at in range(CHUNKS):
        copies[5, at].wait_recv()
    turn(3)
    for made in copies.values():
        made.wait_send()
    yield 1


def exhaust(main):
    for _ in main:
        pass


def norm_rows(total, rows, residual, gain, hidden):
    values = residual[rows, :] + total
    hidden[rows, :] = values
    return normalize(values, gain)[0].astype(BF16)


def back_rows(total, rows, first, hidden, gain, incoming, own, grad_gain):
    values = hidden[rows, :]
    inverse = lax.rsqrt(jnp.mean(values * values, axis=-1, keepdims=True) + EPSILON)
    made, term = normalize_back(values, inverse, gain, total)
    made = made + incoming[rows, :]
    if own is not None:
        own[rows, :] = made
    term = term.reshape(1, -1)
    grad_gain[...] = term if first else grad_gain[...] + term
    return made.astype(BF16)


def ring_peers(count):
    me = lax.axis_index("dp")
    even = lax.rem(me, 2) == 0
    place = jnp.where(even, me // 2, count - 1 - me // 2)

    def at(position):
        position = lax.rem(position + count, count)
        return jnp.where(position < count // 2, 2 * position, 2 * (count - 1 - position) + 1)

    return at(place + 1), at(place - 1), lambda distance: at(place + distance)


class Rings:
    def __init__(self, devices, sides, segments, held, send, recv, credit, store):
        self.devices, self.sides, self.segments, self.held = devices, sides, segments, held
        self.send, self.recv, self.credit, self.store = send, recv, credit, store
        self.rows = segments[0][0][0].shape[0] // devices
        self.half = self.rows // sides
        self.steps = devices - 1
        self.following, self.previous, self.owner_at = ring_peers(devices)

    def peers(self):
        return [dict(dp=self.following), dict(dp=self.previous)]

    def copy(self, seg, side, step):
        number = (seg * self.sides + side) * self.steps + step
        return remote(
            self.held[seg].at[side, step % SLOTS],
            self.held[seg].at[side, (step + 1) % SLOTS],
            self.send.at[number],
            self.recv.at[number],
            dict(dp=self.following if side == 0 else self.previous),
        )

    def unit(self, seg, step):
        sides, half, steps = self.sides, self.half, self.steps
        last = step == steps
        slot = step % SLOTS
        starts = []
        for side in range(sides):
            if last:
                owner = lax.axis_index("dp")
            else:
                owner = self.owner_at(-1 - step if side == 0 else 1 + step)
            starts.append(pl.multiple_of(owner * self.rows + side * half, 16))
        if step:
            for side in range(sides):
                self.copy(seg, side, step - 1).wait_send()
                if step <= steps + 1 - SLOTS:
                    pl.semaphore_signal(
                        self.credit.at[seg * sides + side],
                        inc=1,
                        device_id=dict(dp=self.previous if side == 0 else self.following),
                        device_id_type=MESH,
                    )
                self.copy(seg, side, step - 1).wait_recv()
        column = 0
        for left, right in self.segments[seg]:
            pieces = [left[pl.ds(start, half), :] for start in starts]
            piece = pieces[0] if sides == 1 else jnp.concatenate(pieces, axis=0)
            made = jnp.dot(piece, right[...], preferred_element_type=F32)
            at = slice(column, column + made.shape[1])
            values = []
            for side in range(sides):
                value = made[side * half : (side + 1) * half]
                if step:
                    value = value + self.held[seg][side, slot, :, at].astype(F32)
                if last:
                    values.append(value)
                else:
                    self.held[seg][side, slot, :, at] = value.astype(BF16)
            if last:
                self.store(seg, column, values[0] if sides == 1 else jnp.concatenate(values, axis=0))
            column += made.shape[1]
        if not last:
            for side in range(sides):
                if step >= SLOTS - 1:
                    pl.semaphore_wait(self.credit.at[seg * sides + side], 1)
                self.copy(seg, side, step).start()


def ring_scratch(devices, sides, rows, widths):
    copies = len(widths) * sides * (devices - 1)
    made = {
        f"held{at}": pltpu.VMEM((sides, SLOTS, rows // sides, w), BF16)
        for at, w in enumerate(widths)
    }
    made["r_send"] = pltpu.SemaphoreType.DMA((copies,))
    made["r_recv"] = pltpu.SemaphoreType.DMA((copies,))
    made["r_credit"] = pltpu.SemaphoreType.REGULAR((len(widths) * sides,))
    return made


def interleave(main, units, first):
    units = iter(units)

    def some(number):
        for _ in range(number):
            unit = next(units, None)
            if unit is not None:
                unit()

    some(first)
    for number in main:
        some(number)
    for unit in units:
        unit()


def piece_sides(width, devices):
    return 2 if width // devices % 32 == 0 else 1


def block_owners(index):
    return [index, index ^ 2, index ^ 1, index ^ 3]


def cross(left, right):
    return lax.dot_general(left, right, (((1,), (1,)), ((), ())), preferred_element_type=F32)


def turn_t(values, cosine, sine, back):
    middle = HEAD // 2
    low, high = values[:middle], values[middle:]
    if back:
        return jnp.concatenate([low * cosine + high * sine, high * cosine - low * sine], axis=0)
    return jnp.concatenate([low * cosine - high * sine, high * cosine + low * sine], axis=0)


def head_norm_t(values, gain):
    inverse = lax.rsqrt(jnp.mean(values * values, axis=0, keepdims=True) + EPSILON)
    return values * inverse * gain


def head_back_t(values, gain, grad):
    inverse = lax.rsqrt(jnp.mean(values * values, axis=0, keepdims=True) + EPSILON)
    weighted = grad * gain
    inner = jnp.mean(weighted * values, axis=0, keepdims=True)
    return inverse * (weighted - values * inverse * inverse * inner), grad * values * inverse


def block_positions(block, quarter, shape, axis):
    place = lax.rem(lax.axis_index("dp"), SPAN)
    owner = block_owners(lax.axis_index("tensor"))[block]
    start = (place * 4 + owner) * quarter
    return start + lax.broadcasted_iota(jnp.int32, shape, axis)


def own_length(r):
    return r.lengths[lax.axis_index("dp") // SPAN]


def fill_bias(r):
    quarter = r.bias.shape[0] // 4
    shape = (quarter, quarter)
    for row in range(4):
        keys = block_positions(row, quarter, shape, 0)
        live = keys < own_length(r)
        for column in range(4):
            allowed = live & (keys <= block_positions(column, quarter, shape, 1))
            at = slice(row * quarter, (row + 1) * quarter)
            r.bias[at, column * quarter : (column + 1) * quarter] = jnp.where(allowed, 0.0, -1e30)


def head_rows(head):
    return slice(head * HEAD, (head + 1) * HEAD)


def attention_forward(
    normed_b, query_weight, kv_weight, head_gains, attn_out, residual, tables, gains, lengths,
    gate_up_t, down, grad_b,
):
    rows, width = normed_b.shape
    columns = query_weight.shape[1]
    kv_columns = kv_weight.shape[1] // 2
    heads, kv_heads = columns // HEAD, kv_columns // HEAD
    units = down.shape[0]

    def body(r):
        me = lax.axis_index("dp")
        place = lax.rem(me, SPAN)
        greet(tensor_peers() + span_peers())
        for copy in hidden_fetch(r, 0, TILE):
            copy.start()

        def pass_on(distance):
            return remote(
                r.own, r.near.at[distance - 1], r.p_send.at[distance - 1], r.p_recv.at[distance - 1],
                dict(dp=me + distance),
            )

        r.need(r.normed, r.kv_weight, r.cosine, r.sine)
        cosine, sine = r.cosine[...], r.sine[...]
        made = jnp.dot(r.normed[...], r.kv_weight[...], preferred_element_type=F32)
        r.key_raw[...] = made[:, :kv_columns].T
        r.own[:, kv_columns:] = made[:, kv_columns:].astype(BF16)
        for group in range(kv_heads):
            keys = head_norm_t(r.key_raw[head_rows(group), :], r.head_gains[:, 1:2])
            r.keys_t[head_rows(group), :] = turn_t(keys, cosine, sine, False).astype(BF16)
        r.own[:, :kv_columns] = r.keys_t[...].T
        for distance in range(1, SPAN):

            @pl.when(place + distance < SPAN)
            def _():
                pass_on(distance).start()

        r.need(r.query_weight)
        made = jnp.dot(r.normed[...], r.query_weight[...], preferred_element_type=F32)
        r.query_raw[...] = made.T
        for head in range(heads):
            query = head_norm_t(r.query_raw[head_rows(head), :], r.head_gains[:, 0:1])
            query = turn_t(query, cosine, sine, False).astype(BF16)
            r.query[head_rows(head), :] = query * jnp.asarray(HEAD ** (-0.5), BF16)
        fill_bias(r)

        def part(piece, first):
            for group in range(kv_heads):
                keys = piece[:, head_rows(group)]
                values_t = piece[:, kv_columns + group * HEAD : kv_columns + (group + 1) * HEAD].T
                for head in range(group * GROUP, (group + 1) * GROUP):
                    at = head_rows(head)
                    scores = jnp.dot(keys, r.query[at, :], preferred_element_type=F32)
                    if first:
                        scores = scores + r.bias[...]
                    expo = jnp.exp(scores)
                    total = jnp.sum(expo, axis=0, keepdims=True)
                    made = jnp.dot(values_t, expo.astype(BF16), preferred_element_type=F32)
                    if first:
                        r.total[head : head + 1, :] = total
                        r.attended_t[at, :] = made
                    else:
                        r.total[head : head + 1, :] += total
                        r.attended_t[at, :] += made

        part(r.own[...], True)

        @pl.loop(1, place + 1)
        def _(distance):
            pass_on(distance).wait_recv()
            part(r.near[distance - 1], False)

        for head in range(heads):
            at = head_rows(head)
            made = r.attended_t[at, :] / r.total[head : head + 1, :]
            r.attended_t[at, :] = made
            r.attended[:, at] = made.T.astype(BF16)
        r.log_total[...] = jnp.log(r.total[...])
        r.need(r.attn_out, r.residual, r.grad_b)
        r.flush(r.query_raw, r.key_raw, r.query, r.own, r.near, r.attended, r.attended_t, r.log_total)
        r.partial[...] = jnp.dot(
            r.attended[...], r.attn_out[...], preferred_element_type=F32
        ).astype(BF16)
        exhaust(
            sum_and_gather(
                r, r.partial, r.gathered, r.gathered_t,
                lambda total, at, first: norm_rows(total, at, r.residual, r.gains[3:4, :], r.hidden),
            )
        )
        r.flush(r.gathered_t, r.hidden)
        for distance in range(1, SPAN):

            @pl.when(place + distance < SPAN)
            def _():
                pass_on(distance).wait_send()

        def tile(number, wide, gate_w, up_w, down_w):
            lanes = tile_lanes(number, wide)
            a = cross(r.gathered[...], gate_w)
            z = cross(r.gathered[...], up_w)
            grad = cross(r.grad_b[...], down_w)
            sigma = jax.nn.sigmoid(a)
            r.active[:, lanes] = (a * sigma * z).astype(BF16)
            grad_gate = (grad * z * sigma * (1.0 + a * (1.0 - sigma))).astype(BF16)
            grad_up = (grad * a * sigma).astype(BF16)
            put_joined(r.joined, number, TILE, (grad_gate, grad_up), units)

        hidden_tiles(r, units, tile)
        r.flush(r.active, r.joined)

    return run_kernel(
        body,
        dict(
            normed=Lazy(normed_b),
            query_weight=Lazy(query_weight),
            kv_weight=Lazy(kv_weight),
            head_gains=head_gains,
            attn_out=Lazy(attn_out),
            residual=Lazy(residual),
            cosine=Lazy(tables[0]),
            sine=Lazy(tables[1]),
            gate_up_t=(gate_up_t, pl.ANY),
            down=(down, pl.ANY),
            grad_b=Lazy(grad_b),
            lengths=(lengths, pltpu.SMEM),
            gains=gains,
        ),
        dict(
            active=Lazy((rows, units), BF16),
            joined=Lazy((rows, 2 * units), BF16),
            gathered_t=Lazy((width, rows), BF16),
            hidden=Lazy(residual.shape, F32),
            query_raw=Lazy((columns, rows), F32),
            key_raw=Lazy((kv_columns, rows), F32),
            query=Lazy((columns, rows), BF16),
            own=Lazy((rows, 2 * kv_columns), BF16),
            near=Lazy((SPAN - 1, rows, 2 * kv_columns), BF16),
            attended=Lazy((rows, columns), BF16),
            attended_t=Lazy((columns, rows), F32),
            log_total=Lazy((heads, rows), F32),
        ),
        dict(
            keys_t=pltpu.VMEM((kv_columns, rows), BF16),
            bias=pltpu.VMEM((rows, rows), F32),
            total=pltpu.VMEM((heads, rows), F32),
            partial=pltpu.VMEM((rows, width), BF16),
            gathered=pltpu.VMEM((rows, width), BF16),
            **hidden_scratch(width),
            p_send=pltpu.SemaphoreType.DMA((SPAN - 1,)),
            p_recv=pltpu.SemaphoreType.DMA((SPAN - 1,)),
            **exchange_scratch(rows, width),
        ),
        2,
        58,
        16 * rows * rows * SPAN * columns,
    )


def stream_product(r, left, weights, parts, out):
    width = weights.shape[2]
    size = r.tile.shape[2]
    tiles = width // size
    depth = sum(part[3] for part in parts)

    def fetch(j):
        return [
            pltpu.make_async_copy(
                weights.at[which, pl.ds(there, count), pl.ds(j * size, size)],
                r.tile.at[j % 2, pl.ds(here, count), :],
                r.tile_sem.at[j % 2, k],
            )
            for k, (which, there, here, count) in enumerate(parts)
        ]

    for copy in fetch(0):
        copy.start()
    for j in range(tiles):
        if j + 1 < tiles:
            for copy in fetch(j + 1):
                copy.start()
        for copy in fetch(j):
            copy.wait()
        made = jnp.dot(left[...], r.tile[j % 2, 0:depth, :], preferred_element_type=F32)
        out[:, j * size : (j + 1) * size] = made.astype(BF16)
        if j % 2:
            yield 1


def stream_scratch(depth, size):
    return dict(
        tile=pltpu.VMEM((2, depth, size), BF16),
        tile_sem=pltpu.SemaphoreType.DMA((2, 4)),
    )


def attention_backward(
    grad_b_t, norm_two_t, active, joined, gate_up_t, down, three, incoming,
    kept, attn_out, query_weight, kv_weight, head_gains, two, tables, gains, lengths, devices,
):
    units, tokens_width = gate_up_t.shape[1:]
    query_raw, key_raw, query, own, near, attended_t, log_total = kept
    rows, width = active.shape[0], tokens_width
    columns = query_weight.shape[1]
    kv_columns = kv_weight.shape[1] // 2
    heads, kv_heads = columns // HEAD, kv_columns // HEAD
    sides = piece_sides(width, devices)
    block = width // devices
    segment_widths = [units] + joined_widths(units)

    def body(r):
        me = lax.axis_index("dp")
        place = lax.rem(me, SPAN)

        def store(seg, column, value):
            if seg == 0:
                r.sum_down[...] = value
                r.flush(r.sum_down)
            else:
                store_joined(r.sum_gate_up, seg - 1, value, units)
                if seg == 2:
                    r.flush(r.sum_gate_up)

        rings = Rings(
            devices, sides,
            [[(r.grad_b_t, r.active)]] + joined_segments(r.norm_two_t, r.joined, units),
            [r.held0, r.held1, r.held2], r.r_send, r.r_recv, r.r_credit, store,
        )
        greet(rings.peers() + tensor_peers() + span_peers())

        def pass_back(distance):
            return remote(
                r.far.at[distance - 1], r.arrived.at[distance - 1],
                r.p_send.at[distance - 1], r.p_recv.at[distance - 1], dict(dp=me - distance),
            )

        def part(piece, write, masked):
            for group in range(kv_heads):
                keys = piece[:, head_rows(group)]
                value_at = slice(kv_columns + group * HEAD, kv_columns + (group + 1) * HEAD)
                values = piece[:, value_at]
                keys_t = keys.T
                grad_k = grad_v = None
                for head in range(group * GROUP, (group + 1) * GROUP):
                    at = head_rows(head)
                    q, grads = r.query[at, :], r.grads[:, at]
                    scores = jnp.dot(keys, q, preferred_element_type=F32)
                    scores = scores - r.log_total[head : head + 1, :]
                    if masked:
                        scores = scores + r.bias[...]
                    probs = jnp.exp(scores)
                    made = jnp.dot(probs.astype(BF16), grads, preferred_element_type=F32)
                    grad_v = made if grad_v is None else grad_v + made
                    grad_probs = cross(values, grads)
                    grad_scores = (probs * (grad_probs - r.delta[head : head + 1, :])).astype(BF16)
                    made = cross(grad_scores, q)
                    grad_k = made if grad_k is None else grad_k + made
                    made = jnp.dot(keys_t, grad_scores, preferred_element_type=F32)
                    if masked:
                        r.grad_q_t[at, :] = made
                    else:
                        r.grad_q_t[at, :] += made
                write(head_rows(group), grad_k)
                write(value_at, grad_v)

        def main():
            yield from stream_product(r, r.joined, r.gate_up_t, joined_parts(units), r.partial)
            fill_bias(r)
            r.need(r.three, r.incoming)
            yield from sum_and_gather(
                r, r.partial, r.gathered, r.grad_three_t,
                lambda total, at, first: back_rows(
                    total, at, first, r.three, r.gains[3:4, :], r.incoming, r.grad_three, r.gain_term
                ),
            )
            r.flush(r.grad_three_t)
            r.small[...] = jnp.zeros_like(r.small)
            r.small[3:4, :] = r.gain_term[...]
            r.need(r.attn_out, r.attended_t, r.own, r.near, r.query, r.log_total)
            r.grads[...] = cross(r.gathered[...], r.attn_out[...]).astype(BF16)
            for head in range(heads):
                at = head_rows(head)
                grads_t = r.grads[:, at].astype(F32).T
                r.delta[head : head + 1, :] = jnp.sum(
                    grads_t * r.attended_t[at, :], axis=0, keepdims=True
                )
            yield 1

            def write_own(at, value):
                r.grad_own[:, at] = value

            part(r.own[...], write_own, True)
            yield 1

            @pl.loop(1, place + 1)
            def _(distance):
                def write_far(at, value):
                    r.far[distance - 1, :, at] = value.astype(BF16)

                part(r.near[distance - 1], write_far, False)
                pass_back(distance).start()

            yield 2
            r.need(r.cosine, r.sine, r.query_raw, r.key_raw, r.query_weight, r.kv_weight, r.two)
            cosine, sine = r.cosine[...], r.sine[...]
            terms = None
            for head in range(heads):
                at = head_rows(head)
                grad = turn_t(r.grad_q_t[at, :] * HEAD ** (-0.5), cosine, sine, True)
                made, term = head_back_t(r.query_raw[at, :], r.head_gains[:, 0:1], grad)
                terms = term if terms is None else terms + term
                r.grad_query[:, at] = made.T.astype(BF16)
            r.small[4:5, 0:HEAD] = jnp.sum(terms.T, axis=0, keepdims=True)
            yield 1
            for distance in range(1, SPAN):

                @pl.when(place + distance < SPAN)
                def _():
                    pass_back(distance).wait_recv()
                    r.grad_own[...] += r.arrived[distance - 1].astype(F32)

            terms = None
            for group in range(kv_heads):
                at = head_rows(group)
                grad = turn_t(r.grad_own[:, at].T, cosine, sine, True)
                made, term = head_back_t(r.key_raw[at, :], r.head_gains[:, 1:2], grad)
                terms = term if terms is None else terms + term
                r.grad_kv[:, at] = made.T.astype(BF16)
            r.small[4:5, HEAD : 2 * HEAD] = jnp.sum(terms.T, axis=0, keepdims=True)
            r.grad_kv[:, kv_columns:] = r.grad_own[:, kv_columns:].astype(BF16)
            r.flush(r.grad_query, r.grad_kv)
            r.partial[...] = (
                cross(r.grad_query[...], r.query_weight[...]) + cross(r.grad_kv[...], r.kv_weight[...])
            ).astype(BF16)
            yield 1
            yield from sum_and_gather(
                r, r.partial, r.grad_two_b, r.grad_two_t,
                lambda total, at, first: back_rows(
                    total, at, first, r.two, r.gains[2:3, :], r.grad_three, r.grad_two, r.gain_term
                ),
            )
            r.small[2:3, :] = r.gain_term[...]
            r.flush(r.grad_two_b, r.grad_two_t, r.grad_two, r.small)
            for distance in range(1, SPAN):

                @pl.when(place >= distance)
                def _():
                    pass_back(distance).wait_send()

            yield from stream_product(r, r.active, r.down, [(0, 0, 0, units)], r.partial)
            yield from sum_and_gather(
                r, r.partial, r.output, None,
                lambda total, at, first: (r.three[at, :] + total).astype(BF16),
            )
            r.flush_blocks(r.output, block_owners(lax.axis_index("tensor")))

        def first(seg):
            r.need(*((r.grad_b_t, r.active), (r.norm_two_t, r.joined), ())[seg])
            rings.unit(seg, 0)

        order = [(seg, step) for step in range(1, devices) for seg in range(3)]
        units_left = [lambda s=seg: first(s) for seg in range(3)]
        units_left += [lambda u=u: rings.unit(*u) for u in order]
        interleave(main(), units_left, 3)

    quarter = rows // 4
    return run_kernel(
        body,
        dict(
            grad_b_t=Lazy(grad_b_t),
            active=Lazy(active),
            norm_two_t=Lazy(norm_two_t),
            joined=Lazy(joined),
            gate_up_t=(gate_up_t, pl.ANY),
            down=(down.reshape((1,) + down.shape), pl.ANY),
            three=Lazy(three),
            incoming=Lazy(incoming),
            query_raw=Lazy(query_raw),
            key_raw=Lazy(key_raw),
            query=Lazy(query),
            own=Lazy(own),
            near=Lazy(near),
            attended_t=Lazy(attended_t),
            log_total=Lazy(log_total),
            attn_out=Lazy(attn_out),
            query_weight=Lazy(query_weight),
            kv_weight=Lazy(kv_weight),
            head_gains=head_gains,
            two=Lazy(two),
            cosine=Lazy(tables[0]),
            sine=Lazy(tables[1]),
            lengths=(lengths, pltpu.SMEM),
            gains=gains,
        ),
        dict(
            grad_three_t=Lazy((width, rows), BF16),
            grad_query=Lazy((rows, columns), BF16),
            grad_kv=Lazy((rows, 2 * kv_columns), BF16),
            grad_two_b=Lazy((rows, width), BF16),
            grad_two_t=Lazy((width, rows), BF16),
            grad_two=Lazy((quarter, width), F32),
            small=Lazy((8, width), F32),
            sum_down=Lazy((block, units), F32),
            sum_gate_up=Lazy((block, 2, units), F32),
            output=Lazy((rows, width), BF16),
        ),
        dict(
            partial=pltpu.VMEM((rows, width), BF16),
            gathered=pltpu.VMEM((rows, width), BF16),
            grad_three=pltpu.VMEM((quarter, width), F32),
            grads=pltpu.VMEM((rows, columns), BF16),
            gain_term=pltpu.VMEM((1, width), F32),
            delta=pltpu.VMEM((heads, rows), F32),
            bias=pltpu.VMEM((rows, rows), F32),
            grad_q_t=pltpu.VMEM((columns, rows), F32),
            grad_own=pltpu.VMEM((rows, 2 * kv_columns), F32),
            far=pltpu.VMEM((SPAN - 1, rows, 2 * kv_columns), BF16),
            arrived=pltpu.VMEM((SPAN - 1, rows, 2 * kv_columns), BF16),
            p_send=pltpu.SemaphoreType.DMA((SPAN - 1,)),
            p_recv=pltpu.SemaphoreType.DMA((SPAN - 1,)),
            **stream_scratch(2 * units, 256),
            **exchange_scratch(rows, width),
            **ring_scratch(devices, sides, block, segment_widths),
        ),
        3 + 2,
        61,
        2 * rows * width * units * 10,
    )


TILE = 512


def unit_tiles(units):
    return [(at, min(TILE, units - at)) for at in range(0, units, TILE)]


def hidden_fetch(r, number, wide):
    slot = lax.rem(number, 2)
    rows = pl.ds(number * TILE, wide)
    pairs = [
        (r.gate_up_t.at[:, rows, :], r.gate_up_tile.at[slot, :, 0:wide, :]),
        (r.down.at[rows, :], r.down_tile.at[slot, 0:wide, :]),
    ]
    return [pltpu.make_async_copy(a, b, r.h_sem.at[slot, k]) for k, (a, b) in enumerate(pairs)]


def hidden_tiles(r, units, tile):
    count = pl.cdiv(units, TILE)
    rest = units - (count - 1) * TILE

    def run(number, wide):
        for copy in hidden_fetch(r, number, wide):
            copy.wait()
        slot = lax.rem(number, 2)
        tile(
            number, wide,
            r.gate_up_tile[slot, 0, 0:wide, :],
            r.gate_up_tile[slot, 1, 0:wide, :],
            r.down_tile[slot, 0:wide, :],
        )

    @pl.loop(0, count - 1)
    def _(number):
        @pl.when(number + 1 < count - 1)
        def _():
            for copy in hidden_fetch(r, number + 1, TILE):
                copy.start()

        @pl.when(number + 1 == count - 1)
        def _():
            for copy in hidden_fetch(r, number + 1, rest):
                copy.start()

        run(number, TILE)

    run(count - 1, rest)


def joined_parts(units):
    main = units // 128 * 128
    rest = units - main
    return [
        (0, 0, 0, main),
        (1, 0, main, main),
        (0, main, 2 * main, rest),
        (1, main, 2 * main + rest, rest),
    ]


def put_joined(ref, number, size, values, units):
    main = units // 128 * 128
    rest = units - main
    wide = values[0].shape[1]
    for which, value in enumerate(values):
        if isinstance(number, int):
            at = number * size
            cut = min(wide, main - at)
            ref[:, which * main + at : which * main + at + cut] = value[:, :cut]
            if cut < wide:
                at = 2 * main + which * rest
                ref[:, at : at + rest] = value[:, cut:]
        else:
            ref[:, pl.ds(pl.multiple_of(which * main + number * size, 128), wide)] = value


def joined_segments(left, joined, units):
    main = units // 128 * 128
    return [
        [(left, joined.at[:, pl.ds(0, main)])],
        [(left, joined.at[:, pl.ds(main, 2 * units - main)])],
    ]


def joined_widths(units):
    main = units // 128 * 128
    return [main, 2 * units - main]


def store_joined(ref, part, value, units):
    main = units // 128 * 128
    rest = units - main
    if part == 0:
        ref[:, 0, 0:main] = value
    else:
        ref[:, 1, 0:main] = value[:, :main]
        ref[:, 0, main:units] = value[:, main : main + rest]
        ref[:, 1, main:units] = value[:, main + rest :]


def tile_lanes(number, wide):
    start = number * TILE
    return pl.ds(start if isinstance(start, int) else pl.multiple_of(start, TILE), wide)


def hidden_scratch(width):
    return dict(
        gate_up_tile=pltpu.VMEM((2, 2, TILE, width), BF16),
        down_tile=pltpu.VMEM((2, TILE, width), BF16),
        h_sem=pltpu.SemaphoreType.DMA((2, 2)),
    )


def first_forward(
    tokens, cotangent, conv_in_t, kernel, conv_out, gate_up_t, down, gains, lengths
):
    rows, width = tokens.shape
    channels = conv_out.shape[0]
    units = down.shape[0]
    quarter = rows // 4
    count = len(unit_tiles(units))

    def body(r):
        me = lax.axis_index("dp")
        index = lax.axis_index("tensor")
        place = lax.rem(me, SPAN)
        greet(tensor_peers() + span_peers())
        for copy in hidden_fetch(r, 0, TILE):
            copy.start()
        r.need(r.tokens)
        for at in range(4):
            part = slice(at * quarter, (at + 1) * quarter)
            values = r.tokens[part, :].astype(F32)
            r.normed[part, :] = normalize(values, r.gains[0:1, :])[0].astype(BF16)
        r.need(r.conv_in_t)
        for at in range(3):
            made = jnp.dot(r.normed[...], r.conv_in_t[at], preferred_element_type=F32)
            r.projected[:, at * channels : (at + 1) * channels] = made
        r.flush(r.projected)
        pad = 8
        r.mixed[0:pad, :] = jnp.zeros((pad, channels), F32)
        r.mixed[pad:, :] = r.projected[:, :channels] * r.projected[:, 2 * channels :]
        r.rim_out[...] = r.mixed[rows : rows + pad, :]
        rim_copy = remote(r.rim_out, r.rim_in, r.m_sem.at[0], r.m_sem.at[1], dict(dp=me + 1))

        @pl.when(place < SPAN - 1)
        def _():
            rim_copy.start()

        start = pl.multiple_of(index * quarter, quarter)
        r.inputs_own[...] = r.tokens[pl.ds(start, quarter), :].astype(F32)
        r.flush(r.inputs_own)

        @pl.when(place > 0)
        def _():
            rim_copy.wait_recv()
            r.mixed[0:pad, :] = r.rim_in[...]

        r.rim[...] = r.mixed[0:pad, :]
        r.flush(r.rim)
        taps = r.kernel[...].astype(F32)
        convolved = None
        for k in range(KW):
            term = taps[k : k + 1, :] * r.mixed[pad - KW + 1 + k : pad - KW + 1 + k + rows, :]
            convolved = term if convolved is None else convolved + term
        r.gated_true[...] = (r.projected[:, channels : 2 * channels] * convolved).astype(BF16)
        for at, owner in enumerate(block_owners(index)):
            start = pl.multiple_of(owner * quarter, quarter)
            r.gated[at * quarter : (at + 1) * quarter, :] = r.gated_true[pl.ds(start, quarter), :]
        r.need(r.conv_out)
        r.partial[...] = jnp.dot(r.gated[...], r.conv_out[...], preferred_element_type=F32).astype(BF16)
        r.flush(r.gated)
        waits = sum_and_gather(
            r, r.partial, r.gathered_one, r.norm_one_t,
            lambda total, at, first: norm_rows(total, at, r.inputs_own, r.gains[1:2, :], r.one),
        )
        next(waits)
        r.need(r.cotangent)
        for at, owner in enumerate(block_owners(index)):
            part = slice(at * quarter, (at + 1) * quarter)
            start = pl.multiple_of(owner * quarter, quarter)
            live = block_positions(at, quarter, (quarter, width), 0) < own_length(r)
            values = jnp.where(live, r.cotangent[pl.ds(start, quarter), :].astype(F32), 0.0)
            if at == 0:
                r.incoming[...] = values
            r.grad_b[part, :] = values.astype(BF16)
        next(waits)
        r.normed_t[...] = r.normed[...].T
        r.grad_b_t[...] = r.grad_b[...].T
        r.flush(r.normed_t, r.grad_b, r.grad_b_t, r.incoming)
        exhaust(waits)
        r.flush(r.one, r.norm_one_t)
        r.total[...] = jnp.zeros_like(r.total)

        def tile(number, wide, gate_w, up_w, down_w):
            a = cross(r.gathered_one[...], gate_w)
            z = cross(r.gathered_one[...], up_w)
            r.gate[number, :, 0:wide] = a
            r.upward[number, :, 0:wide] = z
            s = (a * jax.nn.sigmoid(a) * z).astype(BF16)
            r.active[:, tile_lanes(number, wide)] = s
            r.total[...] += jnp.dot(s, down_w, preferred_element_type=F32)

        hidden_tiles(r, units, tile)
        r.partial[...] = r.total[...].astype(BF16)
        r.flush(r.active, r.gate, r.upward)
        exhaust(
            sum_and_gather(
                r, r.partial, r.gathered, r.normed_attn_t,
                lambda total, at, first: norm_rows(total, at, r.one, r.gains[2:3, :], r.two),
            )
        )
        r.flush(r.gathered, r.normed_attn_t, r.two)

        @pl.when(place < SPAN - 1)
        def _():
            rim_copy.wait_send()

    return run_kernel(
        body,
        dict(
            tokens=Lazy(tokens),
            cotangent=Lazy(cotangent),
            conv_in_t=Lazy(conv_in_t),
            kernel=kernel,
            conv_out=Lazy(conv_out),
            gate_up_t=(gate_up_t, pl.ANY),
            down=(down, pl.ANY),
            lengths=(lengths, pltpu.SMEM),
            gains=gains,
        ),
        dict(
            gathered=Lazy((rows, width), BF16),
            normed_attn_t=Lazy((width, rows), BF16),
            two=Lazy((quarter, width), F32),
            one=Lazy((quarter, width), F32),
            inputs_own=Lazy((quarter, width), F32),
            norm_one_t=Lazy((width, rows), BF16),
            normed_t=Lazy((width, rows), BF16),
            active=Lazy((rows, units), BF16),
            gate=Lazy((count, rows, TILE), F32),
            upward=Lazy((count, rows, TILE), F32),
            gated=Lazy((rows, channels), BF16),
            projected=Lazy((rows, 3 * channels), F32),
            rim=Lazy((8, channels), F32),
            grad_b=Lazy((rows, width), BF16),
            grad_b_t=Lazy((width, rows), BF16),
            incoming=Lazy((quarter, width), F32),
        ),
        dict(
            normed=pltpu.VMEM((rows, width), BF16),
            partial=pltpu.VMEM((rows, width), BF16),
            gathered_one=pltpu.VMEM((rows, width), BF16),
            total=pltpu.VMEM((rows, width), F32),
            gated_true=pltpu.VMEM((rows, channels), BF16),
            mixed=pltpu.VMEM((rows + 8, channels), F32),
            rim_out=pltpu.VMEM((8, channels), F32),
            rim_in=pltpu.VMEM((8, channels), F32),
            m_sem=pltpu.SemaphoreType.DMA((2,)),
            **hidden_scratch(width),
            **exchange_scratch(rows, width),
        ),
        1,
        60,
        6 * rows * width * units,
    )


class Pump:
    def __init__(self, rings, ready):
        self.rings, self.ready = rings, list(ready)
        self.step = [0] * len(rings.segments)
        self.before = None

    def run(self, number):
        for _ in range(number):
            left = [s for s in self.ready if self.step[s] <= self.rings.steps]
            if not left:
                return
            seg = min(left, key=lambda s: (s == self.before, self.step[s], s))
            self.rings.unit(seg, self.step[seg])
            self.step[seg] += 1
            self.before = seg

    def rest(self):
        self.run(len(self.step) * (self.rings.steps + 1))


def first_backward(
    lefts, rights, grad_two_b, down, gate_up_t, gate, upward, one, grad_two, conv_out,
    conv_in_t, projected, rim, kernel, inputs, gains, small, devices,
):
    rows, width = grad_two_b.shape
    units = down.shape[0]
    channels = conv_out.shape[0]
    quarter = rows // 4
    block = width // devices
    sides = piece_sides(width, devices)
    grad_three_t, normed_attn_t, grad_two_t, norm_one_t, normed_conv_t = lefts
    attended, grad_query, grad_kv, active, gated = rights
    columns, kv_columns = grad_query.shape[1], grad_kv.shape[1]
    widths = [channels + columns + kv_columns, units, *joined_widths(units), 4 * channels]
    bits = []
    bit = 1
    while bit < devices:
        bits.append(bit)
        bit *= 2
    stages = 2 + len(bits)
    size = TILE // 2
    tiles = [(at, min(size, units - at)) for at in range(0, units, size)]

    def body(r):
        me = lax.axis_index("dp")
        index = lax.axis_index("tensor")
        place = lax.rem(me, SPAN)

        done = []

        def store(seg, column, value):
            if seg == 0:
                at = (0, channels, channels + columns).index(column)
                if at == 2:
                    r.sum_kv[:, 0, :] = value[:, : kv_columns // 2]
                    r.sum_kv[:, 1, :] = value[:, kv_columns // 2 :]
                else:
                    (r.sum_attn_out, r.sum_query)[at][...] = value
                r.flush((r.sum_attn_out, r.sum_query, r.sum_kv)[at])
            elif seg == 1:
                r.sum_down[...] = value
                r.flush(r.sum_down)
            elif seg < 4:
                store_joined(r.sum_gate_up, seg - 2, value, units)
                done.append(seg)
                if len(done) == 2:
                    r.flush(r.sum_gate_up)
            elif column == 0:
                r.sum_conv_out[...] = value
                r.flush(r.sum_conv_out)
            else:
                for at in range(3):
                    r.sum_conv_in[at] = value[:, at * channels : (at + 1) * channels]
                r.flush(r.sum_conv_in)

        rings = Rings(
            devices, sides,
            [
                [
                    (r.grad_three_t, r.attended),
                    (r.normed_attn_t, r.grad_query),
                    (r.normed_attn_t, r.grad_kv),
                ],
                [(r.grad_two_t, r.active)],
            ]
            + joined_segments(r.norm_one_t, r.joined, units)
            + [[(r.grad_one_t, r.gated), (r.normed_conv_t, r.grad_projected)]],
            [r.held0, r.held1, r.held2, r.held3, r.held4], r.r_send, r.r_recv, r.r_credit, store,
        )
        pump = Pump(rings, [0, 1])
        small_peers = tensor_peers() + [dict(dp=me ^ bit) for bit in bits]
        greet(rings.peers() + small_peers + span_peers())

        def fetch(number):
            at, wide = tiles[number]
            slot = number % 2
            pairs = [
                (r.down.at[at : at + wide, :], r.down_tile.at[slot, 0:wide, :]),
                (r.gate.at[at // TILE, :, pl.ds(at % TILE, size)], r.gate_tile.at[slot]),
                (r.upward.at[at // TILE, :, pl.ds(at % TILE, size)], r.up_tile.at[slot]),
            ]
            return [
                pltpu.make_async_copy(a, b, r.h_sem.at[slot, k]) for k, (a, b) in enumerate(pairs)
            ]

        def fetch_conv(number):
            slot = number % 2
            return [
                pltpu.make_async_copy(
                    r.conv_in_t.at[k, pl.ds(number * size, size), :],
                    r.conv_tile.at[slot, k],
                    r.c_sem.at[slot, k],
                )
                for k in range(3)
            ]

        def main():
            first = pltpu.make_async_copy(r.grad_two_b, r.gathered, r.e_sem)
            first.start()
            for copy in fetch(0):
                copy.start()
            first.wait()
            for number, (at, wide) in enumerate(tiles):
                if number + 1 < len(tiles):
                    for copy in fetch(number + 1):
                        copy.start()
                for copy in fetch(number):
                    copy.wait()
                slot = number % 2
                grad = cross(r.gathered[...], r.down_tile[slot, 0:wide, :])
                gates, ups = r.gate_tile[slot, :, 0:wide], r.up_tile[slot, :, 0:wide]
                sigma = jax.nn.sigmoid(gates)
                grad_gate = (grad * ups * sigma * (1.0 + gates * (1.0 - sigma))).astype(BF16)
                grad_up = (grad * gates * sigma).astype(BF16)
                put_joined(r.joined, number, size, (grad_gate, grad_up), units)
                if number % 3 == 2:
                    yield 1
            r.need(r.norm_one_t, r.one, r.grad_two)
            pump.ready += [2, 3]
            yield 2
            yield from stream_product(r, r.joined, r.gate_up_t, joined_parts(units), r.partial)
            yield from sum_and_gather(
                r, r.partial, r.gathered, r.grad_one_t,
                lambda total, at, first: back_rows(
                    total, at, first, r.one, r.gains[1:2, :], r.grad_two, r.grad_one, r.gain_term
                ),
            )
            r.small_out[...] = r.small[...]
            r.small_out[1:2, :] = r.gain_term[...]

            r.need(r.conv_out, r.projected, r.rim, r.gated, r.normed_conv_t, r.inputs)
            made = cross(r.gathered[...], r.conv_out[...])
            for at, owner in enumerate(block_owners(index)):
                start = pl.multiple_of(owner * quarter, quarter)
                r.grad_gated[pl.ds(start, quarter), :] = made[at * quarter : (at + 1) * quarter]
            before = r.projected[:, :channels]
            signal = r.projected[:, 2 * channels :]
            taps = r.kernel[...].astype(F32)
            pad = 8
            r.mixed[pad:, :] = before * signal
            r.mixed[0:pad, :] = r.rim[...]
            grad_gated = r.grad_gated[...]
            r.grad_conv[0:rows, :] = grad_gated * r.projected[:, channels : 2 * channels]
            r.grad_conv[rows:, :] = jnp.zeros_like(r.grad_conv[rows:, :])
            r.rim_out[...] = r.grad_conv[0:pad, :]
            rim_copy = remote(r.rim_out, r.rim_in, r.m_sem.at[0], r.m_sem.at[1], dict(dp=me - 1))

            @pl.when(place > 0)
            def _():
                rim_copy.start()

            yield 1
            convolved = None
            for k in range(KW):
                shifted = r.mixed[pad - KW + 1 + k : pad - KW + 1 + k + rows, :]
                term = taps[k : k + 1, :] * shifted
                convolved = term if convolved is None else convolved + term
                term = jnp.sum(r.grad_conv[0:rows, :] * shifted, axis=0, keepdims=True)
                r.small_out[5 + k : 6 + k, 0:channels] = term
            r.grad_projected[:, channels : 2 * channels] = (grad_gated * convolved).astype(BF16)

            @pl.when(place < SPAN - 1)
            def _():
                rim_copy.wait_recv()
                r.grad_conv[rows:, :] = r.rim_in[...]

            grad_mixed = None
            for k in range(KW):
                term = taps[k : k + 1, :] * r.grad_conv[KW - 1 - k : KW - 1 - k + rows, :]
                grad_mixed = term if grad_mixed is None else grad_mixed + term
            r.grad_projected[:, :channels] = (grad_mixed * signal).astype(BF16)
            r.grad_projected[:, 2 * channels :] = (grad_mixed * before).astype(BF16)

            @pl.when(place > 0)
            def _():
                rim_copy.wait_send()

            pump.ready += [4]
            yield 2
            for copy in fetch_conv(0):
                copy.start()
            for number in range(width // size):
                if number + 1 < width // size:
                    for copy in fetch_conv(number + 1):
                        copy.start()
                for copy in fetch_conv(number):
                    copy.wait()
                for at, owner in enumerate(block_owners(index)):
                    start = pl.multiple_of(owner * quarter, quarter)
                    made = None
                    for k in range(3):
                        piece = r.grad_projected[
                            pl.ds(start, quarter), k * channels : (k + 1) * channels
                        ]
                        term = cross(piece, r.conv_tile[number % 2, k])
                        made = term if made is None else made + term
                    r.partial[
                        at * quarter : (at + 1) * quarter, number * size : (number + 1) * size
                    ] = made.astype(BF16)
                if number % 2:
                    yield 1
            yield from sum_and_gather(
                r, r.partial, r.input_grad, None,
                lambda total, at, first: back_rows(
                    total, at, first, r.inputs, r.gains[0:1, :], r.grad_one, None, r.gain_term
                ),
            )
            out_copies = []
            small_rows = quarter // 2
            for at in range(8):
                start = pl.multiple_of(block_owners(index)[at // 2] * quarter + at % 2 * small_rows, 8)
                if at >= 2:
                    out_copies[at - 2].wait()
                r.final[at % 2] = r.input_grad[at * small_rows : (at + 1) * small_rows, :].astype(F32)
                out_copies.append(
                    pltpu.make_async_copy(
                        r.final.at[at % 2], r.result.at[pl.ds(start, small_rows), :], r.g_sem.at[at]
                    )
                )
                out_copies[-1].start()
            for copy in out_copies[-2:]:
                copy.wait()
            r.small_out[0:1, :] = r.gain_term[...]
            row = lax.broadcasted_iota(jnp.int32, small.shape, 0)
            for stage in range(stages):
                copy = remote(
                    r.small_out, r.slots.at[stage], r.s_send.at[stage], r.s_recv.at[stage],
                    small_peers[stage],
                )
                copy.start()
                yield 1
                copy.wait()
                if stage < 2:
                    r.small_out[...] += jnp.where(row < 5, r.slots[stage], 0.0)
                else:
                    r.small_out[...] += r.slots[stage]
            r.flush(r.small_out)

        r.need(r.grad_three_t, r.attended, r.normed_attn_t, r.grad_query, r.grad_kv)
        pump.run(1)
        r.need(r.grad_two_t, r.active)
        pump.run(1)
        for number in main():
            pump.run(number)
        pump.rest()

    return run_kernel(
        body,
        dict(
            grad_three_t=Lazy(grad_three_t),
            attended=Lazy(attended),
            normed_attn_t=Lazy(normed_attn_t),
            grad_query=Lazy(grad_query),
            grad_kv=Lazy(grad_kv),
            grad_two_t=Lazy(grad_two_t),
            active=Lazy(active),
            norm_one_t=Lazy(norm_one_t),
            one=Lazy(one),
            grad_two=Lazy(grad_two),
            conv_out=Lazy(conv_out),
            projected=Lazy(projected),
            rim=Lazy(rim),
            gated=Lazy(gated),
            normed_conv_t=Lazy(normed_conv_t),
            inputs=Lazy(inputs),
            grad_two_b=(grad_two_b, pl.ANY),
            down=(down, pl.ANY),
            gate_up_t=(gate_up_t, pl.ANY),
            gate=(gate, pl.ANY),
            upward=(upward, pl.ANY),
            conv_in_t=(conv_in_t, pl.ANY),
            kernel=kernel,
            gains=gains,
            small=small,
        ),
        dict(
            result=((rows, width), F32, pl.ANY),
            small_out=Lazy(small.shape, F32),
            sum_attn_out=Lazy((block, channels), F32),
            sum_query=Lazy((block, columns), F32),
            sum_kv=Lazy((block, 2, kv_columns // 2), F32),
            sum_down=Lazy((block, units), F32),
            sum_gate_up=Lazy((block, 2, units), F32),
            sum_conv_out=Lazy((block, channels), F32),
            sum_conv_in=Lazy((3, block, channels), F32),
        ),
        dict(
            gathered=pltpu.VMEM((rows, width), BF16),
            partial=pltpu.VMEM((rows, width), BF16),
            grad_one_t=pltpu.VMEM((width, rows), BF16),
            grad_one=pltpu.VMEM((quarter, width), F32),
            joined=pltpu.VMEM((rows, 2 * units), BF16),
            input_grad=pltpu.VMEM((rows, width), BF16),
            final=pltpu.VMEM((2, quarter // 2, width), F32),
            g_sem=pltpu.SemaphoreType.DMA((8,)),
            grad_projected=pltpu.VMEM((rows, 3 * channels), BF16),
            grad_gated=pltpu.VMEM((rows, channels), F32),
            mixed=pltpu.VMEM((rows + 8, channels), F32),
            grad_conv=pltpu.VMEM((rows + 8, channels), F32),
            rim_out=pltpu.VMEM((8, channels), F32),
            rim_in=pltpu.VMEM((8, channels), F32),
            m_sem=pltpu.SemaphoreType.DMA((2,)),
            e_sem=pltpu.SemaphoreType.DMA,
            down_tile=pltpu.VMEM((2, size, width), BF16),
            gate_tile=pltpu.VMEM((2, rows, size), F32),
            up_tile=pltpu.VMEM((2, rows, size), F32),
            h_sem=pltpu.SemaphoreType.DMA((2, 3)),
            conv_tile=pltpu.VMEM((2, 3, size, channels), BF16),
            c_sem=pltpu.SemaphoreType.DMA((2, 3)),
            gain_term=pltpu.VMEM((1, width), F32),
            slots=pltpu.VMEM((stages,) + small.shape, F32),
            s_send=pltpu.SemaphoreType.DMA((stages,)),
            s_recv=pltpu.SemaphoreType.DMA((stages,)),
            **stream_scratch(2 * units, 128),
            **exchange_scratch(rows, width),
            **ring_scratch(devices, sides, block, widths),
        ),
        4,
        62,
        2 * rows * width * sum(widths) * 3,
    )


def local(
    tokens,
    lengths,
    norm_conv,
    conv_in,
    conv_kernel,
    conv_out,
    norm_mlp_one,
    gate_up_one,
    down_one,
    norm_attn,
    query_weight,
    kv_weight,
    query_gain,
    key_gain,
    attn_out,
    norm_mlp_two,
    gate_up_two,
    down_two,
    cotangent,
):
    row_count = tokens.shape[0]
    width = tokens.shape[1]
    quarter = row_count // 4
    local_kv = kv_weight.shape[2] // HEAD
    device = lax.axis_index("dp")
    devices = lax.axis_size("dp")
    index = lax.axis_index("tensor")
    place_index = device % SPAN
    offsets = jnp.concatenate(
        [o * quarter + jnp.arange(quarter, dtype=jnp.int32) for o in block_owners(index)]
    )
    positions = place_index * row_count + offsets
    gains = jnp.stack([norm_conv, norm_mlp_one, norm_attn, norm_mlp_two])
    head_gains = jnp.stack([query_gain, key_gain], axis=1)
    frequency = THETA ** (-2.0 * jnp.arange(HEAD // 2, dtype=jnp.float32) / HEAD)
    angles = frequency[:, None] * positions.astype(jnp.float32)[None, :]
    tables = (jnp.cos(angles), jnp.sin(angles))
    gate_up_one_t = jnp.transpose(gate_up_one, (1, 2, 0))
    gate_up_two_t = jnp.transpose(gate_up_two, (1, 2, 0))
    conv_in_t = jnp.transpose(conv_in, (1, 0, 2))
    kv_flat = kv_weight.reshape(width, 2 * local_kv * HEAD)

    (
        normed_attn_b,
        normed_attn_t,
        two_own,
        one_own,
        inputs_own,
        norm_one_t,
        normed_conv_t,
        active_one,
        gate_one,
        up_one,
        gated_b,
        projected,
        rim,
        grad_b,
        grad_b_t,
        incoming,
    ) = first_forward(
        tokens, cotangent, conv_in_t, conv_kernel, conv_out, gate_up_one_t, down_one, gains, lengths
    )
    (
        active_two,
        joined_two,
        norm_two_t,
        three_own,
        *kept,
        attended_b,
        attended_t,
        log_total,
    ) = attention_forward(
        normed_attn_b,
        query_weight,
        kv_flat,
        head_gains,
        attn_out,
        two_own,
        tables,
        gains,
        lengths,
        gate_up_two_t,
        down_two,
        grad_b,
    )
    kept = (*kept, attended_t, log_total)
    (
        grad_three_t,
        grad_query,
        grad_kv,
        grad_two_b,
        grad_two_t,
        grad_two,
        small,
        sum_down_two,
        sum_gate_up_two,
        output,
    ) = attention_backward(
        grad_b_t,
        norm_two_t,
        active_two,
        joined_two,
        gate_up_two_t,
        down_two,
        three_own,
        incoming,
        kept,
        attn_out,
        query_weight,
        kv_flat,
        head_gains,
        two_own,
        tables,
        gains,
        lengths,
        devices,
    )

    (
        grad_inputs,
        small,
        sum_attn_out,
        sum_query,
        sum_kv,
        sum_down_one,
        sum_gate_up_one,
        sum_conv_out,
        sum_conv_in,
    ) = first_backward(
        [grad_three_t, normed_attn_t, grad_two_t, norm_one_t, normed_conv_t],
        [attended_b, grad_query, grad_kv, active_one, gated_b],
        grad_two_b,
        down_one,
        gate_up_one_t,
        gate_one,
        up_one,
        one_own,
        grad_two,
        conv_out,
        conv_in_t,
        projected,
        rim,
        conv_kernel,
        inputs_own,
        gains,
        small,
        devices,
    )
    out_rows = width // devices
    return (
        output,
        grad_inputs,
        small[0],
        jnp.transpose(sum_conv_in, (1, 0, 2)),
        small[5:, : conv_out.shape[0]],
        sum_conv_out.T,
        small[1],
        sum_gate_up_one,
        sum_down_one.T,
        small[2],
        sum_query,
        sum_kv,
        small[4, :HEAD],
        small[4, HEAD : 2 * HEAD],
        sum_attn_out.T,
        small[3],
        sum_gate_up_two,
        sum_down_two.T,
    )


def solution(mesh):
    in_specs = (
        P("dp", None),
        P(),
        P(),
        P(None, None, "tensor"),
        P(None, "tensor"),
        P("tensor", None),
        P(),
        P(None, None, "tensor"),
        P("tensor", None),
        P(),
        P(None, "tensor"),
        P(None, None, "tensor"),
        P(),
        P(),
        P("tensor", None),
        P(),
        P(None, None, "tensor"),
        P("tensor", None),
        P("dp", None),
    )
    out_specs = (
        P("dp", None),
        P("dp", None),
        P(),
        P("dp", None, "tensor"),
        P(None, "tensor"),
        P("tensor", "dp"),
        P(),
        P("dp", None, "tensor"),
        P("tensor", "dp"),
        P(),
        P("dp", "tensor"),
        P("dp", None, "tensor"),
        P(),
        P(),
        P("tensor", "dp"),
        P(),
        P("dp", None, "tensor"),
        P("tensor", "dp"),
    )
    return jax.shard_map(local, mesh=mesh, in_specs=in_specs, out_specs=out_specs, check_vma=False)
```

```python
import jax
import jax.numpy as jnp
from jax import lax
from jax.experimental import pallas as pl
from jax.experimental.pallas import tpu as pltpu
from jax.sharding import PartitionSpec as P

HEAD = 64
KW = 3
SPAN = 4
GROUP = 3


EPSILON = 1e-05
THETA = 1000000.0
BF16 = jnp.bfloat16
F32 = jnp.float32


def matmul(left, right):
    return jnp.dot(left, right, preferred_element_type=F32)


def inner_back(left, right):
    return lax.dot_general(left, right, (((1,), (1,)), ((), ())), preferred_element_type=F32)


def normalize(values, gain):
    inverse = lax.rsqrt(jnp.mean(values * values, axis=-1, keepdims=True) + EPSILON)
    return (values * inverse * gain, inverse)


def normalize_back(values, inverse, gain, grad_result):
    weighted = grad_result * gain
    grad_gain = jnp.sum(grad_result * values * inverse, axis=tuple(range(values.ndim - 1)))
    inner = jnp.mean(weighted * values, axis=-1, keepdims=True)
    grad_values = inverse * (weighted - values * inverse * inverse * inner)
    return (grad_values, grad_gain)


CHUNKS = 4
SLOTS = 3
MESH = pl.DeviceIdType.MESH


class Lazy:
    def __init__(self, value, dtype=None):
        self.value, self.dtype = value, dtype


class Refs:
    def __init__(self, names, refs):
        self.__dict__.update(zip(names, refs))

    def begin(self, inputs, outputs, refs):
        self.arriving, self.leaving, self.homes = {}, [], {}
        for at, name in enumerate(inputs):
            ref = self.__dict__[name]
            copy = pltpu.make_async_copy(refs[at], ref, self.lazy_in.at[at])
            copy.start()
            self.arriving[id(ref)] = copy
        for at, name in enumerate(outputs):
            self.homes[id(self.__dict__[name])] = (refs[len(inputs) + at], at)

    def need(self, *refs):
        for ref in refs:
            self.arriving.pop(id(ref)).wait()

    def flush(self, *refs):
        for ref in refs:
            home, at = self.homes.pop(id(ref))
            copy = pltpu.make_async_copy(ref, home, self.lazy_out.at[at, 0])
            copy.start()
            self.leaving.append(copy)

    def flush_blocks(self, ref, owners):
        home, at = self.homes.pop(id(ref))
        rows = ref.shape[0] // 4
        for block, owner in enumerate(owners):
            copy = pltpu.make_async_copy(
                ref.at[pl.ds(block * rows, rows)],
                home.at[pl.ds(pl.multiple_of(owner * rows, rows), rows)],
                self.lazy_out.at[at, block],
            )
            copy.start()
            self.leaving.append(copy)

    def end(self):
        assert not self.homes
        for copy in list(self.arriving.values()) + self.leaving:
            copy.wait()


def run_kernel(body, inputs, outputs, scratch, collective_id, limit, flops):
    arrays, specs, names, out_names = [], [], [], []
    scratch = dict(scratch)
    lazy_in = [name for name, value in inputs.items() if isinstance(value, Lazy)]
    lazy_out = [name for name, value in outputs.items() if isinstance(value, Lazy)]
    for name, value in inputs.items():
        if isinstance(value, Lazy):
            array, space = value.value, pl.ANY
            scratch[name] = pltpu.VMEM(array.shape, array.dtype)
            names.append(None)
        else:
            array, space = value if isinstance(value, tuple) else (value, pltpu.VMEM)
            names.append(name)
        arrays.append(array)
        specs.append(pl.BlockSpec(memory_space=space))
    shapes, out_specs = [], []
    for name, value in outputs.items():
        if isinstance(value, Lazy):
            shape, dtype, space = value.value, value.dtype, pl.ANY
            scratch[name] = pltpu.VMEM(shape, dtype)
            names.append(None)
        else:
            shape, dtype, space = value if len(value) == 3 else (*value, pltpu.VMEM)
            names.append(name)
        shapes.append(jax.ShapeDtypeStruct(shape, dtype))
        out_specs.append(pl.BlockSpec(memory_space=space))
    scratch["lazy_in"] = pltpu.SemaphoreType.DMA((max(len(lazy_in), 1),))
    scratch["lazy_out"] = pltpu.SemaphoreType.DMA((max(len(lazy_out), 1), 4))
    names += list(scratch)

    def whole(*refs):
        r = Refs([n for n in names if n], [ref for n, ref in zip(names, refs) if n])
        r.begin(lazy_in, lazy_out, [ref for n, ref in zip(names, refs) if not n])
        body(r)
        r.end()

    return pl.pallas_call(
        whole,
        in_specs=specs,
        out_specs=out_specs,
        out_shape=shapes,
        scratch_shapes=list(scratch.values()),
        compiler_params=pltpu.CompilerParams(
            collective_id=collective_id, has_side_effects=True, vmem_limit_bytes=limit * 2**20
        ),
        cost_estimate=pl.CostEstimate(
            flops=flops,
            bytes_accessed=sum(a.size * a.dtype.itemsize for a in arrays),
            transcendentals=0,
        ),
    )(*arrays)


def greet(peers):
    barrier = pltpu.get_barrier_semaphore()
    for peer in peers:
        pl.semaphore_signal(barrier, inc=1, device_id=peer, device_id_type=MESH)
    pl.semaphore_wait(barrier, len(peers))


def tensor_peers():
    me = lax.axis_index("tensor")
    return [dict(tensor=me ^ 1), dict(tensor=me ^ 2)]


def span_peers():
    me = lax.axis_index("dp")
    place = lax.rem(me, SPAN)
    return [dict(dp=me - place + lax.rem(place + k, SPAN)) for k in range(1, SPAN)]


def remote(src, dst, send, recv, peer):
    return pltpu.make_async_remote_copy(
        src_ref=src, dst_ref=dst, send_sem=send, recv_sem=recv, device_id=peer, device_id_type=MESH
    )


def exchange_scratch(rows, width):
    quarter = rows // 4
    return dict(
        near_rows=pltpu.VMEM((2 * quarter, width), BF16),
        across_rows=pltpu.VMEM((quarter, width), BF16),
        far_rows=pltpu.VMEM((quarter, width), BF16),
        x_send=pltpu.SemaphoreType.DMA((6 * CHUNKS,)),
        x_recv=pltpu.SemaphoreType.DMA((6 * CHUNKS,)),
    )


def sum_and_gather(r, partial, gathered, gathered_t, compute):
    near, across, far = r.near_rows, r.across_rows, r.far_rows
    core, other = tensor_peers()
    quarter = partial.shape[0] // 4
    size = quarter // CHUNKS
    copies = {}

    def copy(kind, at, src, dst, peer):
        number = kind * CHUNKS + at
        copies[kind, at] = remote(src, dst, r.x_send.at[number], r.x_recv.at[number], peer)
        copies[kind, at].start()

    def part(block, at):
        return pl.ds(block * quarter + at * size, size)

    def turn(block):
        if gathered_t is not None:
            rows = slice(block * quarter, (block + 1) * quarter)
            gathered_t[:, rows] = gathered[rows, :].T

    for at in range(CHUNKS):
        copy(0, at, partial.at[part(3, at)], near.at[part(1, at)], core)
    for at in range(CHUNKS):
        copy(1, at, partial.at[part(2, at)], near.at[part(0, at)], core)
    for at in range(CHUNKS):
        copies[0, at].wait_recv()
        far[part(0, at), :] = (
            partial[part(1, at), :].astype(F32) + near[part(1, at), :].astype(F32)
        ).astype(BF16)
        copy(2, at, far.at[part(0, at)], across.at[part(0, at)], other)
    yield 1
    for at in range(CHUNKS):
        copies[1, at].wait_recv()
        copies[2, at].wait_recv()
        total = (
            partial[part(0, at), :].astype(F32)
            + near[part(0, at), :].astype(F32)
            + across[part(0, at), :].astype(F32)
        )
        gathered[part(0, at), :] = compute(total, part(0, at), at == 0)
        copy(3, at, gathered.at[part(0, at)], gathered.at[part(1, at)], other)
        copy(4, at, gathered.at[part(0, at)], gathered.at[part(2, at)], core)
    turn(0)
    yield 1
    for at in range(CHUNKS):
        copies[3, at].wait_recv()
        copy(5, at, gathered.at[part(1, at)], gathered.at[part(3, at)], core)
    turn(1)
    for at in range(CHUNKS):
        copies[4, at].wait_recv()
    turn(2)
    for at in range(CHUNKS):
        copies[5, at].wait_recv()
    turn(3)
    for made in copies.values():
        made.wait_send()
    yield 1


def exhaust(main):
    for _ in main:
        pass


def norm_rows(total, rows, residual, gain, hidden):
    values = residual[rows, :] + total
    hidden[rows, :] = values
    return normalize(values, gain)[0].astype(BF16)


def back_rows(total, rows, first, hidden, gain, incoming, own, grad_gain):
    values = hidden[rows, :]
    inverse = lax.rsqrt(jnp.mean(values * values, axis=-1, keepdims=True) + EPSILON)
    made, term = normalize_back(values, inverse, gain, total)
    made = made + incoming[rows, :]
    if own is not None:
        own[rows, :] = made
    term = term.reshape(1, -1)
    grad_gain[...] = term if first else grad_gain[...] + term
    return made.astype(BF16)


def ring_peers(count):
    me = lax.axis_index("dp")
    even = lax.rem(me, 2) == 0
    place = jnp.where(even, me // 2, count - 1 - me // 2)

    def at(position):
        position = lax.rem(position + count, count)
        return jnp.where(position < count // 2, 2 * position, 2 * (count - 1 - position) + 1)

    return at(place + 1), at(place - 1), lambda distance: at(place + distance)


class Rings:
    def __init__(self, devices, sides, segments, held, send, recv, credit, store):
        self.devices, self.sides, self.segments, self.held = devices, sides, segments, held
        self.send, self.recv, self.credit, self.store = send, recv, credit, store
        self.rows = segments[0][0][0].shape[0] // devices
        self.half = self.rows // sides
        self.steps = devices - 1
        self.following, self.previous, self.owner_at = ring_peers(devices)

    def peers(self):
        return [dict(dp=self.following), dict(dp=self.previous)]

    def copy(self, seg, side, step):
        number = (seg * self.sides + side) * self.steps + step
        return remote(
            self.held[seg].at[side, step % SLOTS],
            self.held[seg].at[side, (step + 1) % SLOTS],
            self.send.at[number],
            self.recv.at[number],
            dict(dp=self.following if side == 0 else self.previous),
        )

    def unit(self, seg, step):
        sides, half, steps = self.sides, self.half, self.steps
        last = step == steps
        slot = step % SLOTS
        starts = []
        for side in range(sides):
            if last:
                owner = lax.axis_index("dp")
            else:
                owner = self.owner_at(-1 - step if side == 0 else 1 + step)
            starts.append(pl.multiple_of(owner * self.rows + side * half, 16))
        if step:
            for side in range(sides):
                self.copy(seg, side, step - 1).wait_send()
                if step <= steps + 1 - SLOTS:
                    pl.semaphore_signal(
                        self.credit.at[seg * sides + side],
                        inc=1,
                        device_id=dict(dp=self.previous if side == 0 else self.following),
                        device_id_type=MESH,
                    )
                self.copy(seg, side, step - 1).wait_recv()
        column = 0
        for left, right in self.segments[seg]:
            pieces = [left[pl.ds(start, half), :] for start in starts]
            piece = pieces[0] if sides == 1 else jnp.concatenate(pieces, axis=0)
            made = jnp.dot(piece, right[...], preferred_element_type=F32)
            at = slice(column, column + made.shape[1])
            values = []
            for side in range(sides):
                value = made[side * half : (side + 1) * half]
                if step:
                    value = value + self.held[seg][side, slot, :, at].astype(F32)
                if last:
                    values.append(value)
                else:
                    self.held[seg][side, slot, :, at] = value.astype(BF16)
            if last:
                self.store(seg, column, values[0] if sides == 1 else jnp.concatenate(values, axis=0))
            column += made.shape[1]
        if not last:
            for side in range(sides):
                if step >= SLOTS - 1:
                    pl.semaphore_wait(self.credit.at[seg * sides + side], 1)
                self.copy(seg, side, step).start()


def ring_scratch(devices, sides, rows, widths):
    copies = len(widths) * sides * (devices - 1)
    made = {
        f"held{at}": pltpu.VMEM((sides, SLOTS, rows // sides, w), BF16)
        for at, w in enumerate(widths)
    }
    made["r_send"] = pltpu.SemaphoreType.DMA((copies,))
    made["r_recv"] = pltpu.SemaphoreType.DMA((copies,))
    made["r_credit"] = pltpu.SemaphoreType.REGULAR((len(widths) * sides,))
    return made


def interleave(main, units, first):
    units = iter(units)

    def some(number):
        for _ in range(number):
            unit = next(units, None)
            if unit is not None:
                unit()

    some(first)
    for number in main:
        some(number)
    for unit in units:
        unit()


def piece_sides(width, devices):
    return 2 if width // devices % 32 == 0 else 1


def block_owners(index):
    return [index, index ^ 2, index ^ 1, index ^ 3]


def cross(left, right):
    return lax.dot_general(left, right, (((1,), (1,)), ((), ())), preferred_element_type=F32)


def turn_t(values, cosine, sine, back):
    middle = HEAD // 2
    low, high = values[:middle], values[middle:]
    if back:
        return jnp.concatenate([low * cosine + high * sine, high * cosine - low * sine], axis=0)
    return jnp.concatenate([low * cosine - high * sine, high * cosine + low * sine], axis=0)


def head_norm_t(values, gain):
    inverse = lax.rsqrt(jnp.mean(values * values, axis=0, keepdims=True) + EPSILON)
    return values * inverse * gain


def head_back_t(values, gain, grad):
    inverse = lax.rsqrt(jnp.mean(values * values, axis=0, keepdims=True) + EPSILON)
    weighted = grad * gain
    inner = jnp.mean(weighted * values, axis=0, keepdims=True)
    return inverse * (weighted - values * inverse * inverse * inner), grad * values * inverse


def block_positions(block, quarter, shape, axis):
    place = lax.rem(lax.axis_index("dp"), SPAN)
    owner = block_owners(lax.axis_index("tensor"))[block]
    start = (place * 4 + owner) * quarter
    return start + lax.broadcasted_iota(jnp.int32, shape, axis)


def own_length(r):
    return r.lengths[lax.axis_index("dp") // SPAN]


def fill_bias(r):
    quarter = r.bias.shape[0] // 4
    shape = (quarter, quarter)
    for row in range(4):
        keys = block_positions(row, quarter, shape, 0)
        live = keys < own_length(r)
        for column in range(4):
            allowed = live & (keys <= block_positions(column, quarter, shape, 1))
            at = slice(row * quarter, (row + 1) * quarter)
            r.bias[at, column * quarter : (column + 1) * quarter] = jnp.where(allowed, 0.0, -1e30)


def head_rows(head):
    return slice(head * HEAD, (head + 1) * HEAD)


def attention_forward(
    normed_b, query_weight, kv_weight, head_gains, attn_out, residual, tables, gains, lengths,
    gate_up_t, down, grad_b,
):
    rows, width = normed_b.shape
    columns = query_weight.shape[1]
    kv_columns = kv_weight.shape[1] // 2
    heads, kv_heads = columns // HEAD, kv_columns // HEAD
    units = down.shape[0]

    def body(r):
        me = lax.axis_index("dp")
        place = lax.rem(me, SPAN)
        greet(tensor_peers() + span_peers())
        for copy in hidden_fetch(r, 0, TILE):
            copy.start()

        def pass_on(distance):
            return remote(
                r.own, r.near.at[distance - 1], r.p_send.at[distance - 1], r.p_recv.at[distance - 1],
                dict(dp=me + distance),
            )

        r.need(r.normed, r.kv_weight, r.cosine, r.sine)
        cosine, sine = r.cosine[...], r.sine[...]
        made = jnp.dot(r.normed[...], r.kv_weight[...], preferred_element_type=F32)
        r.key_raw[...] = made[:, :kv_columns].T
        r.own[:, kv_columns:] = made[:, kv_columns:].astype(BF16)
        for group in range(kv_heads):
            keys = head_norm_t(r.key_raw[head_rows(group), :], r.head_gains[:, 1:2])
            r.keys_t[head_rows(group), :] = turn_t(keys, cosine, sine, False).astype(BF16)
        r.own[:, :kv_columns] = r.keys_t[...].T
        for distance in range(1, SPAN):

            @pl.when(place + distance < SPAN)
            def _():
                pass_on(distance).start()

        r.need(r.query_weight)
        made = jnp.dot(r.normed[...], r.query_weight[...], preferred_element_type=F32)
        r.query_raw[...] = made.T
        for head in range(heads):
            query = head_norm_t(r.query_raw[head_rows(head), :], r.head_gains[:, 0:1])
            query = turn_t(query, cosine, sine, False).astype(BF16)
            r.query[head_rows(head), :] = query * jnp.asarray(HEAD ** (-0.5), BF16)
        fill_bias(r)

        def part(piece, first):
            for group in range(kv_heads):
                keys = piece[:, head_rows(group)]
                values_t = piece[:, kv_columns + group * HEAD : kv_columns + (group + 1) * HEAD].T
                for head in range(group * GROUP, (group + 1) * GROUP):
                    at = head_rows(head)
                    scores = jnp.dot(keys, r.query[at, :], preferred_element_type=F32)
                    if first:
                        scores = scores + r.bias[...]
                    expo = jnp.exp(scores)
                    total = jnp.sum(expo, axis=0, keepdims=True)
                    made = jnp.dot(values_t, expo.astype(BF16), preferred_element_type=F32)
                    if first:
                        r.total[head : head + 1, :] = total
                        r.attended_t[at, :] = made
                    else:
                        r.total[head : head + 1, :] += total
                        r.attended_t[at, :] += made

        part(r.own[...], True)

        @pl.loop(1, place + 1)
        def _(distance):
            pass_on(distance).wait_recv()
            part(r.near[distance - 1], False)

        for head in range(heads):
            at = head_rows(head)
            made = r.attended_t[at, :] / r.total[head : head + 1, :]
            r.attended_t[at, :] = made
            r.attended[:, at] = made.T.astype(BF16)
        r.log_total[...] = jnp.log(r.total[...])
        r.need(r.attn_out, r.residual, r.grad_b)
        r.flush(r.query_raw, r.key_raw, r.query, r.own, r.near, r.attended, r.attended_t, r.log_total)
        r.partial[...] = jnp.dot(
            r.attended[...], r.attn_out[...], preferred_element_type=F32
        ).astype(BF16)
        exhaust(
            sum_and_gather(
                r, r.partial, r.gathered, r.gathered_t,
                lambda total, at, first: norm_rows(total, at, r.residual, r.gains[3:4, :], r.hidden),
            )
        )
        r.flush(r.gathered_t, r.hidden)
        for distance in range(1, SPAN):

            @pl.when(place + distance < SPAN)
            def _():
                pass_on(distance).wait_send()

        def tile(number, wide, gate_w, up_w, down_w):
            lanes = tile_lanes(number, wide)
            a = cross(r.gathered[...], gate_w)
            z = cross(r.gathered[...], up_w)
            grad = cross(r.grad_b[...], down_w)
            sigma = jax.nn.sigmoid(a)
            r.active[:, lanes] = (a * sigma * z).astype(BF16)
            grad_gate = (grad * z * sigma * (1.0 + a * (1.0 - sigma))).astype(BF16)
            grad_up = (grad * a * sigma).astype(BF16)
            put_joined(r.joined, number, TILE, (grad_gate, grad_up), units)

        hidden_tiles(r, units, tile)
        r.flush(r.active, r.joined)

    return run_kernel(
        body,
        dict(
            normed=Lazy(normed_b),
            query_weight=Lazy(query_weight),
            kv_weight=Lazy(kv_weight),
            head_gains=head_gains,
            attn_out=Lazy(attn_out),
            residual=Lazy(residual),
            cosine=Lazy(tables[0]),
            sine=Lazy(tables[1]),
            gate_up_t=(gate_up_t, pl.ANY),
            down=(down, pl.ANY),
            grad_b=Lazy(grad_b),
            lengths=(lengths, pltpu.SMEM),
            gains=gains,
        ),
        dict(
            active=Lazy((rows, units), BF16),
            joined=Lazy((rows, 2 * units), BF16),
            gathered_t=Lazy((width, rows), BF16),
            hidden=Lazy(residual.shape, F32),
            query_raw=Lazy((columns, rows), F32),
            key_raw=Lazy((kv_columns, rows), F32),
            query=Lazy((columns, rows), BF16),
            own=Lazy((rows, 2 * kv_columns), BF16),
            near=Lazy((SPAN - 1, rows, 2 * kv_columns), BF16),
            attended=Lazy((rows, columns), BF16),
            attended_t=Lazy((columns, rows), F32),
            log_total=Lazy((heads, rows), F32),
        ),
        dict(
            keys_t=pltpu.VMEM((kv_columns, rows), BF16),
            bias=pltpu.VMEM((rows, rows), F32),
            total=pltpu.VMEM((heads, rows), F32),
            partial=pltpu.VMEM((rows, width), BF16),
            gathered=pltpu.VMEM((rows, width), BF16),
            **hidden_scratch(width),
            p_send=pltpu.SemaphoreType.DMA((SPAN - 1,)),
            p_recv=pltpu.SemaphoreType.DMA((SPAN - 1,)),
            **exchange_scratch(rows, width),
        ),
        2,
        58,
        16 * rows * rows * SPAN * columns,
    )


def stream_product(r, left, weights, parts, out):
    width = weights.shape[2]
    size = r.tile.shape[2]
    tiles = width // size
    depth = sum(part[3] for part in parts)

    def fetch(j):
        return [
            pltpu.make_async_copy(
                weights.at[which, pl.ds(there, count), pl.ds(j * size, size)],
                r.tile.at[j % 2, pl.ds(here, count), :],
                r.tile_sem.at[j % 2, k],
            )
            for k, (which, there, here, count) in enumerate(parts)
        ]

    for copy in fetch(0):
        copy.start()
    for j in range(tiles):
        if j + 1 < tiles:
            for copy in fetch(j + 1):
                copy.start()
        for copy in fetch(j):
            copy.wait()
        made = jnp.dot(left[...], r.tile[j % 2, 0:depth, :], preferred_element_type=F32)
        out[:, j * size : (j + 1) * size] = made.astype(BF16)
        if j % 2:
            yield 1


def stream_scratch(depth, size):
    return dict(
        tile=pltpu.VMEM((2, depth, size), BF16),
        tile_sem=pltpu.SemaphoreType.DMA((2, 4)),
    )


def attention_backward(
    grad_b_t, norm_two_t, active, joined, gate_up_t, down, three, incoming,
    kept, attn_out, query_weight, kv_weight, head_gains, two, tables, gains, lengths, devices,
):
    units, tokens_width = gate_up_t.shape[1:]
    query_raw, key_raw, query, own, near, attended_t, log_total = kept
    rows, width = active.shape[0], tokens_width
    columns = query_weight.shape[1]
    kv_columns = kv_weight.shape[1] // 2
    heads, kv_heads = columns // HEAD, kv_columns // HEAD
    sides = piece_sides(width, devices)
    block = width // devices
    segment_widths = [units] + joined_widths(units)

    def body(r):
        me = lax.axis_index("dp")
        place = lax.rem(me, SPAN)

        def store(seg, column, value):
            if seg == 0:
                r.sum_down[...] = value
                r.flush(r.sum_down)
            else:
                store_joined(r.sum_gate_up, seg - 1, value, units)
                if seg == 2:
                    r.flush(r.sum_gate_up)

        rings = Rings(
            devices, sides,
            [[(r.grad_b_t, r.active)]] + joined_segments(r.norm_two_t, r.joined, units),
            [r.held0, r.held1, r.held2], r.r_send, r.r_recv, r.r_credit, store,
        )
        greet(rings.peers() + tensor_peers() + span_peers())

        def pass_back(distance):
            return remote(
                r.far.at[distance - 1], r.arrived.at[distance - 1],
                r.p_send.at[distance - 1], r.p_recv.at[distance - 1], dict(dp=me - distance),
            )

        def part(piece, write, masked):
            for group in range(kv_heads):
                keys = piece[:, head_rows(group)]
                value_at = slice(kv_columns + group * HEAD, kv_columns + (group + 1) * HEAD)
                values = piece[:, value_at]
                keys_t = keys.T
                grad_k = grad_v = None
                for head in range(group * GROUP, (group + 1) * GROUP):
                    at = head_rows(head)
                    q, grads = r.query[at, :], r.grads[:, at]
                    scores = jnp.dot(keys, q, preferred_element_type=F32)
                    scores = scores - r.log_total[head : head + 1, :]
                    if masked:
                        scores = scores + r.bias[...]
                    probs = jnp.exp(scores)
                    made = jnp.dot(probs.astype(BF16), grads, preferred_element_type=F32)
                    grad_v = made if grad_v is None else grad_v + made
                    grad_probs = cross(values, grads)
                    grad_scores = (probs * (grad_probs - r.delta[head : head + 1, :])).astype(BF16)
                    made = cross(grad_scores, q)
                    grad_k = made if grad_k is None else grad_k + made
                    made = jnp.dot(keys_t, grad_scores, preferred_element_type=F32)
                    if masked:
                        r.grad_q_t[at, :] = made
                    else:
                        r.grad_q_t[at, :] += made
                write(head_rows(group), grad_k)
                write(value_at, grad_v)

        def main():
            yield from stream_product(r, r.joined, r.gate_up_t, joined_parts(units), r.partial)
            fill_bias(r)
            r.need(r.three, r.incoming)
            yield from sum_and_gather(
                r, r.partial, r.gathered, r.grad_three_t,
                lambda total, at, first: back_rows(
                    total, at, first, r.three, r.gains[3:4, :], r.incoming, r.grad_three, r.gain_term
                ),
            )
            r.flush(r.grad_three_t)
            r.small[...] = jnp.zeros_like(r.small)
            r.small[3:4, :] = r.gain_term[...]
            r.need(r.attn_out, r.attended_t, r.own, r.near, r.query, r.log_total)
            r.grads[...] = cross(r.gathered[...], r.attn_out[...]).astype(BF16)
            for head in range(heads):
                at = head_rows(head)
                grads_t = r.grads[:, at].astype(F32).T
                r.delta[head : head + 1, :] = jnp.sum(
                    grads_t * r.attended_t[at, :], axis=0, keepdims=True
                )
            yield 1

            def write_own(at, value):
                r.grad_own[:, at] = value

            part(r.own[...], write_own, True)
            yield 1

            @pl.loop(1, place + 1)
            def _(distance):
                def write_far(at, value):
                    r.far[distance - 1, :, at] = value.astype(BF16)

                part(r.near[distance - 1], write_far, False)
                pass_back(distance).start()

            yield 2
            r.need(r.cosine, r.sine, r.query_raw, r.key_raw, r.query_weight, r.kv_weight, r.two)
            cosine, sine = r.cosine[...], r.sine[...]
            terms = None
            for head in range(heads):
                at = head_rows(head)
                grad = turn_t(r.grad_q_t[at, :] * HEAD ** (-0.5), cosine, sine, True)
                made, term = head_back_t(r.query_raw[at, :], r.head_gains[:, 0:1], grad)
                terms = term if terms is None else terms + term
                r.grad_query[:, at] = made.T.astype(BF16)
            r.small[4:5, 0:HEAD] = jnp.sum(terms.T, axis=0, keepdims=True)
            yield 1
            for distance in range(1, SPAN):

                @pl.when(place + distance < SPAN)
                def _():
                    pass_back(distance).wait_recv()
                    r.grad_own[...] += r.arrived[distance - 1].astype(F32)

            terms = None
            for group in range(kv_heads):
                at = head_rows(group)
                grad = turn_t(r.grad_own[:, at].T, cosine, sine, True)
                made, term = head_back_t(r.key_raw[at, :], r.head_gains[:, 1:2], grad)
                terms = term if terms is None else terms + term
                r.grad_kv[:, at] = made.T.astype(BF16)
            r.small[4:5, HEAD : 2 * HEAD] = jnp.sum(terms.T, axis=0, keepdims=True)
            r.grad_kv[:, kv_columns:] = r.grad_own[:, kv_columns:].astype(BF16)
            r.flush(r.grad_query, r.grad_kv)
            r.partial[...] = (
                cross(r.grad_query[...], r.query_weight[...]) + cross(r.grad_kv[...], r.kv_weight[...])
            ).astype(BF16)
            yield 1
            yield from sum_and_gather(
                r, r.partial, r.grad_two_b, r.grad_two_t,
                lambda total, at, first: back_rows(
                    total, at, first, r.two, r.gains[2:3, :], r.grad_three, r.grad_two, r.gain_term
                ),
            )
            r.small[2:3, :] = r.gain_term[...]
            r.flush(r.grad_two_b, r.grad_two_t, r.grad_two, r.small)
            for distance in range(1, SPAN):

                @pl.when(place >= distance)
                def _():
                    pass_back(distance).wait_send()

            yield from stream_product(r, r.active, r.down, [(0, 0, 0, units)], r.partial)
            yield from sum_and_gather(
                r, r.partial, r.output, None,
                lambda total, at, first: (r.three[at, :] + total).astype(BF16),
            )
            r.flush_blocks(r.output, block_owners(lax.axis_index("tensor")))

        def first(seg):
            r.need(*((r.grad_b_t, r.active), (r.norm_two_t, r.joined), ())[seg])
            rings.unit(seg, 0)

        order = [(seg, step) for step in range(1, devices) for seg in range(3)]
        units_left = [lambda s=seg: first(s) for seg in range(3)]
        units_left += [lambda u=u: rings.unit(*u) for u in order]
        interleave(main(), units_left, 3)

    quarter = rows // 4
    return run_kernel(
        body,
        dict(
            grad_b_t=Lazy(grad_b_t),
            active=Lazy(active),
            norm_two_t=Lazy(norm_two_t),
            joined=Lazy(joined),
            gate_up_t=(gate_up_t, pl.ANY),
            down=(down.reshape((1,) + down.shape), pl.ANY),
            three=Lazy(three),
            incoming=Lazy(incoming),
            query_raw=Lazy(query_raw),
            key_raw=Lazy(key_raw),
            query=Lazy(query),
            own=Lazy(own),
            near=Lazy(near),
            attended_t=Lazy(attended_t),
            log_total=Lazy(log_total),
            attn_out=Lazy(attn_out),
            query_weight=Lazy(query_weight),
            kv_weight=Lazy(kv_weight),
            head_gains=head_gains,
            two=Lazy(two),
            cosine=Lazy(tables[0]),
            sine=Lazy(tables[1]),
            lengths=(lengths, pltpu.SMEM),
            gains=gains,
        ),
        dict(
            grad_three_t=Lazy((width, rows), BF16),
            grad_query=Lazy((rows, columns), BF16),
            grad_kv=Lazy((rows, 2 * kv_columns), BF16),
            grad_two_b=Lazy((rows, width), BF16),
            grad_two_t=Lazy((width, rows), BF16),
            grad_two=Lazy((quarter, width), F32),
            small=Lazy((8, width), F32),
            sum_down=Lazy((block, units), F32),
            sum_gate_up=Lazy((block, 2, units), F32),
            output=Lazy((rows, width), BF16),
        ),
        dict(
            partial=pltpu.VMEM((rows, width), BF16),
            gathered=pltpu.VMEM((rows, width), BF16),
            grad_three=pltpu.VMEM((quarter, width), F32),
            grads=pltpu.VMEM((rows, columns), BF16),
            gain_term=pltpu.VMEM((1, width), F32),
            delta=pltpu.VMEM((heads, rows), F32),
            bias=pltpu.VMEM((rows, rows), F32),
            grad_q_t=pltpu.VMEM((columns, rows), F32),
            grad_own=pltpu.VMEM((rows, 2 * kv_columns), F32),
            far=pltpu.VMEM((SPAN - 1, rows, 2 * kv_columns), BF16),
            arrived=pltpu.VMEM((SPAN - 1, rows, 2 * kv_columns), BF16),
            p_send=pltpu.SemaphoreType.DMA((SPAN - 1,)),
            p_recv=pltpu.SemaphoreType.DMA((SPAN - 1,)),
            **stream_scratch(2 * units, 256),
            **exchange_scratch(rows, width),
            **ring_scratch(devices, sides, block, segment_widths),
        ),
        3 + 2,
        61,
        2 * rows * width * units * 10,
    )


TILE = 512


def unit_tiles(units):
    return [(at, min(TILE, units - at)) for at in range(0, units, TILE)]


def hidden_fetch(r, number, wide):
    slot = lax.rem(number, 2)
    rows = pl.ds(number * TILE, wide)
    pairs = [
        (r.gate_up_t.at[:, rows, :], r.gate_up_tile.at[slot, :, 0:wide, :]),
        (r.down.at[rows, :], r.down_tile.at[slot, 0:wide, :]),
    ]
    return [pltpu.make_async_copy(a, b, r.h_sem.at[slot, k]) for k, (a, b) in enumerate(pairs)]


def hidden_tiles(r, units, tile):
    count = pl.cdiv(units, TILE)
    rest = units - (count - 1) * TILE

    def run(number, wide):
        for copy in hidden_fetch(r, number, wide):
            copy.wait()
        slot = lax.rem(number, 2)
        tile(
            number, wide,
            r.gate_up_tile[slot, 0, 0:wide, :],
            r.gate_up_tile[slot, 1, 0:wide, :],
            r.down_tile[slot, 0:wide, :],
        )

    @pl.loop(0, count - 1)
    def _(number):
        @pl.when(number + 1 < count - 1)
        def _():
            for copy in hidden_fetch(r, number + 1, TILE):
                copy.start()

        @pl.when(number + 1 == count - 1)
        def _():
            for copy in hidden_fetch(r, number + 1, rest):
                copy.start()

        run(number, TILE)

    run(count - 1, rest)


def joined_parts(units):
    main = units // 128 * 128
    rest = units - main
    return [
        (0, 0, 0, main),
        (1, 0, main, main),
        (0, main, 2 * main, rest),
        (1, main, 2 * main + rest, rest),
    ]


def put_joined(ref, number, size, values, units):
    main = units // 128 * 128
    rest = units - main
    wide = values[0].shape[1]
    for which, value in enumerate(values):
        if isinstance(number, int):
            at = number * size
            cut = min(wide, main - at)
            ref[:, which * main + at : which * main + at + cut] = value[:, :cut]
            if cut < wide:
                at = 2 * main + which * rest
                ref[:, at : at + rest] = value[:, cut:]
        else:
            ref[:, pl.ds(pl.multiple_of(which * main + number * size, 128), wide)] = value


def joined_segments(left, joined, units):
    main = units // 128 * 128
    return [
        [(left, joined.at[:, pl.ds(0, main)])],
        [(left, joined.at[:, pl.ds(main, 2 * units - main)])],
    ]


def joined_widths(units):
    main = units // 128 * 128
    return [main, 2 * units - main]


def store_joined(ref, part, value, units):
    main = units // 128 * 128
    rest = units - main
    if part == 0:
        ref[:, 0, 0:main] = value
    else:
        ref[:, 1, 0:main] = value[:, :main]
        ref[:, 0, main:units] = value[:, main : main + rest]
        ref[:, 1, main:units] = value[:, main + rest :]


def tile_lanes(number, wide):
    start = number * TILE
    return pl.ds(start if isinstance(start, int) else pl.multiple_of(start, TILE), wide)


def hidden_scratch(width):
    return dict(
        gate_up_tile=pltpu.VMEM((2, 2, TILE, width), BF16),
        down_tile=pltpu.VMEM((2, TILE, width), BF16),
        h_sem=pltpu.SemaphoreType.DMA((2, 2)),
    )


def first_forward(
    tokens, cotangent, conv_in_t, kernel, conv_out, gate_up_t, down, gains, lengths
):
    rows, width = tokens.shape
    channels = conv_out.shape[0]
    units = down.shape[0]
    quarter = rows // 4
    count = len(unit_tiles(units))

    def body(r):
        me = lax.axis_index("dp")
        index = lax.axis_index("tensor")
        place = lax.rem(me, SPAN)
        greet(tensor_peers() + span_peers())
        for copy in hidden_fetch(r, 0, TILE):
            copy.start()
        r.need(r.tokens)
        for at in range(4):
            part = slice(at * quarter, (at + 1) * quarter)
            values = r.tokens[part, :].astype(F32)
            r.normed[part, :] = normalize(values, r.gains[0:1, :])[0].astype(BF16)
        r.need(r.conv_in_t)
        for at in range(3):
            made = jnp.dot(r.normed[...], r.conv_in_t[at], preferred_element_type=F32)
            r.projected[:, at * channels : (at + 1) * channels] = made
        r.flush(r.projected)
        pad = 8
        r.mixed[0:pad, :] = jnp.zeros((pad, channels), F32)
        r.mixed[pad:, :] = r.projected[:, :channels] * r.projected[:, 2 * channels :]
        r.rim_out[...] = r.mixed[rows : rows + pad, :]
        rim_copy = remote(r.rim_out, r.rim_in, r.m_sem.at[0], r.m_sem.at[1], dict(dp=me + 1))

        @pl.when(place < SPAN - 1)
        def _():
            rim_copy.start()

        start = pl.multiple_of(index * quarter, quarter)
        r.inputs_own[...] = r.tokens[pl.ds(start, quarter), :].astype(F32)
        r.flush(r.inputs_own)

        @pl.when(place > 0)
        def _():
            rim_copy.wait_recv()
            r.mixed[0:pad, :] = r.rim_in[...]

        r.rim[...] = r.mixed[0:pad, :]
        r.flush(r.rim)
        taps = r.kernel[...].astype(F32)
        convolved = None
        for k in range(KW):
            term = taps[k : k + 1, :] * r.mixed[pad - KW + 1 + k : pad - KW + 1 + k + rows, :]
            convolved = term if convolved is None else convolved + term
        r.gated_true[...] = (r.projected[:, channels : 2 * channels] * convolved).astype(BF16)
        for at, owner in enumerate(block_owners(index)):
            start = pl.multiple_of(owner * quarter, quarter)
            r.gated[at * quarter : (at + 1) * quarter, :] = r.gated_true[pl.ds(start, quarter), :]
        r.need(r.conv_out)
        r.partial[...] = jnp.dot(r.gated[...], r.conv_out[...], preferred_element_type=F32).astype(BF16)
        r.flush(r.gated)
        waits = sum_and_gather(
            r, r.partial, r.gathered_one, r.norm_one_t,
            lambda total, at, first: norm_rows(total, at, r.inputs_own, r.gains[1:2, :], r.one),
        )
        next(waits)
        r.need(r.cotangent)
        for at, owner in enumerate(block_owners(index)):
            part = slice(at * quarter, (at + 1) * quarter)
            start = pl.multiple_of(owner * quarter, quarter)
            live = block_positions(at, quarter, (quarter, width), 0) < own_length(r)
            values = jnp.where(live, r.cotangent[pl.ds(start, quarter), :].astype(F32), 0.0)
            if at == 0:
                r.incoming[...] = values
            r.grad_b[part, :] = values.astype(BF16)
        next(waits)
        r.normed_t[...] = r.normed[...].T
        r.grad_b_t[...] = r.grad_b[...].T
        r.flush(r.normed_t, r.grad_b, r.grad_b_t, r.incoming)
        exhaust(waits)
        r.flush(r.one, r.norm_one_t)
        r.total[...] = jnp.zeros_like(r.total)

        def tile(number, wide, gate_w, up_w, down_w):
            a = cross(r.gathered_one[...], gate_w)
            z = cross(r.gathered_one[...], up_w)
            r.gate[number, :, 0:wide] = a
            r.upward[number, :, 0:wide] = z
            s = (a * jax.nn.sigmoid(a) * z).astype(BF16)
            r.active[:, tile_lanes(number, wide)] = s
            r.total[...] += jnp.dot(s, down_w, preferred_element_type=F32)

        hidden_tiles(r, units, tile)
        r.partial[...] = r.total[...].astype(BF16)
        r.flush(r.active, r.gate, r.upward)
        exhaust(
            sum_and_gather(
                r, r.partial, r.gathered, r.normed_attn_t,
                lambda total, at, first: norm_rows(total, at, r.one, r.gains[2:3, :], r.two),
            )
        )
        r.flush(r.gathered, r.normed_attn_t, r.two)

        @pl.when(place < SPAN - 1)
        def _():
            rim_copy.wait_send()

    return run_kernel(
        body,
        dict(
            tokens=Lazy(tokens),
            cotangent=Lazy(cotangent),
            conv_in_t=Lazy(conv_in_t),
            kernel=kernel,
            conv_out=Lazy(conv_out),
            gate_up_t=(gate_up_t, pl.ANY),
            down=(down, pl.ANY),
            lengths=(lengths, pltpu.SMEM),
            gains=gains,
        ),
        dict(
            gathered=Lazy((rows, width), BF16),
            normed_attn_t=Lazy((width, rows), BF16),
            two=Lazy((quarter, width), F32),
            one=Lazy((quarter, width), F32),
            inputs_own=Lazy((quarter, width), F32),
            norm_one_t=Lazy((width, rows), BF16),
            normed_t=Lazy((width, rows), BF16),
            active=Lazy((rows, units), BF16),
            gate=Lazy((count, rows, TILE), F32),
            upward=Lazy((count, rows, TILE), F32),
            gated=Lazy((rows, channels), BF16),
            projected=Lazy((rows, 3 * channels), F32),
            rim=Lazy((8, channels), F32),
            grad_b=Lazy((rows, width), BF16),
            grad_b_t=Lazy((width, rows), BF16),
            incoming=Lazy((quarter, width), F32),
        ),
        dict(
            normed=pltpu.VMEM((rows, width), BF16),
            partial=pltpu.VMEM((rows, width), BF16),
            gathered_one=pltpu.VMEM((rows, width), BF16),
            total=pltpu.VMEM((rows, width), F32),
            gated_true=pltpu.VMEM((rows, channels), BF16),
            mixed=pltpu.VMEM((rows + 8, channels), F32),
            rim_out=pltpu.VMEM((8, channels), F32),
            rim_in=pltpu.VMEM((8, channels), F32),
            m_sem=pltpu.SemaphoreType.DMA((2,)),
            **hidden_scratch(width),
            **exchange_scratch(rows, width),
        ),
        1,
        60,
        6 * rows * width * units,
    )


class Pump:
    def __init__(self, rings, ready):
        self.rings, self.ready = rings, list(ready)
        self.step = [0] * len(rings.segments)
        self.before = None

    def run(self, number):
        for _ in range(number):
            left = [s for s in self.ready if self.step[s] <= self.rings.steps]
            if not left:
                return
            seg = min(left, key=lambda s: (s == self.before, self.step[s], s))
            self.rings.unit(seg, self.step[seg])
            self.step[seg] += 1
            self.before = seg

    def rest(self):
        self.run(len(self.step) * (self.rings.steps + 1))


def first_backward(
    lefts, rights, grad_two_b, down, gate_up_t, gate, upward, one, grad_two, conv_out,
    conv_in_t, projected, rim, kernel, inputs, gains, small, devices,
):
    rows, width = grad_two_b.shape
    units = down.shape[0]
    channels = conv_out.shape[0]
    quarter = rows // 4
    block = width // devices
    sides = piece_sides(width, devices)
    grad_three_t, normed_attn_t, grad_two_t, norm_one_t, normed_conv_t = lefts
    attended, grad_query, grad_kv, active, gated = rights
    columns, kv_columns = grad_query.shape[1], grad_kv.shape[1]
    widths = [channels + columns + kv_columns, units, *joined_widths(units), 4 * channels]
    bits = []
    bit = 1
    while bit < devices:
        bits.append(bit)
        bit *= 2
    stages = 2 + len(bits)
    size = TILE // 2
    tiles = [(at, min(size, units - at)) for at in range(0, units, size)]

    def body(r):
        me = lax.axis_index("dp")
        index = lax.axis_index("tensor")
        place = lax.rem(me, SPAN)

        done = []

        def store(seg, column, value):
            if seg == 0:
                at = (0, channels, channels + columns).index(column)
                if at == 2:
                    r.sum_kv[:, 0, :] = value[:, : kv_columns // 2]
                    r.sum_kv[:, 1, :] = value[:, kv_columns // 2 :]
                else:
                    (r.sum_attn_out, r.sum_query)[at][...] = value
                r.flush((r.sum_attn_out, r.sum_query, r.sum_kv)[at])
            elif seg == 1:
                r.sum_down[...] = value
                r.flush(r.sum_down)
            elif seg < 4:
                store_joined(r.sum_gate_up, seg - 2, value, units)
                done.append(seg)
                if len(done) == 2:
                    r.flush(r.sum_gate_up)
            elif column == 0:
                r.sum_conv_out[...] = value
                r.flush(r.sum_conv_out)
            else:
                for at in range(3):
                    r.sum_conv_in[at] = value[:, at * channels : (at + 1) * channels]
                r.flush(r.sum_conv_in)

        rings = Rings(
            devices, sides,
            [
                [
                    (r.grad_three_t, r.attended),
                    (r.normed_attn_t, r.grad_query),
                    (r.normed_attn_t, r.grad_kv),
                ],
                [(r.grad_two_t, r.active)],
            ]
            + joined_segments(r.norm_one_t, r.joined, units)
            + [[(r.grad_one_t, r.gated), (r.normed_conv_t, r.grad_projected)]],
            [r.held0, r.held1, r.held2, r.held3, r.held4], r.r_send, r.r_recv, r.r_credit, store,
        )
        pump = Pump(rings, [0, 1])
        small_peers = tensor_peers() + [dict(dp=me ^ bit) for bit in bits]
        greet(rings.peers() + small_peers + span_peers())

        def fetch(number):
            at, wide = tiles[number]
            slot = number % 2
            pairs = [
                (r.down.at[at : at + wide, :], r.down_tile.at[slot, 0:wide, :]),
                (r.gate.at[at // TILE, :, pl.ds(at % TILE, size)], r.gate_tile.at[slot]),
                (r.upward.at[at // TILE, :, pl.ds(at % TILE, size)], r.up_tile.at[slot]),
            ]
            return [
                pltpu.make_async_copy(a, b, r.h_sem.at[slot, k]) for k, (a, b) in enumerate(pairs)
            ]

        def fetch_conv(number):
            slot = number % 2
            return [
                pltpu.make_async_copy(
                    r.conv_in_t.at[k, pl.ds(number * size, size), :],
                    r.conv_tile.at[slot, k],
                    r.c_sem.at[slot, k],
                )
                for k in range(3)
            ]

        def main():
            first = pltpu.make_async_copy(r.grad_two_b, r.gathered, r.e_sem)
            first.start()
            for copy in fetch(0):
                copy.start()
            first.wait()
            for number, (at, wide) in enumerate(tiles):
                if number + 1 < len(tiles):
                    for copy in fetch(number + 1):
                        copy.start()
                for copy in fetch(number):
                    copy.wait()
                slot = number % 2
                grad = cross(r.gathered[...], r.down_tile[slot, 0:wide, :])
                gates, ups = r.gate_tile[slot, :, 0:wide], r.up_tile[slot, :, 0:wide]
                sigma = jax.nn.sigmoid(gates)
                grad_gate = (grad * ups * sigma * (1.0 + gates * (1.0 - sigma))).astype(BF16)
                grad_up = (grad * gates * sigma).astype(BF16)
                put_joined(r.joined, number, size, (grad_gate, grad_up), units)
                if number % 3 == 2:
                    yield 1
            r.need(r.norm_one_t, r.one, r.grad_two)
            pump.ready += [2, 3]
            yield 2
            yield from stream_product(r, r.joined, r.gate_up_t, joined_parts(units), r.partial)
            yield from sum_and_gather(
                r, r.partial, r.gathered, r.grad_one_t,
                lambda total, at, first: back_rows(
                    total, at, first, r.one, r.gains[1:2, :], r.grad_two, r.grad_one, r.gain_term
                ),
            )
            r.small_out[...] = r.small[...]
            r.small_out[1:2, :] = r.gain_term[...]

            r.need(r.conv_out, r.projected, r.rim, r.gated, r.normed_conv_t, r.inputs)
            made = cross(r.gathered[...], r.conv_out[...])
            for at, owner in enumerate(block_owners(index)):
                start = pl.multiple_of(owner * quarter, quarter)
                r.grad_gated[pl.ds(start, quarter), :] = made[at * quarter : (at + 1) * quarter]
            before = r.projected[:, :channels]
            signal = r.projected[:, 2 * channels :]
            taps = r.kernel[...].astype(F32)
            pad = 8
            r.mixed[pad:, :] = before * signal
            r.mixed[0:pad, :] = r.rim[...]
            grad_gated = r.grad_gated[...]
            r.grad_conv[0:rows, :] = grad_gated * r.projected[:, channels : 2 * channels]
            r.grad_conv[rows:, :] = jnp.zeros_like(r.grad_conv[rows:, :])
            r.rim_out[...] = r.grad_conv[0:pad, :]
            rim_copy = remote(r.rim_out, r.rim_in, r.m_sem.at[0], r.m_sem.at[1], dict(dp=me - 1))

            @pl.when(place > 0)
            def _():
                rim_copy.start()

            yield 1
            convolved = None
            for k in range(KW):
                shifted = r.mixed[pad - KW + 1 + k : pad - KW + 1 + k + rows, :]
                term = taps[k : k + 1, :] * shifted
                convolved = term if convolved is None else convolved + term
                term = jnp.sum(r.grad_conv[0:rows, :] * shifted, axis=0, keepdims=True)
                r.small_out[5 + k : 6 + k, 0:channels] = term
            r.grad_projected[:, channels : 2 * channels] = (grad_gated * convolved).astype(BF16)

            @pl.when(place < SPAN - 1)
            def _():
                rim_copy.wait_recv()
                r.grad_conv[rows:, :] = r.rim_in[...]

            grad_mixed = None
            for k in range(KW):
                term = taps[k : k + 1, :] * r.grad_conv[KW - 1 - k : KW - 1 - k + rows, :]
                grad_mixed = term if grad_mixed is None else grad_mixed + term
            r.grad_projected[:, :channels] = (grad_mixed * signal).astype(BF16)
            r.grad_projected[:, 2 * channels :] = (grad_mixed * before).astype(BF16)

            @pl.when(place > 0)
            def _():
                rim_copy.wait_send()

            pump.ready += [4]
            yield 2
            for copy in fetch_conv(0):
                copy.start()
            for number in range(width // size):
                if number + 1 < width // size:
                    for copy in fetch_conv(number + 1):
                        copy.start()
                for copy in fetch_conv(number):
                    copy.wait()
                for at, owner in enumerate(block_owners(index)):
                    start = pl.multiple_of(owner * quarter, quarter)
                    made = None
                    for k in range(3):
                        piece = r.grad_projected[
                            pl.ds(start, quarter), k * channels : (k + 1) * channels
                        ]
                        term = cross(piece, r.conv_tile[number % 2, k])
                        made = term if made is None else made + term
                    r.partial[
                        at * quarter : (at + 1) * quarter, number * size : (number + 1) * size
                    ] = made.astype(BF16)
                if number % 2:
                    yield 1
            yield from sum_and_gather(
                r, r.partial, r.input_grad, None,
                lambda total, at, first: back_rows(
                    total, at, first, r.inputs, r.gains[0:1, :], r.grad_one, None, r.gain_term
                ),
            )
            out_copies = []
            small_rows = quarter // 2
            for at in range(8):
                start = pl.multiple_of(block_owners(index)[at // 2] * quarter + at % 2 * small_rows, 8)
                if at >= 2:
                    out_copies[at - 2].wait()
                r.final[at % 2] = r.input_grad[at * small_rows : (at + 1) * small_rows, :].astype(F32)
                out_copies.append(
                    pltpu.make_async_copy(
                        r.final.at[at % 2], r.result.at[pl.ds(start, small_rows), :], r.g_sem.at[at]
                    )
                )
                out_copies[-1].start()
            for copy in out_copies[-2:]:
                copy.wait()
            r.small_out[0:1, :] = r.gain_term[...]
            row = lax.broadcasted_iota(jnp.int32, small.shape, 0)
            for stage in range(stages):
                copy = remote(
                    r.small_out, r.slots.at[stage], r.s_send.at[stage], r.s_recv.at[stage],
                    small_peers[stage],
                )
                copy.start()
                yield 1
                copy.wait()
                if stage < 2:
                    r.small_out[...] += jnp.where(row < 5, r.slots[stage], 0.0)
                else:
                    r.small_out[...] += r.slots[stage]
            r.flush(r.small_out)

        r.need(r.grad_three_t, r.attended, r.normed_attn_t, r.grad_query, r.grad_kv)
        pump.run(1)
        r.need(r.grad_two_t, r.active)
        pump.run(1)
        for number in main():
            pump.run(number)
        pump.rest()

    return run_kernel(
        body,
        dict(
            grad_three_t=Lazy(grad_three_t),
            attended=Lazy(attended),
            normed_attn_t=Lazy(normed_attn_t),
            grad_query=Lazy(grad_query),
            grad_kv=Lazy(grad_kv),
            grad_two_t=Lazy(grad_two_t),
            active=Lazy(active),
            norm_one_t=Lazy(norm_one_t),
            one=Lazy(one),
            grad_two=Lazy(grad_two),
            conv_out=Lazy(conv_out),
            projected=Lazy(projected),
            rim=Lazy(rim),
            gated=Lazy(gated),
            normed_conv_t=Lazy(normed_conv_t),
            inputs=Lazy(inputs),
            grad_two_b=(grad_two_b, pl.ANY),
            down=(down, pl.ANY),
            gate_up_t=(gate_up_t, pl.ANY),
            gate=(gate, pl.ANY),
            upward=(upward, pl.ANY),
            conv_in_t=(conv_in_t, pl.ANY),
            kernel=kernel,
            gains=gains,
            small=small,
        ),
        dict(
            result=((rows, width), F32, pl.ANY),
            small_out=Lazy(small.shape, F32),
            sum_attn_out=Lazy((block, channels), F32),
            sum_query=Lazy((block, columns), F32),
            sum_kv=Lazy((block, 2, kv_columns // 2), F32),
            sum_down=Lazy((block, units), F32),
            sum_gate_up=Lazy((block, 2, units), F32),
            sum_conv_out=Lazy((block, channels), F32),
            sum_conv_in=Lazy((3, block, channels), F32),
        ),
        dict(
            gathered=pltpu.VMEM((rows, width), BF16),
            partial=pltpu.VMEM((rows, width), BF16),
            grad_one_t=pltpu.VMEM((width, rows), BF16),
            grad_one=pltpu.VMEM((quarter, width), F32),
            joined=pltpu.VMEM((rows, 2 * units), BF16),
            input_grad=pltpu.VMEM((rows, width), BF16),
            final=pltpu.VMEM((2, quarter // 2, width), F32),
            g_sem=pltpu.SemaphoreType.DMA((8,)),
            grad_projected=pltpu.VMEM((rows, 3 * channels), BF16),
            grad_gated=pltpu.VMEM((rows, channels), F32),
            mixed=pltpu.VMEM((rows + 8, channels), F32),
            grad_conv=pltpu.VMEM((rows + 8, channels), F32),
            rim_out=pltpu.VMEM((8, channels), F32),
            rim_in=pltpu.VMEM((8, channels), F32),
            m_sem=pltpu.SemaphoreType.DMA((2,)),
            e_sem=pltpu.SemaphoreType.DMA,
            down_tile=pltpu.VMEM((2, size, width), BF16),
            gate_tile=pltpu.VMEM((2, rows, size), F32),
            up_tile=pltpu.VMEM((2, rows, size), F32),
            h_sem=pltpu.SemaphoreType.DMA((2, 3)),
            conv_tile=pltpu.VMEM((2, 3, size, channels), BF16),
            c_sem=pltpu.SemaphoreType.DMA((2, 3)),
            gain_term=pltpu.VMEM((1, width), F32),
            slots=pltpu.VMEM((stages,) + small.shape, F32),
            s_send=pltpu.SemaphoreType.DMA((stages,)),
            s_recv=pltpu.SemaphoreType.DMA((stages,)),
            **stream_scratch(2 * units, 128),
            **exchange_scratch(rows, width),
            **ring_scratch(devices, sides, block, widths),
        ),
        4,
        62,
        2 * rows * width * sum(widths) * 3,
    )


def assemble(arrays):
    count = len(arrays)

    def body(*refs):
        held, arrive, leave = refs[2 * count : 3 * count], refs[-2], refs[-1]
        first = [
            pltpu.make_async_copy(refs[at], held[at], arrive.at[at]) for at in range(count)
        ]
        second = [
            pltpu.make_async_copy(held[at], refs[count + at], leave.at[at]) for at in range(count)
        ]
        for copy in first:
            copy.start()
        for one, two in zip(first, second):
            one.wait()
            two.start()
        for copy in second:
            copy.wait()

    return pl.pallas_call(
        body,
        in_specs=[pl.BlockSpec(memory_space=pl.ANY)] * count,
        out_specs=[pl.BlockSpec(memory_space=pl.ANY)] * count,
        out_shape=[jax.ShapeDtypeStruct(a.shape, a.dtype) for a in arrays],
        scratch_shapes=[pltpu.VMEM(a.shape, a.dtype) for a in arrays]
        + [pltpu.SemaphoreType.DMA((count,))] * 2,
        compiler_params=pltpu.CompilerParams(vmem_limit_bytes=60 * 2**20),
    )(*arrays)


def local(
    tokens,
    lengths,
    norm_conv,
    conv_in,
    conv_kernel,
    conv_out,
    norm_mlp_one,
    gate_up_one,
    down_one,
    norm_attn,
    query_weight,
    kv_weight,
    query_gain,
    key_gain,
    attn_out,
    norm_mlp_two,
    gate_up_two,
    down_two,
    cotangent,
):
    row_count = tokens.shape[0]
    width = tokens.shape[1]
    quarter = row_count // 4
    local_kv = kv_weight.shape[2] // HEAD
    device = lax.axis_index("dp")
    devices = lax.axis_size("dp")
    index = lax.axis_index("tensor")
    place_index = device % SPAN
    offsets = jnp.concatenate(
        [o * quarter + jnp.arange(quarter, dtype=jnp.int32) for o in block_owners(index)]
    )
    positions = place_index * row_count + offsets
    gains = jnp.concatenate([norm_conv, norm_mlp_one, norm_attn, norm_mlp_two]).reshape(4, width)
    head_gains = jnp.stack([query_gain, key_gain], axis=1)
    frequency = THETA ** (-2.0 * jnp.arange(HEAD // 2, dtype=jnp.float32) / HEAD)
    angles = frequency[:, None] * positions.astype(jnp.float32)[None, :]
    tables = (jnp.cos(angles), jnp.sin(angles))
    gate_up_one_t = jnp.transpose(gate_up_one, (1, 2, 0))
    gate_up_two_t = jnp.transpose(gate_up_two, (1, 2, 0))
    conv_in_t = jnp.transpose(conv_in, (1, 0, 2))
    kv_flat = kv_weight.reshape(width, 2 * local_kv * HEAD)

    (
        normed_attn_b,
        normed_attn_t,
        two_own,
        one_own,
        inputs_own,
        norm_one_t,
        normed_conv_t,
        active_one,
        gate_one,
        up_one,
        gated_b,
        projected,
        rim,
        grad_b,
        grad_b_t,
        incoming,
    ) = first_forward(
        tokens, cotangent, conv_in_t, conv_kernel, conv_out, gate_up_one_t, down_one, gains, lengths
    )
    (
        active_two,
        joined_two,
        norm_two_t,
        three_own,
        *kept,
        attended_b,
        attended_t,
        log_total,
    ) = attention_forward(
        normed_attn_b,
        query_weight,
        kv_flat,
        head_gains,
        attn_out,
        two_own,
        tables,
        gains,
        lengths,
        gate_up_two_t,
        down_two,
        grad_b,
    )
    kept = (*kept, attended_t, log_total)
    (
        grad_three_t,
        grad_query,
        grad_kv,
        grad_two_b,
        grad_two_t,
        grad_two,
        small,
        sum_down_two,
        sum_gate_up_two,
        output,
    ) = attention_backward(
        grad_b_t,
        norm_two_t,
        active_two,
        joined_two,
        gate_up_two_t,
        down_two,
        three_own,
        incoming,
        kept,
        attn_out,
        query_weight,
        kv_flat,
        head_gains,
        two_own,
        tables,
        gains,
        lengths,
        devices,
    )

    (
        grad_inputs,
        small,
        sum_attn_out,
        sum_query,
        sum_kv,
        sum_down_one,
        sum_gate_up_one,
        sum_conv_out,
        sum_conv_in,
    ) = first_backward(
        [grad_three_t, normed_attn_t, grad_two_t, norm_one_t, normed_conv_t],
        [attended_b, grad_query, grad_kv, active_one, gated_b],
        grad_two_b,
        down_one,
        gate_up_one_t,
        gate_one,
        up_one,
        one_own,
        grad_two,
        conv_out,
        conv_in_t,
        projected,
        rim,
        conv_kernel,
        inputs_own,
        gains,
        small,
        devices,
    )
    out_rows = width // devices
    (
        output, grad_inputs, sum_conv_in, sum_conv_out, sum_gate_up_one, sum_down_one, sum_query, sum_kv,
        sum_attn_out, sum_gate_up_two, sum_down_two,
    ) = assemble(
        [
            output, grad_inputs, jnp.reshape(sum_conv_in, (-1, sum_conv_in.shape[2])), sum_conv_out,
            sum_gate_up_one, sum_down_one, sum_query, sum_kv, sum_attn_out, sum_gate_up_two, sum_down_two,
        ]
    )
    sum_conv_in = sum_conv_in.reshape(3, -1, sum_conv_in.shape[1])
    return (
        output,
        grad_inputs,
        small[0],
        jnp.transpose(sum_conv_in, (1, 0, 2)),
        small[5:, : conv_out.shape[0]],
        sum_conv_out.T,
        small[1],
        sum_gate_up_one,
        sum_down_one.T,
        small[2],
        sum_query,
        sum_kv,
        small[4, :HEAD],
        small[4, HEAD : 2 * HEAD],
        sum_attn_out.T,
        small[3],
        sum_gate_up_two,
        sum_down_two.T,
    )


def solution(mesh):
    in_specs = (
        P("dp", None),
        P(),
        P(),
        P(None, None, "tensor"),
        P(None, "tensor"),
        P("tensor", None),
        P(),
        P(None, None, "tensor"),
        P("tensor", None),
        P(),
        P(None, "tensor"),
        P(None, None, "tensor"),
        P(),
        P(),
        P("tensor", None),
        P(),
        P(None, None, "tensor"),
        P("tensor", None),
        P("dp", None),
    )
    out_specs = (
        P("dp", None),
        P("dp", None),
        P(),
        P("dp", None, "tensor"),
        P(None, "tensor"),
        P("tensor", "dp"),
        P(),
        P("dp", None, "tensor"),
        P("tensor", "dp"),
        P(),
        P("dp", "tensor"),
        P("dp", None, "tensor"),
        P(),
        P(),
        P("tensor", "dp"),
        P(),
        P("dp", None, "tensor"),
        P("tensor", "dp"),
    )
    return jax.shard_map(local, mesh=mesh, in_specs=in_specs, out_specs=out_specs, check_vma=False)
```

```python
import jax
import jax.numpy as jnp
from jax import lax
from jax.experimental import pallas as pl
from jax.experimental.pallas import tpu as pltpu
from jax.sharding import PartitionSpec as P

HEAD = 64
KW = 3
SPAN = 4
GROUP = 3


EPSILON = 1e-05
THETA = 1000000.0
BF16 = jnp.bfloat16
F32 = jnp.float32


def matmul(left, right):
    return jnp.dot(left, right, preferred_element_type=F32)


def inner_back(left, right):
    return lax.dot_general(left, right, (((1,), (1,)), ((), ())), preferred_element_type=F32)


def normalize(values, gain):
    inverse = lax.rsqrt(jnp.mean(values * values, axis=-1, keepdims=True) + EPSILON)
    return (values * inverse * gain, inverse)


def normalize_back(values, inverse, gain, grad_result):
    weighted = grad_result * gain
    grad_gain = jnp.sum(grad_result * values * inverse, axis=tuple(range(values.ndim - 1)))
    inner = jnp.mean(weighted * values, axis=-1, keepdims=True)
    grad_values = inverse * (weighted - values * inverse * inverse * inner)
    return (grad_values, grad_gain)


CHUNKS = 4
SLOTS = 3
MESH = pl.DeviceIdType.MESH


class Lazy:
    def __init__(self, value, dtype=None):
        self.value, self.dtype = value, dtype


class Refs:
    def __init__(self, names, refs):
        self.__dict__.update(zip(names, refs))

    def begin(self, inputs, outputs, refs):
        self.arriving, self.leaving, self.homes = {}, [], {}
        for at, name in enumerate(inputs):
            ref = self.__dict__[name]
            copy = pltpu.make_async_copy(refs[at], ref, self.lazy_in.at[at])
            copy.start()
            self.arriving[id(ref)] = copy
        for at, name in enumerate(outputs):
            self.homes[id(self.__dict__[name])] = (refs[len(inputs) + at], at)

    def need(self, *refs):
        for ref in refs:
            self.arriving.pop(id(ref)).wait()

    def flush(self, *refs):
        for ref in refs:
            home, at = self.homes.pop(id(ref))
            copy = pltpu.make_async_copy(ref, home, self.lazy_out.at[at, 0])
            copy.start()
            self.leaving.append(copy)

    def flush_blocks(self, ref, owners):
        home, at = self.homes.pop(id(ref))
        rows = ref.shape[0] // 4
        for block, owner in enumerate(owners):
            copy = pltpu.make_async_copy(
                ref.at[pl.ds(block * rows, rows)],
                home.at[pl.ds(pl.multiple_of(owner * rows, rows), rows)],
                self.lazy_out.at[at, block],
            )
            copy.start()
            self.leaving.append(copy)

    def end(self):
        assert not self.homes
        for copy in list(self.arriving.values()) + self.leaving:
            copy.wait()


def run_kernel(body, inputs, outputs, scratch, collective_id, limit, flops):
    arrays, specs, names, out_names = [], [], [], []
    scratch = dict(scratch)
    lazy_in = [name for name, value in inputs.items() if isinstance(value, Lazy)]
    lazy_out = [name for name, value in outputs.items() if isinstance(value, Lazy)]
    for name, value in inputs.items():
        if isinstance(value, Lazy):
            array, space = value.value, pl.ANY
            scratch[name] = pltpu.VMEM(array.shape, array.dtype)
            names.append(None)
        else:
            array, space = value if isinstance(value, tuple) else (value, pltpu.VMEM)
            names.append(name)
        arrays.append(array)
        specs.append(pl.BlockSpec(memory_space=space))
    shapes, out_specs = [], []
    for name, value in outputs.items():
        if isinstance(value, Lazy):
            shape, dtype, space = value.value, value.dtype, pl.ANY
            scratch[name] = pltpu.VMEM(shape, dtype)
            names.append(None)
        else:
            shape, dtype, space = value if len(value) == 3 else (*value, pltpu.VMEM)
            names.append(name)
        shapes.append(jax.ShapeDtypeStruct(shape, dtype))
        out_specs.append(pl.BlockSpec(memory_space=space))
    scratch["lazy_in"] = pltpu.SemaphoreType.DMA((max(len(lazy_in), 1),))
    scratch["lazy_out"] = pltpu.SemaphoreType.DMA((max(len(lazy_out), 1), 4))
    names += list(scratch)

    def whole(*refs):
        r = Refs([n for n in names if n], [ref for n, ref in zip(names, refs) if n])
        r.begin(lazy_in, lazy_out, [ref for n, ref in zip(names, refs) if not n])
        body(r)
        r.end()

    return pl.pallas_call(
        whole,
        in_specs=specs,
        out_specs=out_specs,
        out_shape=shapes,
        scratch_shapes=list(scratch.values()),
        compiler_params=pltpu.CompilerParams(
            collective_id=collective_id, has_side_effects=True, vmem_limit_bytes=limit * 2**20
        ),
        cost_estimate=pl.CostEstimate(
            flops=flops,
            bytes_accessed=sum(a.size * a.dtype.itemsize for a in arrays),
            transcendentals=0,
        ),
    )(*arrays)


def greet(peers):
    barrier = pltpu.get_barrier_semaphore()
    for peer in peers:
        pl.semaphore_signal(barrier, inc=1, device_id=peer, device_id_type=MESH)
    pl.semaphore_wait(barrier, len(peers))


def tensor_peers():
    me = lax.axis_index("tensor")
    return [dict(tensor=me ^ 1), dict(tensor=me ^ 2)]


def span_peers():
    me = lax.axis_index("dp")
    place = lax.rem(me, SPAN)
    return [dict(dp=me - place + lax.rem(place + k, SPAN)) for k in range(1, SPAN)]


def remote(src, dst, send, recv, peer):
    return pltpu.make_async_remote_copy(
        src_ref=src, dst_ref=dst, send_sem=send, recv_sem=recv, device_id=peer, device_id_type=MESH
    )


def exchange_scratch(rows, width):
    quarter = rows // 4
    return dict(
        near_rows=pltpu.VMEM((2 * quarter, width), BF16),
        across_rows=pltpu.VMEM((quarter, width), BF16),
        far_rows=pltpu.VMEM((quarter, width), BF16),
        x_send=pltpu.SemaphoreType.DMA((6 * CHUNKS,)),
        x_recv=pltpu.SemaphoreType.DMA((6 * CHUNKS,)),
    )


def sum_and_gather(r, partial, gathered, gathered_t, compute):
    near, across, far = r.near_rows, r.across_rows, r.far_rows
    core, other = tensor_peers()
    quarter = partial.shape[0] // 4
    size = quarter // CHUNKS
    copies = {}

    def copy(kind, at, src, dst, peer):
        number = kind * CHUNKS + at
        copies[kind, at] = remote(src, dst, r.x_send.at[number], r.x_recv.at[number], peer)
        copies[kind, at].start()

    def part(block, at):
        return pl.ds(block * quarter + at * size, size)

    def turn(block):
        if gathered_t is not None:
            rows = slice(block * quarter, (block + 1) * quarter)
            gathered_t[:, rows] = gathered[rows, :].T

    for at in range(CHUNKS):
        copy(0, at, partial.at[part(3, at)], near.at[part(1, at)], core)
    for at in range(CHUNKS):
        copy(1, at, partial.at[part(2, at)], near.at[part(0, at)], core)
    for at in range(CHUNKS):
        copies[0, at].wait_recv()
        far[part(0, at), :] = (
            partial[part(1, at), :].astype(F32) + near[part(1, at), :].astype(F32)
        ).astype(BF16)
        copy(2, at, far.at[part(0, at)], across.at[part(0, at)], other)
    yield 1
    for at in range(CHUNKS):
        copies[1, at].wait_recv()
        copies[2, at].wait_recv()
        total = (
            partial[part(0, at), :].astype(F32)
            + near[part(0, at), :].astype(F32)
            + across[part(0, at), :].astype(F32)
        )
        gathered[part(0, at), :] = compute(total, part(0, at), at == 0)
        copy(3, at, gathered.at[part(0, at)], gathered.at[part(1, at)], other)
        copy(4, at, gathered.at[part(0, at)], gathered.at[part(2, at)], core)
    turn(0)
    yield 1
    for at in range(CHUNKS):
        copies[3, at].wait_recv()
        copy(5, at, gathered.at[part(1, at)], gathered.at[part(3, at)], core)
    turn(1)
    for at in range(CHUNKS):
        copies[4, at].wait_recv()
    turn(2)
    for at in range(CHUNKS):
        copies[5, at].wait_recv()
    turn(3)
    for made in copies.values():
        made.wait_send()
    yield 1


def exhaust(main):
    for _ in main:
        pass


def norm_rows(total, rows, residual, gain, hidden):
    values = residual[rows, :] + total
    hidden[rows, :] = values
    return normalize(values, gain)[0].astype(BF16)


def back_rows(total, rows, first, hidden, gain, incoming, own, grad_gain):
    values = hidden[rows, :]
    inverse = lax.rsqrt(jnp.mean(values * values, axis=-1, keepdims=True) + EPSILON)
    made, term = normalize_back(values, inverse, gain, total)
    made = made + incoming[rows, :]
    if own is not None:
        own[rows, :] = made
    term = term.reshape(1, -1)
    grad_gain[...] = term if first else grad_gain[...] + term
    return made.astype(BF16)


def ring_peers(count):
    me = lax.axis_index("dp")
    even = lax.rem(me, 2) == 0
    place = jnp.where(even, me // 2, count - 1 - me // 2)

    def at(position):
        position = lax.rem(position + count, count)
        return jnp.where(position < count // 2, 2 * position, 2 * (count - 1 - position) + 1)

    return at(place + 1), at(place - 1), lambda distance: at(place + distance)


class Rings:
    def __init__(self, devices, sides, segments, held, send, recv, credit, store):
        self.devices, self.sides, self.segments, self.held = devices, sides, segments, held
        self.send, self.recv, self.credit, self.store = send, recv, credit, store
        self.rows = segments[0][0][0].shape[0] // devices
        self.half = self.rows // sides
        self.steps = devices - 1
        self.following, self.previous, self.owner_at = ring_peers(devices)

    def peers(self):
        return [dict(dp=self.following), dict(dp=self.previous)]

    def copy(self, seg, side, step):
        number = (seg * self.sides + side) * self.steps + step
        return remote(
            self.held[seg].at[side, step % SLOTS],
            self.held[seg].at[side, (step + 1) % SLOTS],
            self.send.at[number],
            self.recv.at[number],
            dict(dp=self.following if side == 0 else self.previous),
        )

    def unit(self, seg, step):
        sides, half, steps = self.sides, self.half, self.steps
        last = step == steps
        slot = step % SLOTS
        starts = []
        for side in range(sides):
            if last:
                owner = lax.axis_index("dp")
            else:
                owner = self.owner_at(-1 - step if side == 0 else 1 + step)
            starts.append(pl.multiple_of(owner * self.rows + side * half, 16))
        if step:
            for side in range(sides):
                self.copy(seg, side, step - 1).wait_send()
                if step <= steps + 1 - SLOTS:
                    pl.semaphore_signal(
                        self.credit.at[seg * sides + side],
                        inc=1,
                        device_id=dict(dp=self.previous if side == 0 else self.following),
                        device_id_type=MESH,
                    )
                self.copy(seg, side, step - 1).wait_recv()
        column = 0
        for left, right in self.segments[seg]:
            pieces = [left[pl.ds(start, half), :] for start in starts]
            piece = pieces[0] if sides == 1 else jnp.concatenate(pieces, axis=0)
            made = jnp.dot(piece, right[...], preferred_element_type=F32)
            at = slice(column, column + made.shape[1])
            values = []
            for side in range(sides):
                value = made[side * half : (side + 1) * half]
                if step:
                    value = value + self.held[seg][side, slot, :, at].astype(F32)
                if last:
                    values.append(value)
                else:
                    self.held[seg][side, slot, :, at] = value.astype(BF16)
            if last:
                self.store(seg, column, values[0] if sides == 1 else jnp.concatenate(values, axis=0))
            column += made.shape[1]
        if not last:
            for side in range(sides):
                if step >= SLOTS - 1:
                    pl.semaphore_wait(self.credit.at[seg * sides + side], 1)
                self.copy(seg, side, step).start()


def ring_scratch(devices, sides, rows, widths):
    copies = len(widths) * sides * (devices - 1)
    made = {
        f"held{at}": pltpu.VMEM((sides, SLOTS, rows // sides, w), BF16)
        for at, w in enumerate(widths)
    }
    made["r_send"] = pltpu.SemaphoreType.DMA((copies,))
    made["r_recv"] = pltpu.SemaphoreType.DMA((copies,))
    made["r_credit"] = pltpu.SemaphoreType.REGULAR((len(widths) * sides,))
    return made


def interleave(main, units, first):
    units = iter(units)

    def some(number):
        for _ in range(number):
            unit = next(units, None)
            if unit is not None:
                unit()

    some(first)
    for number in main:
        some(number)
    for unit in units:
        unit()


def piece_sides(width, devices):
    return 2 if width // devices % 32 == 0 else 1


def block_owners(index):
    return [index, index ^ 2, index ^ 1, index ^ 3]


def cross(left, right):
    return lax.dot_general(left, right, (((1,), (1,)), ((), ())), preferred_element_type=F32)


def turn_t(values, cosine, sine, back):
    middle = HEAD // 2
    low, high = values[:middle], values[middle:]
    if back:
        return jnp.concatenate([low * cosine + high * sine, high * cosine - low * sine], axis=0)
    return jnp.concatenate([low * cosine - high * sine, high * cosine + low * sine], axis=0)


def head_norm_t(values, gain):
    inverse = lax.rsqrt(jnp.mean(values * values, axis=0, keepdims=True) + EPSILON)
    return values * inverse * gain


def head_back_t(values, gain, grad):
    inverse = lax.rsqrt(jnp.mean(values * values, axis=0, keepdims=True) + EPSILON)
    weighted = grad * gain
    inner = jnp.mean(weighted * values, axis=0, keepdims=True)
    return inverse * (weighted - values * inverse * inverse * inner), grad * values * inverse


def block_positions(block, quarter, shape, axis):
    place = lax.rem(lax.axis_index("dp"), SPAN)
    owner = block_owners(lax.axis_index("tensor"))[block]
    start = (place * 4 + owner) * quarter
    return start + lax.broadcasted_iota(jnp.int32, shape, axis)


def own_length(r):
    return r.lengths[lax.axis_index("dp") // SPAN]


def fill_bias(r):
    quarter = r.bias.shape[0] // 4
    shape = (quarter, quarter)
    for row in range(4):
        keys = block_positions(row, quarter, shape, 0)
        live = keys < own_length(r)
        for column in range(4):
            allowed = live & (keys <= block_positions(column, quarter, shape, 1))
            at = slice(row * quarter, (row + 1) * quarter)
            r.bias[at, column * quarter : (column + 1) * quarter] = jnp.where(allowed, 0.0, -1e30)


def head_rows(head):
    return slice(head * HEAD, (head + 1) * HEAD)


def attention_forward(
    normed_b, query_weight, kv_weight, head_gains, attn_out, residual, tables, gains, lengths,
    gate_up_t, down, grad_b,
):
    rows, width = normed_b.shape
    columns = query_weight.shape[1]
    kv_columns = kv_weight.shape[1] // 2
    heads, kv_heads = columns // HEAD, kv_columns // HEAD
    units = down.shape[0]

    def body(r):
        me = lax.axis_index("dp")
        place = lax.rem(me, SPAN)
        greet(tensor_peers() + span_peers())
        for copy in hidden_fetch(r, 0, TILE):
            copy.start()

        def pass_on(distance):
            return remote(
                r.own, r.near.at[distance - 1], r.p_send.at[distance - 1], r.p_recv.at[distance - 1],
                dict(dp=me + distance),
            )

        r.need(r.normed, r.kv_weight, r.cosine, r.sine)
        cosine, sine = r.cosine[...], r.sine[...]
        made = jnp.dot(r.normed[...], r.kv_weight[...], preferred_element_type=F32)
        r.key_raw[...] = made[:, :kv_columns].T
        r.own[:, kv_columns:] = made[:, kv_columns:].astype(BF16)
        for group in range(kv_heads):
            keys = head_norm_t(r.key_raw[head_rows(group), :], r.head_gains[:, 1:2])
            r.keys_t[head_rows(group), :] = turn_t(keys, cosine, sine, False).astype(BF16)
        r.own[:, :kv_columns] = r.keys_t[...].T
        for distance in range(1, SPAN):

            @pl.when(place + distance < SPAN)
            def _():
                pass_on(distance).start()

        r.need(r.query_weight)
        made = jnp.dot(r.normed[...], r.query_weight[...], preferred_element_type=F32)
        r.query_raw[...] = made.T
        for head in range(heads):
            query = head_norm_t(r.query_raw[head_rows(head), :], r.head_gains[:, 0:1])
            query = turn_t(query, cosine, sine, False).astype(BF16)
            r.query[head_rows(head), :] = query * jnp.asarray(HEAD ** (-0.5), BF16)
        fill_bias(r)

        def part(piece, first):
            for group in range(kv_heads):
                keys = piece[:, head_rows(group)]
                values_t = piece[:, kv_columns + group * HEAD : kv_columns + (group + 1) * HEAD].T
                for head in range(group * GROUP, (group + 1) * GROUP):
                    at = head_rows(head)
                    scores = jnp.dot(keys, r.query[at, :], preferred_element_type=F32)
                    if first:
                        scores = scores + r.bias[...]
                    expo = jnp.exp(scores)
                    total = jnp.sum(expo, axis=0, keepdims=True)
                    made = jnp.dot(values_t, expo.astype(BF16), preferred_element_type=F32)
                    if first:
                        r.total[head : head + 1, :] = total
                        r.attended_t[at, :] = made
                    else:
                        r.total[head : head + 1, :] += total
                        r.attended_t[at, :] += made

        part(r.own[...], True)

        @pl.loop(1, place + 1)
        def _(distance):
            pass_on(distance).wait_recv()
            part(r.near[distance - 1], False)

        for head in range(heads):
            at = head_rows(head)
            made = r.attended_t[at, :] / r.total[head : head + 1, :]
            r.attended_t[at, :] = made
            r.attended[:, at] = made.T.astype(BF16)
        r.log_total[...] = jnp.log(r.total[...])
        r.need(r.attn_out, r.residual, r.grad_b)
        r.flush(r.query_raw, r.key_raw, r.query, r.own, r.near, r.attended, r.attended_t, r.log_total)
        r.partial[...] = jnp.dot(
            r.attended[...], r.attn_out[...], preferred_element_type=F32
        ).astype(BF16)
        exhaust(
            sum_and_gather(
                r, r.partial, r.gathered, r.gathered_t,
                lambda total, at, first: norm_rows(total, at, r.residual, r.gains[3:4, :], r.hidden),
            )
        )
        r.flush(r.gathered_t, r.hidden)
        for distance in range(1, SPAN):

            @pl.when(place + distance < SPAN)
            def _():
                pass_on(distance).wait_send()

        def tile(number, wide, gate_w, up_w, down_w):
            lanes = tile_lanes(number, wide)
            a = cross(r.gathered[...], gate_w)
            z = cross(r.gathered[...], up_w)
            grad = cross(r.grad_b[...], down_w)
            sigma = jax.nn.sigmoid(a)
            r.active[:, lanes] = (a * sigma * z).astype(BF16)
            grad_gate = (grad * z * sigma * (1.0 + a * (1.0 - sigma))).astype(BF16)
            grad_up = (grad * a * sigma).astype(BF16)
            put_joined(r.joined, number, TILE, (grad_gate, grad_up), units)

        hidden_tiles(r, units, tile)
        r.flush(r.active, r.joined)

    return run_kernel(
        body,
        dict(
            normed=Lazy(normed_b),
            query_weight=Lazy(query_weight),
            kv_weight=Lazy(kv_weight),
            head_gains=head_gains,
            attn_out=Lazy(attn_out),
            residual=Lazy(residual),
            cosine=Lazy(tables[0]),
            sine=Lazy(tables[1]),
            gate_up_t=(gate_up_t, pl.ANY),
            down=(down, pl.ANY),
            grad_b=Lazy(grad_b),
            lengths=(lengths, pltpu.SMEM),
            gains=gains,
        ),
        dict(
            active=Lazy((rows, units), BF16),
            joined=Lazy((rows, 2 * units), BF16),
            gathered_t=Lazy((width, rows), BF16),
            hidden=Lazy(residual.shape, F32),
            query_raw=Lazy((columns, rows), F32),
            key_raw=Lazy((kv_columns, rows), F32),
            query=Lazy((columns, rows), BF16),
            own=Lazy((rows, 2 * kv_columns), BF16),
            near=Lazy((SPAN - 1, rows, 2 * kv_columns), BF16),
            attended=Lazy((rows, columns), BF16),
            attended_t=Lazy((columns, rows), F32),
            log_total=Lazy((heads, rows), F32),
        ),
        dict(
            keys_t=pltpu.VMEM((kv_columns, rows), BF16),
            bias=pltpu.VMEM((rows, rows), F32),
            total=pltpu.VMEM((heads, rows), F32),
            partial=pltpu.VMEM((rows, width), BF16),
            gathered=pltpu.VMEM((rows, width), BF16),
            **hidden_scratch(width),
            p_send=pltpu.SemaphoreType.DMA((SPAN - 1,)),
            p_recv=pltpu.SemaphoreType.DMA((SPAN - 1,)),
            **exchange_scratch(rows, width),
        ),
        2,
        58,
        16 * rows * rows * SPAN * columns,
    )


def stream_product(r, left, weights, parts, out):
    width = weights.shape[2]
    size = r.tile.shape[2]
    tiles = width // size
    depth = sum(part[3] for part in parts)

    def fetch(j):
        return [
            pltpu.make_async_copy(
                weights.at[which, pl.ds(there, count), pl.ds(j * size, size)],
                r.tile.at[j % 2, pl.ds(here, count), :],
                r.tile_sem.at[j % 2, k],
            )
            for k, (which, there, here, count) in enumerate(parts)
        ]

    for copy in fetch(0):
        copy.start()
    for j in range(tiles):
        if j + 1 < tiles:
            for copy in fetch(j + 1):
                copy.start()
        for copy in fetch(j):
            copy.wait()
        made = jnp.dot(left[...], r.tile[j % 2, 0:depth, :], preferred_element_type=F32)
        out[:, j * size : (j + 1) * size] = made.astype(BF16)
        if j % 2:
            yield 1


def stream_scratch(depth, size):
    return dict(
        tile=pltpu.VMEM((2, depth, size), BF16),
        tile_sem=pltpu.SemaphoreType.DMA((2, 4)),
    )


def attention_backward(
    grad_b_t, norm_two_t, active, joined, gate_up_t, down, three, incoming,
    kept, attn_out, query_weight, kv_weight, head_gains, two, tables, gains, lengths, devices,
):
    units, tokens_width = gate_up_t.shape[1:]
    query_raw, key_raw, query, own, near, attended_t, log_total = kept
    rows, width = active.shape[0], tokens_width
    columns = query_weight.shape[1]
    kv_columns = kv_weight.shape[1] // 2
    heads, kv_heads = columns // HEAD, kv_columns // HEAD
    sides = piece_sides(width, devices)
    block = width // devices
    segment_widths = [units] + joined_widths(units)

    def body(r):
        me = lax.axis_index("dp")
        place = lax.rem(me, SPAN)

        def store(seg, column, value):
            if seg == 0:
                r.sum_down[...] = value
                r.flush(r.sum_down)
            else:
                store_joined(r.sum_gate_up, seg - 1, value, units)
                if seg == 2:
                    r.flush(r.sum_gate_up)

        rings = Rings(
            devices, sides,
            [[(r.grad_b_t, r.active)]] + joined_segments(r.norm_two_t, r.joined, units),
            [r.held0, r.held1, r.held2], r.r_send, r.r_recv, r.r_credit, store,
        )
        greet(rings.peers() + tensor_peers() + span_peers())

        def pass_back(distance):
            return remote(
                r.far.at[distance - 1], r.arrived.at[distance - 1],
                r.p_send.at[distance - 1], r.p_recv.at[distance - 1], dict(dp=me - distance),
            )

        def part(piece, write, masked):
            for group in range(kv_heads):
                keys = piece[:, head_rows(group)]
                value_at = slice(kv_columns + group * HEAD, kv_columns + (group + 1) * HEAD)
                values = piece[:, value_at]
                keys_t = keys.T
                grad_k = grad_v = None
                for head in range(group * GROUP, (group + 1) * GROUP):
                    at = head_rows(head)
                    q, grads = r.query[at, :], r.grads[:, at]
                    scores = jnp.dot(keys, q, preferred_element_type=F32)
                    scores = scores - r.log_total[head : head + 1, :]
                    if masked:
                        scores = scores + r.bias[...]
                    probs = jnp.exp(scores)
                    made = jnp.dot(probs.astype(BF16), grads, preferred_element_type=F32)
                    grad_v = made if grad_v is None else grad_v + made
                    grad_probs = cross(values, grads)
                    grad_scores = (probs * (grad_probs - r.delta[head : head + 1, :])).astype(BF16)
                    made = cross(grad_scores, q)
                    grad_k = made if grad_k is None else grad_k + made
                    made = jnp.dot(keys_t, grad_scores, preferred_element_type=F32)
                    if masked:
                        r.grad_q_t[at, :] = made
                    else:
                        r.grad_q_t[at, :] += made
                write(head_rows(group), grad_k)
                write(value_at, grad_v)

        def main():
            yield from stream_product(r, r.joined, r.gate_up_t, joined_parts(units), r.partial)
            fill_bias(r)
            r.need(r.three, r.incoming)
            yield from sum_and_gather(
                r, r.partial, r.gathered, r.grad_three_t,
                lambda total, at, first: back_rows(
                    total, at, first, r.three, r.gains[3:4, :], r.incoming, r.grad_three, r.gain_term
                ),
            )
            r.flush(r.grad_three_t)
            r.small[...] = jnp.zeros_like(r.small)
            r.small[3:4, :] = r.gain_term[...]
            r.need(r.attn_out, r.attended_t, r.own, r.near, r.query, r.log_total)
            r.grads[...] = cross(r.gathered[...], r.attn_out[...]).astype(BF16)
            for head in range(heads):
                at = head_rows(head)
                grads_t = r.grads[:, at].astype(F32).T
                r.delta[head : head + 1, :] = jnp.sum(
                    grads_t * r.attended_t[at, :], axis=0, keepdims=True
                )
            yield 1

            def write_own(at, value):
                r.grad_own[:, at] = value

            part(r.own[...], write_own, True)

            @pl.loop(1, place + 1)
            def _(distance):
                def write_far(at, value):
                    r.far[distance - 1, :, at] = value.astype(BF16)

                part(r.near[distance - 1], write_far, False)
                pass_back(distance).start()

            yield 1
            r.need(r.cosine, r.sine, r.query_raw, r.key_raw, r.query_weight, r.kv_weight, r.two)
            cosine, sine = r.cosine[...], r.sine[...]
            terms = None
            for head in range(heads):
                at = head_rows(head)
                grad = turn_t(r.grad_q_t[at, :] * HEAD ** (-0.5), cosine, sine, True)
                made, term = head_back_t(r.query_raw[at, :], r.head_gains[:, 0:1], grad)
                terms = term if terms is None else terms + term
                r.grad_query[:, at] = made.T.astype(BF16)
            r.small[4:5, 0:HEAD] = jnp.sum(terms.T, axis=0, keepdims=True)
            yield 1
            for distance in range(1, SPAN):

                @pl.when(place + distance < SPAN)
                def _():
                    pass_back(distance).wait_recv()
                    r.grad_own[...] += r.arrived[distance - 1].astype(F32)

            terms = None
            for group in range(kv_heads):
                at = head_rows(group)
                grad = turn_t(r.grad_own[:, at].T, cosine, sine, True)
                made, term = head_back_t(r.key_raw[at, :], r.head_gains[:, 1:2], grad)
                terms = term if terms is None else terms + term
                r.grad_kv[:, at] = made.T.astype(BF16)
            r.small[4:5, HEAD : 2 * HEAD] = jnp.sum(terms.T, axis=0, keepdims=True)
            r.grad_kv[:, kv_columns:] = r.grad_own[:, kv_columns:].astype(BF16)
            r.flush(r.grad_query, r.grad_kv)
            r.partial[...] = (
                cross(r.grad_query[...], r.query_weight[...]) + cross(r.grad_kv[...], r.kv_weight[...])
            ).astype(BF16)
            yield 1
            yield from sum_and_gather(
                r, r.partial, r.grad_two_b, r.grad_two_t,
                lambda total, at, first: back_rows(
                    total, at, first, r.two, r.gains[2:3, :], r.grad_three, r.grad_two, r.gain_term
                ),
            )
            r.small[2:3, :] = r.gain_term[...]
            r.flush(r.grad_two_b, r.grad_two_t, r.grad_two, r.small)
            for distance in range(1, SPAN):

                @pl.when(place >= distance)
                def _():
                    pass_back(distance).wait_send()

            yield from stream_product(r, r.active, r.down, [(0, 0, 0, units)], r.partial)
            yield from sum_and_gather(
                r, r.partial, r.output, None,
                lambda total, at, first: (r.three[at, :] + total).astype(BF16),
            )
            r.flush_blocks(r.output, block_owners(lax.axis_index("tensor")))

        def first(seg):
            r.need(*((r.grad_b_t, r.active), (r.norm_two_t, r.joined), ())[seg])
            rings.unit(seg, 0)

        order = [(seg, step) for step in range(1, devices) for seg in range(3)]
        units_left = [lambda s=seg: first(s) for seg in range(3)]
        units_left += [lambda u=u: rings.unit(*u) for u in order]
        interleave(main(), units_left, 3)

    quarter = rows // 4
    return run_kernel(
        body,
        dict(
            grad_b_t=Lazy(grad_b_t),
            active=Lazy(active),
            norm_two_t=Lazy(norm_two_t),
            joined=Lazy(joined),
            gate_up_t=(gate_up_t, pl.ANY),
            down=(down.reshape((1,) + down.shape), pl.ANY),
            three=Lazy(three),
            incoming=Lazy(incoming),
            query_raw=Lazy(query_raw),
            key_raw=Lazy(key_raw),
            query=Lazy(query),
            own=Lazy(own),
            near=Lazy(near),
            attended_t=Lazy(attended_t),
            log_total=Lazy(log_total),
            attn_out=Lazy(attn_out),
            query_weight=Lazy(query_weight),
            kv_weight=Lazy(kv_weight),
            head_gains=head_gains,
            two=Lazy(two),
            cosine=Lazy(tables[0]),
            sine=Lazy(tables[1]),
            lengths=(lengths, pltpu.SMEM),
            gains=gains,
        ),
        dict(
            grad_three_t=Lazy((width, rows), BF16),
            grad_query=Lazy((rows, columns), BF16),
            grad_kv=Lazy((rows, 2 * kv_columns), BF16),
            grad_two_b=Lazy((rows, width), BF16),
            grad_two_t=Lazy((width, rows), BF16),
            grad_two=Lazy((quarter, width), F32),
            small=Lazy((8, width), F32),
            sum_down=Lazy((block, units), F32),
            sum_gate_up=Lazy((block, 2, units), F32),
            output=Lazy((rows, width), BF16),
        ),
        dict(
            partial=pltpu.VMEM((rows, width), BF16),
            gathered=pltpu.VMEM((rows, width), BF16),
            grad_three=pltpu.VMEM((quarter, width), F32),
            grads=pltpu.VMEM((rows, columns), BF16),
            gain_term=pltpu.VMEM((1, width), F32),
            delta=pltpu.VMEM((heads, rows), F32),
            bias=pltpu.VMEM((rows, rows), F32),
            grad_q_t=pltpu.VMEM((columns, rows), F32),
            grad_own=pltpu.VMEM((rows, 2 * kv_columns), F32),
            far=pltpu.VMEM((SPAN - 1, rows, 2 * kv_columns), BF16),
            arrived=pltpu.VMEM((SPAN - 1, rows, 2 * kv_columns), BF16),
            p_send=pltpu.SemaphoreType.DMA((SPAN - 1,)),
            p_recv=pltpu.SemaphoreType.DMA((SPAN - 1,)),
            **stream_scratch(2 * units, 256),
            **exchange_scratch(rows, width),
            **ring_scratch(devices, sides, block, segment_widths),
        ),
        3 + 2,
        61,
        2 * rows * width * units * 10,
    )


TILE = 512


def unit_tiles(units):
    return [(at, min(TILE, units - at)) for at in range(0, units, TILE)]


def hidden_fetch(r, number, wide):
    slot = lax.rem(number, 2)
    rows = pl.ds(number * TILE, wide)
    pairs = [
        (r.gate_up_t.at[:, rows, :], r.gate_up_tile.at[slot, :, 0:wide, :]),
        (r.down.at[rows, :], r.down_tile.at[slot, 0:wide, :]),
    ]
    return [pltpu.make_async_copy(a, b, r.h_sem.at[slot, k]) for k, (a, b) in enumerate(pairs)]


def hidden_tiles(r, units, tile):
    count = pl.cdiv(units, TILE)
    rest = units - (count - 1) * TILE

    def run(number, wide):
        for copy in hidden_fetch(r, number, wide):
            copy.wait()
        slot = lax.rem(number, 2)
        tile(
            number, wide,
            r.gate_up_tile[slot, 0, 0:wide, :],
            r.gate_up_tile[slot, 1, 0:wide, :],
            r.down_tile[slot, 0:wide, :],
        )

    @pl.loop(0, count - 1)
    def _(number):
        @pl.when(number + 1 < count - 1)
        def _():
            for copy in hidden_fetch(r, number + 1, TILE):
                copy.start()

        @pl.when(number + 1 == count - 1)
        def _():
            for copy in hidden_fetch(r, number + 1, rest):
                copy.start()

        run(number, TILE)

    run(count - 1, rest)


def joined_parts(units):
    main = units // 128 * 128
    rest = units - main
    return [
        (0, 0, 0, main),
        (1, 0, main, main),
        (0, main, 2 * main, rest),
        (1, main, 2 * main + rest, rest),
    ]


def put_joined(ref, number, size, values, units):
    main = units // 128 * 128
    rest = units - main
    wide = values[0].shape[1]
    for which, value in enumerate(values):
        if isinstance(number, int):
            at = number * size
            cut = min(wide, main - at)
            ref[:, which * main + at : which * main + at + cut] = value[:, :cut]
            if cut < wide:
                at = 2 * main + which * rest
                ref[:, at : at + rest] = value[:, cut:]
        else:
            ref[:, pl.ds(pl.multiple_of(which * main + number * size, 128), wide)] = value


def joined_segments(left, joined, units):
    main = units // 128 * 128
    return [
        [(left, joined.at[:, pl.ds(0, main)])],
        [(left, joined.at[:, pl.ds(main, 2 * units - main)])],
    ]


def joined_widths(units):
    main = units // 128 * 128
    return [main, 2 * units - main]


def store_joined(ref, part, value, units):
    main = units // 128 * 128
    rest = units - main
    if part == 0:
        ref[:, 0, 0:main] = value
    else:
        ref[:, 1, 0:main] = value[:, :main]
        ref[:, 0, main:units] = value[:, main : main + rest]
        ref[:, 1, main:units] = value[:, main + rest :]


def tile_lanes(number, wide):
    start = number * TILE
    return pl.ds(start if isinstance(start, int) else pl.multiple_of(start, TILE), wide)


def hidden_scratch(width):
    return dict(
        gate_up_tile=pltpu.VMEM((2, 2, TILE, width), BF16),
        down_tile=pltpu.VMEM((2, TILE, width), BF16),
        h_sem=pltpu.SemaphoreType.DMA((2, 2)),
    )


def first_forward(
    tokens, cotangent, conv_in_t, kernel, conv_out, gate_up_t, down, gains, lengths
):
    rows, width = tokens.shape
    channels = conv_out.shape[0]
    units = down.shape[0]
    quarter = rows // 4
    count = len(unit_tiles(units))

    def body(r):
        me = lax.axis_index("dp")
        index = lax.axis_index("tensor")
        place = lax.rem(me, SPAN)
        greet(tensor_peers() + span_peers())
        for copy in hidden_fetch(r, 0, TILE):
            copy.start()
        r.need(r.tokens)
        for at in range(4):
            part = slice(at * quarter, (at + 1) * quarter)
            values = r.tokens[part, :].astype(F32)
            r.normed[part, :] = normalize(values, r.gains[0:1, :])[0].astype(BF16)
        r.need(r.conv_in_t)
        for at in range(3):
            made = jnp.dot(r.normed[...], r.conv_in_t[at], preferred_element_type=F32)
            r.projected[:, at * channels : (at + 1) * channels] = made
        r.flush(r.projected)
        pad = 8
        r.mixed[0:pad, :] = jnp.zeros((pad, channels), F32)
        r.mixed[pad:, :] = r.projected[:, :channels] * r.projected[:, 2 * channels :]
        r.rim_out[...] = r.mixed[rows : rows + pad, :]
        rim_copy = remote(r.rim_out, r.rim_in, r.m_sem.at[0], r.m_sem.at[1], dict(dp=me + 1))

        @pl.when(place < SPAN - 1)
        def _():
            rim_copy.start()

        start = pl.multiple_of(index * quarter, quarter)
        r.inputs_own[...] = r.tokens[pl.ds(start, quarter), :].astype(F32)
        r.flush(r.inputs_own)

        @pl.when(place > 0)
        def _():
            rim_copy.wait_recv()
            r.mixed[0:pad, :] = r.rim_in[...]

        r.rim[...] = r.mixed[0:pad, :]
        r.flush(r.rim)
        taps = r.kernel[...].astype(F32)
        convolved = None
        for k in range(KW):
            term = taps[k : k + 1, :] * r.mixed[pad - KW + 1 + k : pad - KW + 1 + k + rows, :]
            convolved = term if convolved is None else convolved + term
        r.gated_true[...] = (r.projected[:, channels : 2 * channels] * convolved).astype(BF16)
        for at, owner in enumerate(block_owners(index)):
            start = pl.multiple_of(owner * quarter, quarter)
            r.gated[at * quarter : (at + 1) * quarter, :] = r.gated_true[pl.ds(start, quarter), :]
        r.need(r.conv_out)
        r.partial[...] = jnp.dot(r.gated[...], r.conv_out[...], preferred_element_type=F32).astype(BF16)
        r.flush(r.gated)
        waits = sum_and_gather(
            r, r.partial, r.gathered_one, r.norm_one_t,
            lambda total, at, first: norm_rows(total, at, r.inputs_own, r.gains[1:2, :], r.one),
        )
        next(waits)
        r.need(r.cotangent)
        for at, owner in enumerate(block_owners(index)):
            part = slice(at * quarter, (at + 1) * quarter)
            start = pl.multiple_of(owner * quarter, quarter)
            live = block_positions(at, quarter, (quarter, width), 0) < own_length(r)
            values = jnp.where(live, r.cotangent[pl.ds(start, quarter), :].astype(F32), 0.0)
            if at == 0:
                r.incoming[...] = values
            r.grad_b[part, :] = values.astype(BF16)
        next(waits)
        r.normed_t[...] = r.normed[...].T
        r.grad_b_t[...] = r.grad_b[...].T
        r.flush(r.normed_t, r.grad_b, r.grad_b_t, r.incoming)
        exhaust(waits)
        r.flush(r.one, r.norm_one_t)
        r.total[...] = jnp.zeros_like(r.total)

        def tile(number, wide, gate_w, up_w, down_w):
            a = cross(r.gathered_one[...], gate_w)
            z = cross(r.gathered_one[...], up_w)
            r.gate[number, :, 0:wide] = a
            r.upward[number, :, 0:wide] = z
            s = (a * jax.nn.sigmoid(a) * z).astype(BF16)
            r.active[:, tile_lanes(number, wide)] = s
            r.total[...] += jnp.dot(s, down_w, preferred_element_type=F32)

        hidden_tiles(r, units, tile)
        r.partial[...] = r.total[...].astype(BF16)
        r.flush(r.active, r.gate, r.upward)
        exhaust(
            sum_and_gather(
                r, r.partial, r.gathered, r.normed_attn_t,
                lambda total, at, first: norm_rows(total, at, r.one, r.gains[2:3, :], r.two),
            )
        )
        r.flush(r.gathered, r.normed_attn_t, r.two)

        @pl.when(place < SPAN - 1)
        def _():
            rim_copy.wait_send()

    return run_kernel(
        body,
        dict(
            tokens=Lazy(tokens),
            cotangent=Lazy(cotangent),
            conv_in_t=Lazy(conv_in_t),
            kernel=kernel,
            conv_out=Lazy(conv_out),
            gate_up_t=(gate_up_t, pl.ANY),
            down=(down, pl.ANY),
            lengths=(lengths, pltpu.SMEM),
            gains=gains,
        ),
        dict(
            gathered=Lazy((rows, width), BF16),
            normed_attn_t=Lazy((width, rows), BF16),
            two=Lazy((quarter, width), F32),
            one=Lazy((quarter, width), F32),
            inputs_own=Lazy((quarter, width), F32),
            norm_one_t=Lazy((width, rows), BF16),
            normed_t=Lazy((width, rows), BF16),
            active=Lazy((rows, units), BF16),
            gate=Lazy((count, rows, TILE), F32),
            upward=Lazy((count, rows, TILE), F32),
            gated=Lazy((rows, channels), BF16),
            projected=Lazy((rows, 3 * channels), F32),
            rim=Lazy((8, channels), F32),
            grad_b=Lazy((rows, width), BF16),
            grad_b_t=Lazy((width, rows), BF16),
            incoming=Lazy((quarter, width), F32),
        ),
        dict(
            normed=pltpu.VMEM((rows, width), BF16),
            partial=pltpu.VMEM((rows, width), BF16),
            gathered_one=pltpu.VMEM((rows, width), BF16),
            total=pltpu.VMEM((rows, width), F32),
            gated_true=pltpu.VMEM((rows, channels), BF16),
            mixed=pltpu.VMEM((rows + 8, channels), F32),
            rim_out=pltpu.VMEM((8, channels), F32),
            rim_in=pltpu.VMEM((8, channels), F32),
            m_sem=pltpu.SemaphoreType.DMA((2,)),
            **hidden_scratch(width),
            **exchange_scratch(rows, width),
        ),
        1,
        60,
        6 * rows * width * units,
    )


class Pump:
    def __init__(self, rings, ready):
        self.rings, self.ready = rings, list(ready)
        self.step = [0] * len(rings.segments)
        self.before = None

    def run(self, number):
        for _ in range(number):
            left = [s for s in self.ready if self.step[s] <= self.rings.steps]
            if not left:
                return
            seg = min(left, key=lambda s: (s == self.before, self.step[s], s))
            self.rings.unit(seg, self.step[seg])
            self.step[seg] += 1
            self.before = seg

    def rest(self):
        self.run(len(self.step) * (self.rings.steps + 1))


def first_backward(
    lefts, rights, grad_two_b, down, gate_up_t, gate, upward, one, grad_two, conv_out,
    conv_in_t, projected, rim, kernel, inputs, gains, small, devices,
):
    rows, width = grad_two_b.shape
    units = down.shape[0]
    channels = conv_out.shape[0]
    quarter = rows // 4
    block = width // devices
    sides = piece_sides(width, devices)
    grad_three_t, normed_attn_t, grad_two_t, norm_one_t, normed_conv_t = lefts
    attended, grad_query, grad_kv, active, gated = rights
    columns, kv_columns = grad_query.shape[1], grad_kv.shape[1]
    widths = [channels + columns + kv_columns, units, *joined_widths(units), 4 * channels]
    bits = []
    bit = 1
    while bit < devices:
        bits.append(bit)
        bit *= 2
    stages = 2 + len(bits)
    size = TILE // 2
    tiles = [(at, min(size, units - at)) for at in range(0, units, size)]

    def body(r):
        me = lax.axis_index("dp")
        index = lax.axis_index("tensor")
        place = lax.rem(me, SPAN)

        done = []

        def store(seg, column, value):
            if seg == 0:
                at = (0, channels, channels + columns).index(column)
                if at == 2:
                    r.sum_kv[:, 0, :] = value[:, : kv_columns // 2]
                    r.sum_kv[:, 1, :] = value[:, kv_columns // 2 :]
                else:
                    (r.sum_attn_out, r.sum_query)[at][...] = value
                r.flush((r.sum_attn_out, r.sum_query, r.sum_kv)[at])
            elif seg == 1:
                r.sum_down[...] = value
                r.flush(r.sum_down)
            elif seg < 4:
                store_joined(r.sum_gate_up, seg - 2, value, units)
                done.append(seg)
                if len(done) == 2:
                    r.flush(r.sum_gate_up)
            elif column == 0:
                r.sum_conv_out[...] = value
                r.flush(r.sum_conv_out)
            else:
                for at in range(3):
                    r.sum_conv_in[at] = value[:, at * channels : (at + 1) * channels]
                r.flush(r.sum_conv_in)

        rings = Rings(
            devices, sides,
            [
                [
                    (r.grad_three_t, r.attended),
                    (r.normed_attn_t, r.grad_query),
                    (r.normed_attn_t, r.grad_kv),
                ],
                [(r.grad_two_t, r.active)],
            ]
            + joined_segments(r.norm_one_t, r.joined, units)
            + [[(r.grad_one_t, r.gated), (r.normed_conv_t, r.grad_projected)]],
            [r.held0, r.held1, r.held2, r.held3, r.held4], r.r_send, r.r_recv, r.r_credit, store,
        )
        pump = Pump(rings, [0, 1])
        small_peers = tensor_peers() + [dict(dp=me ^ bit) for bit in bits]
        greet(rings.peers() + small_peers + span_peers())

        def fetch(number):
            at, wide = tiles[number]
            slot = number % 2
            pairs = [
                (r.down.at[at : at + wide, :], r.down_tile.at[slot, 0:wide, :]),
                (r.gate.at[at // TILE, :, pl.ds(at % TILE, size)], r.gate_tile.at[slot]),
                (r.upward.at[at // TILE, :, pl.ds(at % TILE, size)], r.up_tile.at[slot]),
            ]
            return [
                pltpu.make_async_copy(a, b, r.h_sem.at[slot, k]) for k, (a, b) in enumerate(pairs)
            ]

        def fetch_conv(number):
            slot = number % 2
            return [
                pltpu.make_async_copy(
                    r.conv_in_t.at[k, pl.ds(number * size, size), :],
                    r.conv_tile.at[slot, k],
                    r.c_sem.at[slot, k],
                )
                for k in range(3)
            ]

        def main():
            first = pltpu.make_async_copy(r.grad_two_b, r.gathered, r.e_sem)
            first.start()
            for copy in fetch(0):
                copy.start()
            first.wait()
            for number, (at, wide) in enumerate(tiles):
                if number + 1 < len(tiles):
                    for copy in fetch(number + 1):
                        copy.start()
                for copy in fetch(number):
                    copy.wait()
                slot = number % 2
                grad = cross(r.gathered[...], r.down_tile[slot, 0:wide, :])
                gates, ups = r.gate_tile[slot, :, 0:wide], r.up_tile[slot, :, 0:wide]
                sigma = jax.nn.sigmoid(gates)
                grad_gate = (grad * ups * sigma * (1.0 + gates * (1.0 - sigma))).astype(BF16)
                grad_up = (grad * gates * sigma).astype(BF16)
                put_joined(r.joined, number, size, (grad_gate, grad_up), units)
                if number % 3 == 2:
                    yield 1
            r.need(r.norm_one_t, r.one, r.grad_two)
            pump.ready += [2, 3]
            yield 2
            yield from stream_product(r, r.joined, r.gate_up_t, joined_parts(units), r.partial)
            yield from sum_and_gather(
                r, r.partial, r.gathered, r.grad_one_t,
                lambda total, at, first: back_rows(
                    total, at, first, r.one, r.gains[1:2, :], r.grad_two, r.grad_one, r.gain_term
                ),
            )
            r.small_out[...] = r.small[...]
            r.small_out[1:2, :] = r.gain_term[...]

            r.need(r.conv_out, r.projected, r.rim, r.gated, r.normed_conv_t, r.inputs)
            made = cross(r.gathered[...], r.conv_out[...])
            for at, owner in enumerate(block_owners(index)):
                start = pl.multiple_of(owner * quarter, quarter)
                r.grad_gated[pl.ds(start, quarter), :] = made[at * quarter : (at + 1) * quarter]
            before = r.projected[:, :channels]
            signal = r.projected[:, 2 * channels :]
            taps = r.kernel[...].astype(F32)
            pad = 8
            r.mixed[pad:, :] = before * signal
            r.mixed[0:pad, :] = r.rim[...]
            grad_gated = r.grad_gated[...]
            r.grad_conv[0:rows, :] = grad_gated * r.projected[:, channels : 2 * channels]
            r.grad_conv[rows:, :] = jnp.zeros_like(r.grad_conv[rows:, :])
            r.rim_out[...] = r.grad_conv[0:pad, :]
            rim_copy = remote(r.rim_out, r.rim_in, r.m_sem.at[0], r.m_sem.at[1], dict(dp=me - 1))

            @pl.when(place > 0)
            def _():
                rim_copy.start()

            yield 1
            convolved = None
            for k in range(KW):
                shifted = r.mixed[pad - KW + 1 + k : pad - KW + 1 + k + rows, :]
                term = taps[k : k + 1, :] * shifted
                convolved = term if convolved is None else convolved + term
                term = jnp.sum(r.grad_conv[0:rows, :] * shifted, axis=0, keepdims=True)
                r.small_out[5 + k : 6 + k, 0:channels] = term
            r.grad_projected[:, channels : 2 * channels] = (grad_gated * convolved).astype(BF16)

            @pl.when(place < SPAN - 1)
            def _():
                rim_copy.wait_recv()
                r.grad_conv[rows:, :] = r.rim_in[...]

            grad_mixed = None
            for k in range(KW):
                term = taps[k : k + 1, :] * r.grad_conv[KW - 1 - k : KW - 1 - k + rows, :]
                grad_mixed = term if grad_mixed is None else grad_mixed + term
            r.grad_projected[:, :channels] = (grad_mixed * signal).astype(BF16)
            r.grad_projected[:, 2 * channels :] = (grad_mixed * before).astype(BF16)

            @pl.when(place > 0)
            def _():
                rim_copy.wait_send()

            pump.ready += [4]
            yield 2
            for copy in fetch_conv(0):
                copy.start()
            for number in range(width // size):
                if number + 1 < width // size:
                    for copy in fetch_conv(number + 1):
                        copy.start()
                for copy in fetch_conv(number):
                    copy.wait()
                for at, owner in enumerate(block_owners(index)):
                    start = pl.multiple_of(owner * quarter, quarter)
                    made = None
                    for k in range(3):
                        piece = r.grad_projected[
                            pl.ds(start, quarter), k * channels : (k + 1) * channels
                        ]
                        term = cross(piece, r.conv_tile[number % 2, k])
                        made = term if made is None else made + term
                    r.partial[
                        at * quarter : (at + 1) * quarter, number * size : (number + 1) * size
                    ] = made.astype(BF16)
                if number % 2:
                    yield 1
            yield from sum_and_gather(
                r, r.partial, r.input_grad, None,
                lambda total, at, first: back_rows(
                    total, at, first, r.inputs, r.gains[0:1, :], r.grad_one, None, r.gain_term
                ),
            )
            out_copies = []
            small_rows = quarter // 2
            for at in range(8):
                start = pl.multiple_of(block_owners(index)[at // 2] * quarter + at % 2 * small_rows, 8)
                if at >= 2:
                    out_copies[at - 2].wait()
                r.final[at % 2] = r.input_grad[at * small_rows : (at + 1) * small_rows, :].astype(F32)
                out_copies.append(
                    pltpu.make_async_copy(
                        r.final.at[at % 2], r.result.at[pl.ds(start, small_rows), :], r.g_sem.at[at]
                    )
                )
                out_copies[-1].start()
            for copy in out_copies[-2:]:
                copy.wait()
            r.small_out[0:1, :] = r.gain_term[...]
            row = lax.broadcasted_iota(jnp.int32, small.shape, 0)
            for stage in range(stages):
                copy = remote(
                    r.small_out, r.slots.at[stage], r.s_send.at[stage], r.s_recv.at[stage],
                    small_peers[stage],
                )
                copy.start()
                yield 1
                copy.wait()
                if stage < 2:
                    r.small_out[...] += jnp.where(row < 5, r.slots[stage], 0.0)
                else:
                    r.small_out[...] += r.slots[stage]
            r.flush(r.small_out)

        r.need(r.grad_three_t, r.attended, r.normed_attn_t, r.grad_query, r.grad_kv)
        pump.run(1)
        r.need(r.grad_two_t, r.active)
        pump.run(1)
        for number in main():
            pump.run(number)
        pump.rest()

    return run_kernel(
        body,
        dict(
            grad_three_t=Lazy(grad_three_t),
            attended=Lazy(attended),
            normed_attn_t=Lazy(normed_attn_t),
            grad_query=Lazy(grad_query),
            grad_kv=Lazy(grad_kv),
            grad_two_t=Lazy(grad_two_t),
            active=Lazy(active),
            norm_one_t=Lazy(norm_one_t),
            one=Lazy(one),
            grad_two=Lazy(grad_two),
            conv_out=Lazy(conv_out),
            projected=Lazy(projected),
            rim=Lazy(rim),
            gated=Lazy(gated),
            normed_conv_t=Lazy(normed_conv_t),
            inputs=Lazy(inputs),
            grad_two_b=(grad_two_b, pl.ANY),
            down=(down, pl.ANY),
            gate_up_t=(gate_up_t, pl.ANY),
            gate=(gate, pl.ANY),
            upward=(upward, pl.ANY),
            conv_in_t=(conv_in_t, pl.ANY),
            kernel=kernel,
            gains=gains,
            small=small,
        ),
        dict(
            result=((rows, width), F32, pl.ANY),
            small_out=Lazy(small.shape, F32),
            sum_attn_out=Lazy((block, channels), F32),
            sum_query=Lazy((block, columns), F32),
            sum_kv=Lazy((block, 2, kv_columns // 2), F32),
            sum_down=Lazy((block, units), F32),
            sum_gate_up=Lazy((block, 2, units), F32),
            sum_conv_out=Lazy((block, channels), F32),
            sum_conv_in=Lazy((3, block, channels), F32),
        ),
        dict(
            gathered=pltpu.VMEM((rows, width), BF16),
            partial=pltpu.VMEM((rows, width), BF16),
            grad_one_t=pltpu.VMEM((width, rows), BF16),
            grad_one=pltpu.VMEM((quarter, width), F32),
            joined=pltpu.VMEM((rows, 2 * units), BF16),
            input_grad=pltpu.VMEM((rows, width), BF16),
            final=pltpu.VMEM((2, quarter // 2, width), F32),
            g_sem=pltpu.SemaphoreType.DMA((8,)),
            grad_projected=pltpu.VMEM((rows, 3 * channels), BF16),
            grad_gated=pltpu.VMEM((rows, channels), F32),
            mixed=pltpu.VMEM((rows + 8, channels), F32),
            grad_conv=pltpu.VMEM((rows + 8, channels), F32),
            rim_out=pltpu.VMEM((8, channels), F32),
            rim_in=pltpu.VMEM((8, channels), F32),
            m_sem=pltpu.SemaphoreType.DMA((2,)),
            e_sem=pltpu.SemaphoreType.DMA,
            down_tile=pltpu.VMEM((2, size, width), BF16),
            gate_tile=pltpu.VMEM((2, rows, size), F32),
            up_tile=pltpu.VMEM((2, rows, size), F32),
            h_sem=pltpu.SemaphoreType.DMA((2, 3)),
            conv_tile=pltpu.VMEM((2, 3, size, channels), BF16),
            c_sem=pltpu.SemaphoreType.DMA((2, 3)),
            gain_term=pltpu.VMEM((1, width), F32),
            slots=pltpu.VMEM((stages,) + small.shape, F32),
            s_send=pltpu.SemaphoreType.DMA((stages,)),
            s_recv=pltpu.SemaphoreType.DMA((stages,)),
            **stream_scratch(2 * units, 128),
            **exchange_scratch(rows, width),
            **ring_scratch(devices, sides, block, widths),
        ),
        4,
        62,
        2 * rows * width * sum(widths) * 3,
    )


def assemble(arrays):
    count = len(arrays)

    def body(*refs):
        held, arrive, leave = refs[2 * count : 3 * count], refs[-2], refs[-1]
        first = [
            pltpu.make_async_copy(refs[at], held[at], arrive.at[at]) for at in range(count)
        ]
        second = [
            pltpu.make_async_copy(held[at], refs[count + at], leave.at[at]) for at in range(count)
        ]
        for copy in first:
            copy.start()
        for one, two in zip(first, second):
            one.wait()
            two.start()
        for copy in second:
            copy.wait()

    return pl.pallas_call(
        body,
        in_specs=[pl.BlockSpec(memory_space=pl.ANY)] * count,
        out_specs=[pl.BlockSpec(memory_space=pl.ANY)] * count,
        out_shape=[jax.ShapeDtypeStruct(a.shape, a.dtype) for a in arrays],
        scratch_shapes=[pltpu.VMEM(a.shape, a.dtype) for a in arrays]
        + [pltpu.SemaphoreType.DMA((count,))] * 2,
        compiler_params=pltpu.CompilerParams(vmem_limit_bytes=60 * 2**20),
    )(*arrays)


def local(
    tokens,
    lengths,
    norm_conv,
    conv_in,
    conv_kernel,
    conv_out,
    norm_mlp_one,
    gate_up_one,
    down_one,
    norm_attn,
    query_weight,
    kv_weight,
    query_gain,
    key_gain,
    attn_out,
    norm_mlp_two,
    gate_up_two,
    down_two,
    cotangent,
):
    row_count = tokens.shape[0]
    width = tokens.shape[1]
    quarter = row_count // 4
    local_kv = kv_weight.shape[2] // HEAD
    device = lax.axis_index("dp")
    devices = lax.axis_size("dp")
    index = lax.axis_index("tensor")
    place_index = device % SPAN
    offsets = jnp.concatenate(
        [o * quarter + jnp.arange(quarter, dtype=jnp.int32) for o in block_owners(index)]
    )
    positions = place_index * row_count + offsets
    gains = jnp.concatenate([norm_conv, norm_mlp_one, norm_attn, norm_mlp_two]).reshape(4, width)
    head_gains = jnp.stack([query_gain, key_gain], axis=1)
    frequency = THETA ** (-2.0 * jnp.arange(HEAD // 2, dtype=jnp.float32) / HEAD)
    angles = frequency[:, None] * positions.astype(jnp.float32)[None, :]
    tables = (jnp.cos(angles), jnp.sin(angles))
    gate_up_one_t = jnp.transpose(gate_up_one, (1, 2, 0))
    gate_up_two_t = jnp.transpose(gate_up_two, (1, 2, 0))
    conv_in_t = jnp.transpose(conv_in, (1, 0, 2))
    kv_flat = kv_weight.reshape(width, 2 * local_kv * HEAD)

    (
        normed_attn_b,
        normed_attn_t,
        two_own,
        one_own,
        inputs_own,
        norm_one_t,
        normed_conv_t,
        active_one,
        gate_one,
        up_one,
        gated_b,
        projected,
        rim,
        grad_b,
        grad_b_t,
        incoming,
    ) = first_forward(
        tokens, cotangent, conv_in_t, conv_kernel, conv_out, gate_up_one_t, down_one, gains, lengths
    )
    (
        active_two,
        joined_two,
        norm_two_t,
        three_own,
        *kept,
        attended_b,
        attended_t,
        log_total,
    ) = attention_forward(
        normed_attn_b,
        query_weight,
        kv_flat,
        head_gains,
        attn_out,
        two_own,
        tables,
        gains,
        lengths,
        gate_up_two_t,
        down_two,
        grad_b,
    )
    kept = (*kept, attended_t, log_total)
    (
        grad_three_t,
        grad_query,
        grad_kv,
        grad_two_b,
        grad_two_t,
        grad_two,
        small,
        sum_down_two,
        sum_gate_up_two,
        output,
    ) = attention_backward(
        grad_b_t,
        norm_two_t,
        active_two,
        joined_two,
        gate_up_two_t,
        down_two,
        three_own,
        incoming,
        kept,
        attn_out,
        query_weight,
        kv_flat,
        head_gains,
        two_own,
        tables,
        gains,
        lengths,
        devices,
    )

    (
        grad_inputs,
        small,
        sum_attn_out,
        sum_query,
        sum_kv,
        sum_down_one,
        sum_gate_up_one,
        sum_conv_out,
        sum_conv_in,
    ) = first_backward(
        [grad_three_t, normed_attn_t, grad_two_t, norm_one_t, normed_conv_t],
        [attended_b, grad_query, grad_kv, active_one, gated_b],
        grad_two_b,
        down_one,
        gate_up_one_t,
        gate_one,
        up_one,
        one_own,
        grad_two,
        conv_out,
        conv_in_t,
        projected,
        rim,
        conv_kernel,
        inputs_own,
        gains,
        small,
        devices,
    )
    out_rows = width // devices
    (
        output, grad_inputs, sum_conv_in, sum_conv_out, sum_gate_up_one, sum_down_one, sum_query, sum_kv,
        sum_attn_out, sum_gate_up_two, sum_down_two,
    ) = assemble(
        [
            output, grad_inputs, jnp.reshape(sum_conv_in, (-1, sum_conv_in.shape[2])), sum_conv_out,
            sum_gate_up_one, sum_down_one, sum_query, sum_kv, sum_attn_out, sum_gate_up_two, sum_down_two,
        ]
    )
    sum_conv_in = sum_conv_in.reshape(3, -1, sum_conv_in.shape[1])
    return (
        output,
        grad_inputs,
        small[0],
        jnp.transpose(sum_conv_in, (1, 0, 2)),
        small[5:, : conv_out.shape[0]],
        sum_conv_out.T,
        small[1],
        sum_gate_up_one,
        sum_down_one.T,
        small[2],
        sum_query,
        sum_kv,
        small[4, :HEAD],
        small[4, HEAD : 2 * HEAD],
        sum_attn_out.T,
        small[3],
        sum_gate_up_two,
        sum_down_two.T,
    )


def solution(mesh):
    in_specs = (
        P("dp", None),
        P(),
        P(),
        P(None, None, "tensor"),
        P(None, "tensor"),
        P("tensor", None),
        P(),
        P(None, None, "tensor"),
        P("tensor", None),
        P(),
        P(None, "tensor"),
        P(None, None, "tensor"),
        P(),
        P(),
        P("tensor", None),
        P(),
        P(None, None, "tensor"),
        P("tensor", None),
        P("dp", None),
    )
    out_specs = (
        P("dp", None),
        P("dp", None),
        P(),
        P("dp", None, "tensor"),
        P(None, "tensor"),
        P("tensor", "dp"),
        P(),
        P("dp", None, "tensor"),
        P("tensor", "dp"),
        P(),
        P("dp", "tensor"),
        P("dp", None, "tensor"),
        P(),
        P(),
        P("tensor", "dp"),
        P(),
        P("dp", None, "tensor"),
        P("tensor", "dp"),
    )
    return jax.shard_map(local, mesh=mesh, in_specs=in_specs, out_specs=out_specs, check_vma=False)
```
